32 devices in a mesh: river: 4 (over y, core), coast: 8 (over z, x).
Axes of the slice: x: 2, y: 2, z: 4, core: 2. Of those that a mesh axis runs over, the one named last changes fastest.
Arguments:
- reach_depth: float32 [2048, 128], P(('river', 'coast')), may hold values from 0.02 to 4
- reach_flow: float32 [2048, 128], P(('river', 'coast')), may hold values from -3 to 3
- reach_bed: float32 [2048, 128], P(('river', 'coast')), may hold values from 0 to 1
- reach_width: float32 [2048, 128], P(('river', 'coast')), may hold values from 200 to 800
- reach_length: float32 [2048, 128], P(('river', 'coast')), may hold values from 4000 to 12000
- runoff: float32 [2048, 128], P(('river', 'coast')), may hold values from 1 to 100
- flows_into: int32 [2048, 128], P(('river', 'coast')), may hold values from 1 to 128, as said below
- mouth_prev: float32 [2048, 32], P(('river', 'coast')), may hold values from -1.5 to 1.5
- mouth_tile: int32 [2048, 32, 1], P(('river', 'coast')), may hold values from 0 to 31; in each aligned block of 2048 rows (0 to 2047, 2048 to 4095, ..., all dimensions but the last counted through in order) at most 128 rows name the same one
- mouth_cell: int32 [2048, 32], P(('river', 'coast')), may hold values from 0 to 4095
- sea_level: float32 [128, 1024], P('river', 'coast'), may hold values from -1.2 to 1.2
- sea_bed: float32 [128, 1024], P('river', 'coast'), may hold values from -4 to 0.5
- wet_mask: int32 [128, 1024], P('river', 'coast'), may hold values 0 or 1
- flux_east: float32 [128, 1024], P('river', 'coast'), may hold values from -3 to 3
- flux_north: float32 [128, 1024], P('river', 'coast'), may hold values from -3 to 3
Outputs:
- depth_after: float32 [2048, 128], P(('river', 'coast'))
- level_after: float32 [128, 1024], P('river', 'coast')
- mouth_level: float32 [2048, 384], P(('river', 'coast'))
The draws below stay inside these ranges and needn't reach their ends.
Inputs may be any that keep to these rules, and one draw needn't show every extreme that they name: `flows_into`: in every block the last 32 reaches have the value 128 (they flow to the sea); every other reach i names a reach of the same block with index i + 1 to i + 16. `mouth_tile`: among the mouths of one device (the rows of one device, in order), no tile is named more than 128 times, a bound that some block reaches; every tile is named by some mouth.
All inputs are finite; a program needn't handle non-finite values. No bound on the sum of `wet_mask` on one device may be relied on, other than what follows from the above.
Results may differ from the reference program's by a relative error of at most 0.0002.
Values sent between devices are 32-bit elements; how exact they have to be, the bound alone decides.
No kernel may reach another device: no remote copies, remote signals or barrier semaphores. Data moves between devices by JAX's collectives and lax.ppermute only.
A program may use at most 64 MiB of HBM per device.

```python
import math
import jax
import jax.numpy as jnp
import numpy as np

RB = 128
MPB = 32
STEPS = 12
BLK_DEV = 64
TX = 32
TY = 128
CAP = 128
NBLK = 2048
OX = 128
OY = 1024
N_COAST = 8
DEVICES = 32


def draw_flows_into(key, part):
    position = jnp.broadcast_to(jnp.arange(RB, dtype=jnp.int32)[None, :], (NBLK, RB))
    lowest = jnp.minimum(position + 1, RB - 1)
    highest = jnp.maximum(jnp.minimum(position + 17, RB), lowest + 1)
    picked = jax.random.randint(key, (NBLK, RB), lowest, highest, dtype=jnp.int32)
    return jnp.where(position >= RB - MPB, RB, picked).astype(jnp.int32)


def set_ends(values, key, smallest, high):
    index_at = [jax.random.randint(jax.random.fold_in(key, axis), (), 0, length) for axis, length in enumerate(values.shape)]
    widest = values.shape.index(max(values.shape))
    neighbour = index_at[:widest] + [(index_at[widest] + 1) % values.shape[widest]] + index_at[widest + 1:]
    return values.at[tuple(index_at)].set(smallest).at[tuple(neighbour)].set(high)


def block_scale(own_key, shape, pieces, low, largest):
    def one(dim, shards_of):
        draws = jax.random.uniform(jax.random.fold_in(jax.random.fold_in(own_key, 6), dim), (shards_of,), jnp.float32, low / len(pieces), largest / len(pieces))
        return jnp.repeat(jnp.exp(draws), shape[dim] // shards_of).reshape((-1,) + (1,) * (len(shape) - dim - 1))

    level = one(*pieces[0])
    for cut in pieces[1:]:
        level = level * one(*cut)
    return level


def deal_out(own_key, own, number, rows, amount, top, bound, skew):
    sequence = jax.random.permutation(own_key, amount)
    packed, common = portions_of(amount, rows * top, bound, skew, True), portions_of(amount, rows * top, bound, skew, False)
    places = jnp.arange(amount)

    def named(sizes, turn):
        used = int((sizes > 0).sum())
        fixed = max(1, used // 4)
        passed = fixed + (places - fixed + turn * (used - fixed)) % max(1, amount - fixed)
        return jnp.zeros((amount,), jnp.int32).at[sequence[jnp.where(places < fixed, places, passed)]].set(jnp.asarray(sizes, jnp.int32))

    sizes = jnp.where(number % 4 == 0, named(packed, number // 4), named(common, number - number // 4 - 1))
    mixed = jax.random.permutation(jax.random.fold_in(own, 3), amount)
    donor, receiver = mixed[0:amount // 2 * 2:2], mixed[1:amount // 2 * 2:2]
    margin = jnp.minimum(sizes[donor] - 1, bound - sizes[receiver]) // 2
    margin = jnp.where((donor == sequence[0]) | (receiver == sequence[0]) | (sizes[receiver] == 0), 0, jnp.maximum(margin, 0))
    passed = jax.random.randint(jax.random.fold_in(own, 4), (amount // 2,), 0, 1 << 20) % (margin + 1)
    sizes = sizes.at[donor].add(-passed).at[receiver].add(passed)
    labels = jnp.searchsorted(jnp.cumsum(sizes), jnp.arange(rows * top), side="right").astype(jnp.int32)
    listing = labels.reshape(top, rows).T
    listing = listing[jax.random.permutation(jax.random.fold_in(own, 1), rows)]
    turn = jax.random.randint(jax.random.fold_in(own, 2), (rows, 1), 0, top)
    return jnp.take_along_axis(listing, (jnp.arange(top)[None, :] + turn) % top, axis=1)


def portions_of(amount, total, bound, lean, full):
    loads = [(1 << 20) // math.isqrt(grade ** lean) + 1 for grade in range(1, amount + 1)]
    largest = bound if full else min(bound, max(-(-total // amount), total * loads[0] // sum(loads)))
    least = 1 if total - largest >= amount - 1 else 0
    given, spare = [largest] + [least] * (amount - 1), total - largest - least * (amount - 1)
    while spare > 0:
        movable = [i for i in range(1, amount) if given[i] < largest] or [i for i in range(1, amount) if given[i] < bound]
        mass, budget = sum([loads[i] for i in movable]), spare
        for i in movable:
            more = min(bound - given[i], max(1, budget * loads[i] // mass), spare)
            given[i] = given[i] + more
            spare = spare - more
    return np.array(given)


def bell_draw(key, dims, scale, limit, cuts=(), kind=jnp.bfloat16):
    factor_of = block_scale(key, dims, cuts, -0.22, 0.18) if cuts else 1.0
    result = jax.random.normal(key, dims, jnp.float32) * scale * factor_of
    return jnp.minimum(jnp.maximum(result, -limit), limit).astype(kind)


def setup_inputs(seed: int = 0) -> dict:
    arg_keys = jax.random.split(jax.random.key(seed), 16)
    reach_depth = jnp.clip(jnp.exp(math.log(4.0) - 5.2983174 * jax.random.uniform(arg_keys[0], (NBLK, RB), jnp.float32) ** block_scale(arg_keys[0], (NBLK, RB), ((0, 32),), -0.2, 0.2)), 0.02, 4.0)
    reach_flow = bell_draw(arg_keys[1], (NBLK, RB), 0.5, 3.0, ((0, 32),), jnp.float32)
    reach_bed = jnp.clip(1.0 * jax.random.uniform(arg_keys[2], (NBLK, RB), jnp.float32) ** block_scale(arg_keys[2], (NBLK, RB), ((0, 32),), -0.2, 0.2), 0.0, 1.0)
    reach_width = jnp.clip(jnp.exp(math.log(800.0) - 1.3862944 * jax.random.uniform(arg_keys[3], (NBLK, RB), jnp.float32) ** block_scale(arg_keys[3], (NBLK, RB), ((0, 32),), -0.2, 0.2)), 200.0, 800.0)
    reach_length = jnp.clip(jnp.exp(math.log(12000.0) - 1.0986123 * jax.random.uniform(arg_keys[4], (NBLK, RB), jnp.float32) ** block_scale(arg_keys[4], (NBLK, RB), ((0, 32),), -0.2, 0.2)), 4000.0, 12000.0)
    runoff = jnp.clip(jnp.exp(math.log(100.0) - 4.6051702 * jax.random.uniform(arg_keys[5], (NBLK, RB), jnp.float32) ** block_scale(arg_keys[5], (NBLK, RB), ((0, 32),), -0.2, 0.2)), 1.0, 100.0)
    flows_into = draw_flows_into(jax.random.fold_in(arg_keys[15], 71), 0)
    mouth_prev = bell_draw(arg_keys[7], (NBLK, MPB), 0.4, 1.5, ((0, 32),), jnp.float32)
    mouth_tile_keys = jax.random.split(jax.random.fold_in(arg_keys[8], 1), NBLK * MPB // (BLK_DEV * MPB))
    mouth_tile_turns = jax.random.permutation(jax.random.fold_in(arg_keys[8], 3), NBLK * MPB // (BLK_DEV * MPB))
    mouth_tile = jax.vmap(lambda own, number: deal_out(jax.random.fold_in(arg_keys[8], 2), own, number, BLK_DEV * MPB, DEVICES, 1, CAP, 2))(mouth_tile_keys, mouth_tile_turns).reshape((NBLK, MPB, 1))
    mouth_cell = set_ends(jax.random.randint(arg_keys[9], (NBLK, MPB), 0, TX * TY), jax.random.fold_in(arg_keys[9], 1), 0, (TX * TY) - 1).astype(jnp.int32)
    sea_level = bell_draw(arg_keys[10], (OX, OY), 0.3, 1.2, ((0, 4), (1, 8)), jnp.float32)
    sea_bed = jnp.clip(-4.0 + 4.5 * jax.random.uniform(arg_keys[11], (OX, OY), jnp.float32) ** block_scale(arg_keys[11], (OX, OY), ((0, 4), (1, 8)), -0.2, 0.2), -4.0, 0.5)
    wet_mask = set_ends((jax.random.randint(arg_keys[12], (OX, OY), 0, 8) < 7).astype(jnp.int32), jax.random.fold_in(arg_keys[12], 1), 0, 1)
    flux_east = bell_draw(arg_keys[13], (OX, OY), 0.5, 3.0, ((0, 4), (1, 8)), jnp.float32)
    flux_north = bell_draw(arg_keys[14], (OX, OY), 0.5, 3.0, ((0, 4), (1, 8)), jnp.float32)
    return dict(reach_depth=reach_depth, reach_flow=reach_flow, reach_bed=reach_bed, reach_width=reach_width, reach_length=reach_length, runoff=runoff, flows_into=flows_into, mouth_prev=mouth_prev, mouth_tile=mouth_tile, mouth_cell=mouth_cell, sea_level=sea_level, sea_bed=sea_bed, wet_mask=wet_mask, flux_east=flux_east, flux_north=flux_north)


gravity = 9.81
step_seconds = 300.0
cell_metres = 3000.0
river_manning = 0.035
ocean_manning = 0.025
depth_floor = 0.05


def inertial(unit_flow, upper_level, lower_level, bed_upper, bed_lower, distance, manning):
    face_depth = jnp.maximum(upper_level, lower_level) - jnp.maximum(bed_upper, bed_lower)
    driving = gravity * step_seconds * jnp.maximum(face_depth, 0.0) * (upper_level - lower_level) / distance
    friction = gravity * step_seconds * manning * manning * jnp.abs(unit_flow) / jnp.power(jnp.maximum(face_depth, depth_floor), 7.0 / 3.0)
    return (unit_flow + driving) / (1.0 + friction)


def river_step(water_depth, unit_flow, reach_bed, reach_width, reach_length, runoff, flows_into, mouth_prev):
    inland = RB - MPB
    surface = reach_bed + water_depth
    down_index = flows_into[:, :inland].astype(jnp.int32)
    below = jnp.concatenate([jnp.take_along_axis(surface, down_index, axis=1), mouth_prev], axis=1)
    bed_below = jnp.concatenate([jnp.take_along_axis(reach_bed, down_index, axis=1), reach_bed[:, inland:]], axis=1)
    unit_flow = inertial(unit_flow, surface, below, reach_bed, bed_below, reach_length, river_manning)
    discharge = unit_flow * reach_width
    row_index = jnp.arange(water_depth.shape[0], dtype=jnp.int32)[:, None]
    inflow = jnp.zeros_like(water_depth).at[row_index, down_index].add(discharge[:, :inland])
    water_depth = water_depth + step_seconds * (inflow + runoff - discharge) / (reach_width * reach_length)
    return water_depth, unit_flow, discharge[:, inland:]


def reference(reach_depth, reach_flow, reach_bed, reach_width, reach_length, runoff, flows_into, mouth_prev, mouth_tile, mouth_cell, sea_level, sea_bed, wet_mask, flux_east, flux_north):
    tile_index = mouth_tile[:, :, 0]
    grid_row = (tile_index // N_COAST) * TX + mouth_cell // TY
    grid_col = (tile_index % N_COAST) * TY + mouth_cell % TY
    target = (grid_row * OY + grid_col).reshape(-1).astype(jnp.int32)
    water_level = jnp.where(wet_mask == 1, jnp.maximum(sea_level, sea_bed), sea_bed)
    bed_padded = jnp.pad(sea_bed, 1)
    east_faces = jnp.concatenate([jnp.zeros((1, OY), jnp.float32), flux_east], axis=0)
    north_faces = jnp.concatenate([jnp.zeros((OX, 1), jnp.float32), flux_north], axis=1)
    water_depth, unit_flow = reach_depth, reach_flow
    sampled = []
    for substep in range(STEPS):
        water_depth, unit_flow, mouth_flow = river_step(water_depth, unit_flow, reach_bed, reach_width, reach_length, runoff, flows_into, mouth_prev)
        source = jnp.zeros((OX * OY,), jnp.float32).at[target].add(mouth_flow.reshape(-1)).reshape(OX, OY)
        padded = jnp.pad(water_level, 1)
        east_faces = inertial(east_faces, padded[:-1, 1:-1], padded[1:, 1:-1], bed_padded[:-1, 1:-1], bed_padded[1:, 1:-1], cell_metres, ocean_manning)
        north_faces = inertial(north_faces, padded[1:-1, :-1], padded[1:-1, 1:], bed_padded[1:-1, :-1], bed_padded[1:-1, 1:], cell_metres, ocean_manning)
        spread = east_faces[1:] - east_faces[:-1] + north_faces[:, 1:] - north_faces[:, :-1]
        water_level = water_level - step_seconds / cell_metres * spread + step_seconds / (cell_metres * cell_metres) * source
        sampled.append(water_level.reshape(-1)[target].reshape(NBLK, MPB))
    mouth_level = jnp.stack(sampled, axis=1).reshape(NBLK, STEPS * MPB)
    return water_depth, water_level, mouth_level
```

```python
import functools
import math

import jax
import jax.numpy as jnp
from jax import lax
from jax.experimental import pallas as pl
from jax.experimental.pallas import tpu as pltpu
from jax.sharding import PartitionSpec as P

RB = 128
MPB = 32
STEPS = 12

gravity = 9.81
step_seconds = 300.0
cell_metres = 3000.0
river_manning = 0.035
ocean_manning = 0.025
depth_floor = 0.05
reach_offsets = 16

LANES = 128
SENT = 13
TALL = 16
WIDE = 256
HALO = 12
STRIP = 16
FIELDS = 16
f32, bf16, i32 = jnp.float32, jnp.bfloat16, jnp.int32

PARAMS = pltpu.CompilerParams(vmem_limit_bytes=40 * 1024 * 1024)


def flow_after(unit_flow, upper, lower, bed_top, drive, manning):
    face_depth = jnp.maximum(upper, lower) - bed_top
    driving = drive * jnp.maximum(face_depth, 0.0) * (upper - lower)
    power = -7.0 / 3.0 * math.log2(math.e)
    thin = jnp.exp2(jnp.log(jnp.maximum(face_depth, depth_floor)) * power)
    friction = (gravity * step_seconds * manning * manning) * jnp.abs(unit_flow) * thin
    divisor = 1.0 + friction
    inverse = pl.reciprocal(divisor, approx=True)
    inverse = inverse * (2.0 - divisor * inverse)
    return (unit_flow + driving) * inverse


def in_two(values):
    high = values.astype(bf16)
    return high, (values - high.astype(f32)).astype(bf16)


def small(labels):
    return jnp.broadcast_to(labels.astype(f32), (TALL, labels.shape[1])).astype(bf16)


def one_hot_columns(columns, rhs, lanes):
    labels = small(columns)
    place = lax.broadcasted_iota(i32, labels.shape, 0).astype(f32).astype(bf16)
    one, none = jnp.ones(labels.shape, bf16), jnp.zeros(labels.shape, bf16)
    for part in range(WIDE // TALL):
        hit = labels - part * TALL == place
        rhs[part * TALL : (part + 1) * TALL, lanes] = jnp.where(hit, one, none)


def lay_out(values, rows, columns, lhs, rhs, lanes):
    high, low = in_two(values)
    labels = small(rows)
    none = jnp.zeros(labels.shape, bf16)
    for row in range(TALL):
        hit = labels == row
        lhs[row * TALL : (row + 1) * TALL, lanes] = jnp.where(hit, high, none)
        lhs[WIDE + row * TALL : WIDE + (row + 1) * TALL, lanes] = jnp.where(hit, low, none)
    one_hot_columns(columns, rhs, lanes)


def add_up(lhs, rhs):
    both = lax.dot_general(
        lhs[...], rhs[...], (((1,), (1,)), ((), ())), preferred_element_type=f32
    )
    return both[:WIDE] + both[WIDE:]


def look_up(table, rows, hot):
    both = jnp.concatenate([hot, hot], axis=0)
    found = jnp.dot(table, both, preferred_element_type=f32)
    total = jnp.zeros((TALL, rows.shape[1]), f32)
    for row in range(TALL):
        hit = jnp.broadcast_to(rows == row, total.shape)
        total = total + jnp.where(hit, found[row * TALL : (row + 1) * TALL], 0.0)
    return total


def cell_labels(cells, tile_cols):
    row, column = cells // tile_cols, cells % tile_cols
    return row % TALL, row // TALL * tile_cols + column


def river_kernel(
    devices,
    capacity,
    *refs,
):
    inputs, (depth_out, send_out, address_out), refs = refs[:10], refs[10:13], refs[13:]
    copies = [
        pltpu.make_async_copy(whole, own, refs[10].at[number])
        for number, (whole, own) in enumerate(zip(inputs, refs[:10]))
    ]
    for copy in copies[::-1]:
        copy.start()
    river_steps(devices, capacity, copies, *refs[:10], depth_out, send_out, address_out, *refs[10:])


def river_steps(
    devices,
    capacity,
    copies,
    depth_in,
    flow_in,
    bed_in,
    width_in,
    length_in,
    runoff_in,
    into_in,
    prev_in,
    tile_in,
    cell_in,
    depth_out,
    send_out,
    address_out,
    arrivals,
    depth_end,
    enters,
    series,
    turned,
    tiles,
    hots,
    lhs,
    rhs,
):
    blocks = depth_in.shape[0]
    groups = LANES // MPB
    rows = blocks // groups
    inland = RB - MPB
    lane = lax.broadcasted_iota(i32, (blocks, RB), 1)

    turned[...] = jnp.zeros_like(turned)
    for copy in copies[7:]:
        copy.wait()
    turned[0:MPB, 0:blocks] = tile_in[...].astype(f32)
    turned[MPB : 2 * MPB, 0:blocks] = cell_in[...].astype(f32)
    turned[inland:RB, 0:blocks] = prev_in[...]
    mouths = jnp.transpose(turned[...])[0:blocks]
    prev = mouths

    def grouped(array, first):
        lanes16 = lax.broadcasted_iota(i32, (rows, LANES), 1)
        result = jnp.zeros((rows, LANES), f32)
        for g in range(groups):
            part = array[g * rows : (g + 1) * rows]
            shift = (g * MPB - first) % LANES
            part = part if shift == 0 else pltpu.roll(part, shift, 1)
            result = jnp.where(lanes16 // MPB == g, part, result)
        return result

    tiles[...] = grouped(mouths, 0).astype(i32)
    series[STEPS * rows : (STEPS + 1) * rows] = grouped(mouths, MPB)
    series[(STEPS + 1) * rows :] = jnp.zeros((series.shape[0] - (STEPS + 1) * rows, LANES), f32)

    for i in range(rows):
        names = jnp.broadcast_to(tiles[i : i + 1], (devices, LANES))
        hit = names == lax.broadcasted_iota(i32, (devices, LANES), 0)
        hots[i * devices : (i + 1) * devices] = jnp.where(hit, 1.0, 0.0).astype(bf16)
    shape = (LANES, 2 * LANES)
    earlier = lax.broadcasted_iota(i32, shape, 0) < lax.broadcasted_iota(i32, shape, 1)
    counted = jnp.dot(
        hots[...], jnp.where(earlier, 1.0, 0.0).astype(bf16), preferred_element_type=f32
    )
    before = jnp.zeros((devices, LANES), f32)
    for i in range(rows):
        part = slice(i * devices, (i + 1) * devices)
        ranks = (counted[part, :LANES] + before) * hots[part].astype(f32)
        rank = jnp.sum(ranks, axis=0, keepdims=True).astype(i32)
        address_out[i : i + 1] = tiles[i : i + 1] * capacity + rank
        before = before + counted[part, LANES:]

    for copy in copies[:7]:
        copy.wait()
    into = into_in[...]
    at_mouth = lane >= inland
    down = jnp.where(at_mouth, 0, into)
    offset = jnp.where(at_mouth, 0, into - lane)
    bed = bed_in[...]
    bed_top = jnp.where(
        at_mouth, bed, jnp.maximum(bed, jnp.take_along_axis(bed, down, axis=1))
    )
    drive = gravity * step_seconds / length_in[...]
    area = step_seconds / (width_in[...] * length_in[...])
    for o in range(1, reach_offsets + 1):
        hit = jnp.where(offset == o, 1.0, 0.0)
        enters[o - 1] = pltpu.roll(hit, o, 1)

    def river_turn(substep, carry):
        depth, flow = carry
        surface = bed + depth
        below = jnp.where(at_mouth, prev, jnp.take_along_axis(surface, down, axis=1))
        flow = flow_after(flow, surface, below, bed_top, drive, river_manning)
        discharge = flow * width_in[...]
        inflow = enters[0] * pltpu.roll(discharge, 1, 1)
        for o in range(2, reach_offsets + 1):
            inflow = inflow + enters[o - 1] * pltpu.roll(discharge, o, 1)
        depth = depth + area * (inflow + runoff_in[...] - discharge)
        series[pl.ds(pl.multiple_of(substep * rows, rows), rows)] = grouped(discharge, inland)
        return depth, flow

    depth, _ = lax.fori_loop(0, STEPS, river_turn, (depth_in[...], flow_in[...]), unroll=2)
    depth_end[...] = depth
    finished = pltpu.make_async_copy(depth_end, depth_out, arrivals.at[len(copies)])
    finished.start()

    for i in range(rows):
        address = address_out[i : i + 1]
        lay_out(
            series[pl.ds(i, TALL, stride=rows)],
            address // WIDE,
            address % WIDE,
            lhs,
            rhs,
            slice(i * LANES, (i + 1) * LANES),
        )
    packed = add_up(lhs, rhs)
    for row in range(TALL):
        part = packed[row * TALL : row * TALL + SENT]
        for half in range(2):
            at = (2 * row + half) * SENT
            send_out[at : at + SENT] = part[:, half * LANES : (half + 1) * LANES]
    finished.wait()


def reach_of(field):
    return STEPS - 1 - field if field < STEPS else HALO


ROW_AT = [sum(reach_of(f) for f in range(field)) for field in range(FIELDS + 1)]
ROWS_SENT = -(-ROW_AT[FIELDS] // 8) * 8


def source_kernel(arrived, *refs):
    inputs, (fields, odd, even, rhs), refs = refs[:5], refs[5:9], refs[9:]
    first_of_pair = lax.axis_index("river") % 2 == 0
    sea_level, sea_bed, wet_mask, flux_east, flux_north, arrivals, lhs, sums = refs
    copies = [
        pltpu.make_async_copy(whole, own, arrivals.at[number])
        for number, (whole, own) in enumerate(zip(inputs, refs[:5]))
    ]
    for copy in copies:
        copy.start()
    groups = arrived.shape[0] // SENT
    tile_rows, tile_cols = sea_level.shape

    def place(s, carry):
        values = arrived[pl.ds(s * SENT, SENT)]
        values = jnp.concatenate([values, jnp.zeros((TALL - SENT, LANES), f32)], axis=0)
        cells = values[STEPS : STEPS + 1].astype(i32)
        rows, columns = cell_labels(cells, tile_cols)
        lay_out(values, rows, columns, lhs, rhs, pl.ds(pl.multiple_of(s * LANES, LANES), LANES))
        return carry

    lax.fori_loop(0, groups, place, 0, unroll=2)
    total = add_up(lhs, rhs)
    for half in range(2):
        sums[half * WIDE : (half + 1) * WIDE] = total[:, half * LANES : (half + 1) * LANES]
    for copy in copies:
        copy.wait()
    bed = sea_bed[...]
    level = jnp.where(wet_mask[...] == 1, jnp.maximum(sea_level[...], bed), bed)

    def put(field, value):
        fields[field * tile_rows : (field + 1) * tile_rows] = value
        reach = reach_of(field)
        if reach:
            last, first = value[tile_rows - reach :], value[:reach]
            part = slice(ROW_AT[field], ROW_AT[field] + reach)
            odd[part] = jnp.where(first_of_pair, first, last)
            even[part] = jnp.where(first_of_pair, last, first)

    for swap_out in (odd, even):
        swap_out[ROWS_SENT - 8 :] = jnp.zeros((8, LANES), f32)
    for step in range(STEPS):
        halves = [sums[pl.ds(half * WIDE + step, TALL, stride=TALL)] for half in range(2)]
        put(step, jnp.concatenate(halves, axis=0))
    for number, value in enumerate((level, bed, flux_east[...], flux_north[...])):
        put(STEPS + number, value)


def strip_kernel(fields, from_odd, from_even, tall, odd, even):
    upper = lax.axis_index("river") % 2 == 0
    first_of_pair = lax.axis_index("coast") % 2 == 0
    from_before = jnp.where(upper, from_odd[...], from_even[...])
    from_after = jnp.where(upper, from_even[...], from_odd[...])
    tile_rows = fields.shape[0] // FIELDS
    height = tall.shape[0] // FIELDS
    per = LANES // STRIP
    lane = lax.broadcasted_iota(i32, (height, LANES), 1)
    for group in range(FIELDS // per):
        ends = jnp.zeros((height, LANES), f32)
        starts = jnp.zeros((height, LANES), f32)
        for place in range(per):
            field = group * per + place
            parts = [fields[field * tile_rows : (field + 1) * tile_rows]]
            reach, at = reach_of(field), ROW_AT[field]
            if reach:
                parts.append(from_after[at : at + reach])
            if reach < HALO:
                parts.append(jnp.zeros((2 * HALO - 2 * reach, LANES), f32))
            if reach:
                parts.append(from_before[at : at + reach])
            value = jnp.concatenate(parts, axis=0)
            tall[field * height : (field + 1) * height] = value
            here = lane // STRIP == place
            shift = (place + 1) * STRIP % LANES
            moved = value if shift == 0 else pltpu.roll(value, shift, 1)
            ends = jnp.where(here, moved, ends)
            moved = value if place == 0 else pltpu.roll(value, place * STRIP, 1)
            starts = jnp.where(here, moved, starts)
        part = slice(group * height, (group + 1) * height)
        odd[part] = jnp.where(first_of_pair, starts, ends)
        even[part] = jnp.where(first_of_pair, ends, starts)


def ocean_kernel(
    tile_rows, tall, from_odd, from_even, arrived, hot, level_out, replies, sources, history
):
    height = tall.shape[0] // FIELDS
    width = 2 * LANES
    per = LANES // STRIP
    river, coast = lax.axis_index("river"), lax.axis_index("coast")
    rivers, coasts = lax.axis_size("river"), lax.axis_size("coast")
    lane = lax.broadcasted_iota(i32, (height, LANES), 1)
    from_left = jnp.where(coast % 2 == 0, from_odd[...], from_even[...])
    from_right = jnp.where(coast % 2 == 0, from_even[...], from_odd[...])

    def whole(field):
        group, place = field // per, field % per
        rows = slice(group * height, (group + 1) * height)
        shift = (LANES - place * STRIP) % LANES
        after = from_right[rows] if shift == 0 else pltpu.roll(from_right[rows], shift, 1)
        shift = (LANES - (place + 1) * STRIP) % LANES
        before = from_left[rows] if shift == 0 else pltpu.roll(from_left[rows], shift, 1)
        beside = jnp.where(lane < STRIP, after, jnp.where(lane >= LANES - STRIP, before, 0.0))
        return jnp.concatenate([tall[field * height : (field + 1) * height], beside], axis=1)

    for step in range(STEPS):
        sources[step] = whole(step) * (step_seconds / (cell_metres * cell_metres))
    level, bed, east, north = [whole(STEPS + number) for number in range(4)]

    row = lax.broadcasted_iota(i32, (height, width), 0)
    column = lax.broadcasted_iota(i32, (height, width), 1)
    row_in = jnp.where(
        row < tile_rows, 1, jnp.where(row < tile_rows + HALO, (river < rivers - 1).astype(i32), (river > 0).astype(i32))
    )
    column_in = jnp.where(
        column < LANES, 1, jnp.where(column < LANES + LANES // 2, (coast < coasts - 1).astype(i32), (coast > 0).astype(i32))
    )
    inside = row_in * column_in == 1

    def next_row(value):
        return pltpu.roll(value, height - 1, 0)

    def next_column(value):
        return pltpu.roll(value, width - 1, 1)

    bed_east = jnp.maximum(bed, next_row(bed))
    bed_north = jnp.maximum(bed, next_column(bed))
    drive = gravity * step_seconds / cell_metres

    def ocean_turn(step, carry):
        level, east, north = carry
        east = flow_after(east, level, next_row(level), bed_east, drive, ocean_manning)
        north = flow_after(north, level, next_column(level), bed_north, drive, ocean_manning)
        spread = east - pltpu.roll(east, 1, 0) + north - pltpu.roll(north, 1, 1)
        level = level - step_seconds / cell_metres * spread + sources[step]
        level = jnp.where(inside, level, 0.0)
        for half in range(2):
            part = level[half * TALL : (half + 1) * TALL, :LANES]
            history[pl.ds(half * WIDE + step, TALL, stride=TALL)] = part
        return level, east, north

    history[...] = jnp.zeros_like(history)
    level, east, north = lax.fori_loop(0, STEPS, ocean_turn, (level, east, north))
    level_out[...] = level[:tile_rows, :LANES]

    halves = [history[:WIDE], history[WIDE:]]
    table = jnp.concatenate(in_two(jnp.concatenate(halves, axis=1)), axis=1)

    def reply(pair, carry):
        at = [2 * pair, 2 * pair + 1]
        cells = [arrived[pl.ds(s * SENT + STEPS, 1)] for s in at]
        rows, _ = cell_labels(jnp.concatenate(cells, axis=1).astype(i32), LANES)
        found = look_up(table, rows, hot[:, pl.ds(pl.multiple_of(pair * WIDE, WIDE), WIDE)])
        for half, s in enumerate(at):
            replies[pl.ds(s * STEPS, STEPS)] = found[:STEPS, half * LANES : (half + 1) * LANES]
        return carry

    lax.fori_loop(0, replies.shape[0] // STEPS // 2, reply, 0, unroll=2)


def mouth_kernel(returned, address, level_out, table, series, hot):
    rows = address.shape[0]
    groups = LANES // MPB
    for row in range(TALL):
        part = slice(row * TALL, (row + 1) * TALL)
        for half in range(2):
            at = (2 * row + half) * STEPS
            values = returned[at : at + STEPS]
            values = jnp.concatenate([values, jnp.zeros((TALL - STEPS, LANES), f32)], axis=0)
            high, low = in_two(values)
            table[part, half * LANES : (half + 1) * LANES] = high
            table[part, WIDE + half * LANES : WIDE + (half + 1) * LANES] = low
    for i in range(0, rows, 2):
        labels = jnp.concatenate([address[i : i + 1], address[i + 1 : i + 2]], axis=1)
        one_hot_columns(labels % WIDE, hot, slice(None))
        found = look_up(table[...], labels // WIDE, hot[...])
        series[pl.ds(i, TALL, stride=rows)] = found[:, :LANES]
        series[pl.ds(i + 1, TALL, stride=rows)] = found[:, LANES:]
    lane = lax.broadcasted_iota(i32, (rows, LANES), 1)
    for block in range(STEPS // groups):
        for g in range(groups):
            result = jnp.zeros((rows, LANES), f32)
            for place in range(groups):
                step = block * groups + place
                part = series[step * rows : (step + 1) * rows]
                shift = (place - g) * MPB % LANES
                part = part if shift == 0 else pltpu.roll(part, shift, 1)
                result = jnp.where(lane // MPB == place, part, result)
            level_out[g * rows : (g + 1) * rows, block * LANES : (block + 1) * LANES] = result


def shape(*dims, dtype=f32):
    return jax.ShapeDtypeStruct(dims, dtype)


def in_hbm(*arrays):
    return [pltpu.with_memory_space_constraint(whole, pltpu.HBM) for whole in arrays]


def swap(values, tall, devices, capacity):
    per = LANES // capacity
    if per > 1:
        values = values.reshape(devices // per, tall, per, capacity).transpose(0, 2, 1, 3)
    values = values.reshape(devices, 1, tall * capacity)
    values = lax.all_to_all(values, ("river", "coast"), split_axis=0, concat_axis=0, tiled=True)
    if per > 1:
        values = values.reshape(devices // per, per, tall, capacity).transpose(0, 2, 1, 3)
    return values.reshape(devices // per * tall, LANES)


def with_neighbours(odd, even, axis):
    size = lax.axis_size(axis)
    routes = [
        [(i + k, i + 1 - k) for i in range(start, size - 1, 2) for k in range(2)]
        for start in (1, 0)
    ]
    return lax.ppermute(odd, axis, routes[0]), lax.ppermute(even, axis, routes[1])


def per_device(
    reach_depth,
    reach_flow,
    reach_bed,
    reach_width,
    reach_length,
    runoff,
    flows_into,
    mouth_prev,
    mouth_tile,
    mouth_cell,
    sea_level,
    sea_bed,
    wet_mask,
    flux_east,
    flux_north,
):
    devices = lax.axis_size("river") * lax.axis_size("coast")
    blocks = reach_depth.shape[0]
    tile_rows, tile_cols = sea_level.shape
    mouths = blocks * MPB
    capacity = max(2, 2 * mouths // devices)
    groups = devices * capacity // LANES
    rows = mouths // LANES
    height = tile_rows + 2 * HALO

    depth_after, sending, address = pl.pallas_call(
        functools.partial(river_kernel, devices, capacity),
        name="river",
        out_shape=(
            shape(blocks, RB),
            shape(groups * SENT, LANES),
            shape(rows, LANES, dtype=i32),
        ),
        in_specs=[pl.BlockSpec(memory_space=pltpu.HBM)] * 10,
        out_specs=(
            pl.BlockSpec(memory_space=pltpu.HBM),
            pl.BlockSpec(memory_space=pltpu.VMEM),
            pl.BlockSpec(memory_space=pltpu.VMEM),
        ),
        scratch_shapes=[pltpu.VMEM((blocks, RB), f32)] * 6
        + [
            pltpu.VMEM((blocks, RB), i32),
            pltpu.VMEM((MPB, blocks), f32),
            pltpu.VMEM((MPB, blocks), i32),
            pltpu.VMEM((MPB, blocks), i32),
            pltpu.SemaphoreType.DMA((11,)),
            pltpu.VMEM((blocks, RB), f32),
            pltpu.VMEM((reach_offsets, blocks, RB), f32),
            pltpu.VMEM((TALL * rows, LANES), f32),
            pltpu.VMEM((RB, LANES), f32),
            pltpu.VMEM((rows, LANES), i32),
            pltpu.VMEM((rows * devices, LANES), bf16),
            pltpu.VMEM((2 * WIDE, mouths), bf16),
            pltpu.VMEM((WIDE, mouths), bf16),
        ],
        compiler_params=PARAMS,
    )(
        *in_hbm(
            reach_depth,
            reach_flow,
            reach_bed,
            reach_width,
            reach_length,
            runoff,
            flows_into,
            mouth_prev.T,
            mouth_tile[:, :, 0].T,
            mouth_cell.T,
        )
    )
    arrived = swap(sending, SENT, devices, capacity)

    fields, odd, even, hot = pl.pallas_call(
        source_kernel,
        name="sources",
        out_shape=(
            shape(FIELDS * tile_rows, LANES),
            shape(ROWS_SENT, LANES),
            shape(ROWS_SENT, LANES),
            shape(WIDE, groups * LANES, dtype=bf16),
        ),
        in_specs=[pl.BlockSpec(memory_space=pltpu.VMEM)]
        + [pl.BlockSpec(memory_space=pltpu.HBM)] * 5,
        scratch_shapes=[
            pltpu.VMEM((tile_rows, tile_cols), f32),
            pltpu.VMEM((tile_rows, tile_cols), f32),
            pltpu.VMEM((tile_rows, tile_cols), i32),
            pltpu.VMEM((tile_rows, tile_cols), f32),
            pltpu.VMEM((tile_rows, tile_cols), f32),
            pltpu.SemaphoreType.DMA((5,)),
            pltpu.VMEM((2 * WIDE, groups * LANES), bf16),
            pltpu.VMEM((2 * WIDE, LANES), f32),
        ],
        compiler_params=PARAMS,
    )(arrived, *in_hbm(sea_level, sea_bed, wet_mask, flux_east, flux_north))
    from_odd, from_even = with_neighbours(odd, even, "river")

    strips = FIELDS * STRIP // LANES * height
    tall, odd, even = pl.pallas_call(
        strip_kernel,
        name="strips",
        out_shape=(shape(FIELDS * height, LANES), shape(strips, LANES), shape(strips, LANES)),
        compiler_params=PARAMS,
    )(fields, from_odd, from_even)
    from_odd, from_even = with_neighbours(odd, even, "coast")

    level_after, replies = pl.pallas_call(
        functools.partial(ocean_kernel, tile_rows),
        name="ocean",
        out_shape=(shape(tile_rows, tile_cols), shape(groups * STEPS, LANES)),
        scratch_shapes=[
            pltpu.VMEM((STEPS, height, 2 * LANES), f32),
            pltpu.VMEM((2 * WIDE, LANES), f32),
        ],
        compiler_params=PARAMS,
    )(tall, from_odd, from_even, arrived, hot)
    returned = swap(replies, STEPS, devices, capacity)

    mouth_level = pl.pallas_call(
        mouth_kernel,
        name="mouths",
        out_shape=shape(blocks, STEPS * MPB),
        scratch_shapes=[
            pltpu.VMEM((WIDE, 2 * WIDE), bf16),
            pltpu.VMEM((TALL * rows, LANES), f32),
            pltpu.VMEM((WIDE, WIDE), bf16),
        ],
        compiler_params=PARAMS,
    )(returned, address)
    return (depth_after, level_after, mouth_level)


def solution(mesh):
    by_block = P(("river", "coast"), None)
    tiled = P("river", "coast")
    return jax.shard_map(
        per_device,
        mesh=mesh,
        in_specs=(by_block,) * 8
        + (P(("river", "coast"), None, None), by_block)
        + (tiled,) * 5,
        out_specs=(by_block, tiled, by_block),
        check_vma=False,
    )
```

```python
import functools
import math

import jax
import jax.numpy as jnp
from jax import lax
from jax.experimental import pallas as pl
from jax.experimental.pallas import tpu as pltpu
from jax.sharding import PartitionSpec as P

RB = 128
MPB = 32
STEPS = 12

gravity = 9.81
step_seconds = 300.0
cell_metres = 3000.0
river_manning = 0.035
ocean_manning = 0.025
depth_floor = 0.05
reach_offsets = 16

LANES = 128
SENT = 13
TALL = 16
WIDE = 256
PARTS = ((0, 8), (8, 4))
CHUNK = 8
HALO = 12
FIELDS = 16
f32, bf16, i32 = jnp.float32, jnp.bfloat16, jnp.int32

PARAMS = pltpu.CompilerParams(vmem_limit_bytes=40 * 1024 * 1024)


def flow_after(unit_flow, upper, lower, bed_top, drive, manning):
    face_depth = jnp.maximum(upper, lower) - bed_top
    driving = drive * jnp.maximum(face_depth, 0.0) * (upper - lower)
    power = -7.0 / 3.0 * math.log2(math.e)
    thin = jnp.exp2(jnp.log(jnp.maximum(face_depth, depth_floor)) * power)
    friction = (gravity * step_seconds * manning * manning) * jnp.abs(unit_flow) * thin
    divisor = 1.0 + friction
    inverse = pl.reciprocal(divisor, approx=True)
    inverse = inverse * (2.0 - divisor * inverse)
    return (unit_flow + driving) * inverse


def in_two(values):
    high = values.astype(bf16)
    return high, (values - high.astype(f32)).astype(bf16)


def small(labels):
    return jnp.broadcast_to(labels.astype(f32), (TALL, labels.shape[1])).astype(bf16)


def one_hot_columns(columns, rhs, lanes):
    labels = small(columns)
    place = lax.broadcasted_iota(i32, labels.shape, 0).astype(f32).astype(bf16)
    one, none = jnp.ones(labels.shape, bf16), jnp.zeros(labels.shape, bf16)
    for part in range(WIDE // TALL):
        hit = labels - part * TALL == place
        rhs[part * TALL : (part + 1) * TALL, lanes] = jnp.where(hit, one, none)


def row_owners(owner, steps):
    for part in range(0, TALL * steps, TALL):
        number = part + lax.broadcasted_iota(i32, (TALL, LANES), 0)
        owner[part : part + TALL] = (number // steps).astype(f32).astype(bf16)


def in_turn(series, at, stride, steps, first):
    parts, row = [], first
    while row < first + 8:
        step = row % steps
        count = min(steps - step, first + 8 - row)
        parts.append(series[pl.ds(at + step * stride, count, stride=stride)])
        row += count
    return parts[0] if len(parts) == 1 else jnp.concatenate(parts, axis=0)


def lay_out(series, at, stride, steps, rows, owner, lhs, lanes):
    turns = math.lcm(steps, 8) // 8
    cycle = [in_turn(series, at, stride, steps, 8 * turn) for turn in range(turns)]
    pairs = [(cycle[2 * k % turns], cycle[(2 * k + 1) % turns]) for k in range(turns)]
    halves = [in_two(jnp.concatenate(pair, axis=0)) for pair in pairs]
    labels = small(rows)
    none = jnp.zeros(labels.shape, bf16)
    for part in range(steps):
        at_rows = slice(part * TALL, (part + 1) * TALL)
        hit = labels == owner[at_rows]
        for number, half in enumerate(halves[part % turns]):
            at_rows = slice((number * steps + part) * TALL, (number * steps + part + 1) * TALL)
            lhs[at_rows, lanes] = jnp.where(hit, half, none)


def look_up(table, rows, hot, steps):
    found = jnp.dot(table, hot, preferred_element_type=f32)
    per = 2 if steps > 6 else 4
    several = (per * steps, rows.shape[1])
    labels = jnp.broadcast_to(rows, several) - lax.broadcasted_iota(i32, several, 0) // steps
    total = jnp.zeros(several, f32)
    for row in range(0, TALL, per):
        high = found[row * steps : (row + per) * steps]
        low = found[(TALL + row) * steps : (TALL + row + per) * steps]
        total = total + jnp.where(labels == row, high + low, 0.0)
    result = total[:steps]
    for number in range(1, per):
        result = result + total[number * steps : (number + 1) * steps]
    return result


def cell_labels(cells, tile_cols):
    row, column = cells // tile_cols, cells % tile_cols
    return row % TALL, row // TALL * tile_cols + column


def river_kernel(
    devices,
    capacity,
    *refs,
):
    inputs, (depth_out, send_out, address_out), refs = refs[:10], refs[10:13], refs[13:]
    copies = [
        pltpu.make_async_copy(whole, own, refs[10].at[number])
        for number, (whole, own) in enumerate(zip(inputs, refs[:10]))
    ]
    for copy in copies[::-1]:
        copy.start()
    river_steps(devices, capacity, copies, *refs[:10], depth_out, send_out, address_out, *refs[10:])


def river_steps(
    devices,
    capacity,
    copies,
    depth_in,
    flow_in,
    bed_in,
    width_in,
    length_in,
    runoff_in,
    into_in,
    prev_in,
    tile_in,
    cell_in,
    depth_out,
    send_out,
    address_out,
    arrivals,
    depth_end,
    enters,
    series,
    turned,
    tiles,
    hots,
    owner_first,
    owner_last,
    lhs_first,
    lhs_last,
    rhs,
):
    blocks = depth_in.shape[0]
    groups = LANES // MPB
    rows = blocks // groups
    inland = RB - MPB
    lane = lax.broadcasted_iota(i32, (blocks, RB), 1)

    for copy in copies[7:]:
        copy.wait()

    turned[...] = jnp.zeros_like(turned)
    turned[0:MPB, 0:blocks] = tile_in[...].astype(f32)
    turned[MPB : 2 * MPB, 0:blocks] = cell_in[...].astype(f32)
    turned[inland:RB, 0:blocks] = prev_in[...]
    mouths = jnp.transpose(turned[...])[0:blocks]
    prev = mouths

    def grouped(array, first):
        lanes16 = lax.broadcasted_iota(i32, (rows, LANES), 1)
        result = jnp.zeros((rows, LANES), f32)
        for g in range(groups):
            part = array[g * rows : (g + 1) * rows]
            shift = (g * MPB - first) % LANES
            part = part if shift == 0 else pltpu.roll(part, shift, 1)
            result = jnp.where(lanes16 // MPB == g, part, result)
        return result

    tiles[...] = grouped(mouths, 0).astype(i32)
    series[STEPS * rows :] = grouped(mouths, MPB)

    for i in range(rows):
        names = jnp.broadcast_to(tiles[i : i + 1], (devices, LANES))
        hit = names == lax.broadcasted_iota(i32, (devices, LANES), 0)
        hots[i * devices : (i + 1) * devices] = jnp.where(hit, 1.0, 0.0).astype(bf16)
    shape = (LANES, 2 * LANES)
    earlier = lax.broadcasted_iota(i32, shape, 0) < lax.broadcasted_iota(i32, shape, 1)
    counted = jnp.dot(
        hots[...], jnp.where(earlier, 1.0, 0.0).astype(bf16), preferred_element_type=f32
    )
    before = jnp.zeros((devices, LANES), f32)
    for i in range(rows):
        part = slice(i * devices, (i + 1) * devices)
        ranks = (counted[part, :LANES] + before) * hots[part].astype(f32)
        rank = jnp.sum(ranks, axis=0, keepdims=True).astype(i32)
        address_out[i : i + 1] = tiles[i : i + 1] * capacity + rank
        before = before + counted[part, LANES:]

    for copy in copies[:7]:
        copy.wait()
    into = into_in[...]
    at_mouth = lane >= inland
    down = jnp.where(at_mouth, 0, into)
    offset = jnp.where(at_mouth, 0, into - lane)
    bed = bed_in[...]
    bed_top = jnp.where(
        at_mouth, bed, jnp.maximum(bed, jnp.take_along_axis(bed, down, axis=1))
    )
    drive = gravity * step_seconds / length_in[...]
    area = step_seconds / (width_in[...] * length_in[...])
    for o in range(1, reach_offsets + 1):
        enters[o - 1] = jnp.where(turn(offset, o) == o, 1.0, 0.0)

    def river_turn(substep, depth, flow):
        surface = bed + depth
        below = jnp.where(at_mouth, prev, jnp.take_along_axis(surface, down, axis=1))
        flow = flow_after(flow, surface, below, bed_top, drive, river_manning)
        discharge = flow * width_in[...]
        sums = [
            enters[o] * turn(discharge, o + 1) + enters[o + 1] * turn(discharge, o + 2)
            for o in range(0, reach_offsets, 2)
        ]
        while len(sums) > 1:
            sums = [one + other for one, other in zip(sums[::2], sums[1::2])]
        depth = depth + area * (sums[0] + (runoff_in[...] - discharge))
        series[substep * rows : (substep + 1) * rows] = grouped(discharge, inland)
        return depth, flow

    columns = jnp.transpose((address_out[...] % WIDE).astype(f32))
    place = lax.broadcasted_iota(i32, (LANES, LANES), 1).astype(f32).astype(bf16)
    one, none = jnp.ones((LANES, LANES), bf16), jnp.zeros((LANES, LANES), bf16)
    number = lax.broadcasted_iota(i32, (TALL, LANES), 0)
    for i in range(rows):
        lanes = slice(i * LANES, (i + 1) * LANES)
        column = jnp.broadcast_to(columns[:, i : i + 1], (LANES, LANES)).astype(bf16)
        for half in range(2):
            hit = column - half * LANES == place
            rhs[lanes, half * LANES : (half + 1) * LANES] = jnp.where(hit, one, none)

    depth, flow = depth_in[...], flow_in[...]
    for (first, steps), owner, lhs in zip(PARTS, (owner_first, owner_last), (lhs_first, lhs_last)):
        high_rows = TALL * steps
        row_owners(owner, steps)
        for substep in range(first, first + steps):
            depth, flow = river_turn(substep, depth, flow)
        if first:
            depth_end[...] = depth
            finished = pltpu.make_async_copy(depth_end, depth_out, arrivals.at[len(copies)])
            finished.start()
        for i in range(rows):
            lanes = slice(i * LANES, (i + 1) * LANES)
            high_label = address_out[i : i + 1] // WIDE
            lay_out(series, first * rows + i, rows, steps, high_label, owner, lhs, lanes)
            if not first:
                cells = series[STEPS * rows + i : STEPS * rows + i + 1]
                cells = jnp.where(number == high_label, cells, 0.0)
                for half, part in enumerate(in_two(cells)):
                    at = 2 * high_rows + half * TALL
                    lhs[at : at + TALL, lanes] = part
        both = jnp.dot(lhs[...], rhs[...], preferred_element_type=f32)
        packed = both[:high_rows] + both[high_rows : 2 * high_rows]
        for half in range(2):
            lanes = slice(half * LANES, (half + 1) * LANES)
            for row in range(TALL):
                at = (2 * row + half) * SENT + first
                send_out[at : at + steps] = packed[row * steps : (row + 1) * steps, lanes]
            if not first:
                cells = both[2 * high_rows : 2 * high_rows + TALL] + both[2 * high_rows + TALL :]
                send_out[pl.ds(half * SENT + STEPS, TALL, stride=2 * SENT)] = cells[:, lanes]
    finished.wait()


def reach_of(field):
    return STEPS - 1 - field if field < STEPS else HALO


def turn(value, lanes):
    lanes %= value.shape[1]
    return value if lanes == 0 else pltpu.roll(value, lanes, 1)


ROW_AT = [sum(reach_of(f) for f in range(field)) for field in range(FIELDS + 1)]
ROWS_SENT = -(-ROW_AT[FIELDS] // 8) * 8


def source_kernel(arrived, *refs):
    inputs, (fields, odd, even, rhs), refs = refs[:5], refs[5:9], refs[9:]
    first_of_pair = lax.axis_index("river") % 2 == 0
    sea_level, sea_bed, wet_mask, flux_east, flux_north, arrivals, owner, lhs, sums = refs
    copies = [
        pltpu.make_async_copy(whole, own, arrivals.at[number])
        for number, (whole, own) in enumerate(zip(inputs, refs[:5]))
    ]
    for copy in copies:
        copy.start()
    groups = arrived.shape[0] // SENT
    tile_rows, tile_cols = sea_level.shape

    high_rows = TALL * STEPS
    row_owners(owner, STEPS)
    both = jnp.zeros((2 * high_rows, WIDE), f32)
    for chunk in range(0, groups, CHUNK):
        for s in range(chunk, chunk + CHUNK):
            at = s * SENT
            lanes = slice(s * LANES, (s + 1) * LANES)
            cells = arrived[at + STEPS : at + SENT].astype(i32)
            rows, columns = cell_labels(cells, tile_cols)
            lay_out(arrived, at, 1, STEPS, rows, owner, lhs, lanes)
            one_hot_columns(columns, rhs, lanes)
        lanes = slice(chunk * LANES, (chunk + CHUNK) * LANES)
        both = both + lax.dot_general(
            lhs[:, lanes], rhs[:, lanes], (((1,), (1,)), ((), ())), preferred_element_type=f32
        )
    total = both[:high_rows] + both[high_rows:]
    for half in range(2):
        part = slice(half * high_rows, (half + 1) * high_rows)
        sums[part] = total[:, half * LANES : (half + 1) * LANES]
    for copy in copies:
        copy.wait()
    bed = sea_bed[...]
    level = jnp.where(wet_mask[...] == 1, jnp.maximum(sea_level[...], bed), bed)

    def put(field, value):
        fields[field * tile_rows : (field + 1) * tile_rows] = value
        reach = reach_of(field)
        if reach:
            last, first = value[tile_rows - reach :], value[:reach]
            part = slice(ROW_AT[field], ROW_AT[field] + reach)
            odd[part] = jnp.where(first_of_pair, first, last)
            even[part] = jnp.where(first_of_pair, last, first)

    for swap_out in (odd, even):
        swap_out[ROWS_SENT - 8 :] = jnp.zeros((8, LANES), f32)
    for step in range(STEPS):
        halves = [sums[pl.ds(half * high_rows + step, TALL, stride=STEPS)] for half in range(2)]
        put(step, jnp.concatenate(halves, axis=0))
    for number, value in enumerate((level, bed, flux_east[...], flux_north[...])):
        put(STEPS + number, value)


def strip_kernel(fields, from_odd, from_even, tall, odd, even):
    upper = lax.axis_index("river") % 2 == 0
    first_of_pair = lax.axis_index("coast") % 2 == 0
    from_before = jnp.where(upper, from_odd[...], from_even[...])
    from_after = jnp.where(upper, from_even[...], from_odd[...])
    tile_rows = fields.shape[0] // FIELDS
    height = tall.shape[0] // FIELDS
    lane = lax.broadcasted_iota(i32, (height, LANES), 1)
    ends = jnp.zeros((height, LANES), f32)
    starts = jnp.zeros((height, LANES), f32)
    for field in range(FIELDS):
        reach, at = reach_of(field), ROW_AT[field]
        parts = [fields[field * tile_rows : (field + 1) * tile_rows]]
        if reach:
            parts.append(from_after[at : at + reach])
        if reach < HALO:
            parts.append(jnp.zeros((2 * HALO - 2 * reach, LANES), f32))
        if reach:
            parts.append(from_before[at : at + reach])
        value = jnp.concatenate(parts, axis=0)
        tall[field * height : (field + 1) * height] = value
        if reach:
            here = (lane >= at) & (lane < at + reach)
            ends = jnp.where(here, turn(value, at + reach - LANES), ends)
            starts = jnp.where(here, turn(value, at), starts)
    odd[...] = jnp.where(first_of_pair, starts, ends)
    even[...] = jnp.where(first_of_pair, ends, starts)


def ocean_kernel(
    tile_rows, tall, from_odd, from_even, arrived, hot, level_out, replies, sources, history
):
    height = tall.shape[0] // FIELDS
    width = 2 * LANES
    river, coast = lax.axis_index("river"), lax.axis_index("coast")
    rivers, coasts = lax.axis_size("river"), lax.axis_size("coast")
    lane = lax.broadcasted_iota(i32, (height, LANES), 1)
    from_left = jnp.where(coast % 2 == 0, from_odd[...], from_even[...])
    from_right = jnp.where(coast % 2 == 0, from_even[...], from_odd[...])

    def whole(field):
        reach, at = reach_of(field), ROW_AT[field]
        beside = jnp.zeros((height, LANES), f32)
        if reach:
            beside = jnp.where(lane < reach, turn(from_right, -at), beside)
            beside = jnp.where(lane >= LANES - reach, turn(from_left, -at - reach), beside)
        return jnp.concatenate([tall[field * height : (field + 1) * height], beside], axis=1)

    for step in range(STEPS):
        sources[step] = whole(step) * (step_seconds / (cell_metres * cell_metres))
    level, bed, east, north = [whole(STEPS + number) for number in range(4)]

    row = lax.broadcasted_iota(i32, (height, width), 0)
    column = lax.broadcasted_iota(i32, (height, width), 1)
    row_in = jnp.where(
        row < tile_rows, 1, jnp.where(row < tile_rows + HALO, (river < rivers - 1).astype(i32), (river > 0).astype(i32))
    )
    column_in = jnp.where(
        column < LANES, 1, jnp.where(column < LANES + LANES // 2, (coast < coasts - 1).astype(i32), (coast > 0).astype(i32))
    )
    inside = row_in * column_in == 1

    def next_row(value):
        return pltpu.roll(value, height - 1, 0)

    def next_column(value):
        return pltpu.roll(value, width - 1, 1)

    bed_east = jnp.maximum(bed, next_row(bed))
    bed_north = jnp.maximum(bed, next_column(bed))
    drive = gravity * step_seconds / cell_metres

    def ocean_turn(first, steps, step, level, east, north):
        east = flow_after(east, level, next_row(level), bed_east, drive, ocean_manning)
        north = flow_after(north, level, next_column(level), bed_north, drive, ocean_manning)
        spread = east - pltpu.roll(east, 1, 0) + north - pltpu.roll(north, 1, 1)
        level = level - step_seconds / cell_metres * spread + sources[step]
        level = jnp.where(inside, level, 0.0)
        for half in range(2):
            part = level[half * TALL : (half + 1) * TALL, :LANES]
            at = TALL * (2 * first + half * steps) + step - first
            history[pl.ds(at, TALL, stride=steps)] = part
        return level, east, north

    for first, steps in PARTS:
        high_rows = TALL * steps
        for step in range(first, first + steps):
            level, east, north = ocean_turn(first, steps, step, level, east, north)
        if first:
            level_out[...] = level[:tile_rows, :LANES]
        at = 2 * TALL * first
        halves = [history[at + half * high_rows : at + (half + 1) * high_rows] for half in range(2)]
        table = jnp.concatenate(in_two(jnp.concatenate(halves, axis=1)), axis=0)
        for s in range(0, replies.shape[0] // STEPS, 2):
            cells = [arrived[(s + i) * SENT + STEPS : (s + i + 1) * SENT] for i in range(2)]
            rows, _ = cell_labels(jnp.concatenate(cells, axis=1).astype(i32), LANES)
            found = look_up(table, rows, hot[:, s * LANES : (s + 2) * LANES], steps)
            for half in range(2):
                at = (s + half) * STEPS + first
                replies[at : at + steps] = found[:, half * LANES : (half + 1) * LANES]


def mouth_kernel(returned, address, level_out, whole, series, hot, block, departures):
    rows = address.shape[0]
    groups = LANES // MPB
    labels = []
    for i in range(0, rows, 2):
        pair = jnp.concatenate([address[i : i + 1], address[i + 1 : i + 2]], axis=1)
        one_hot_columns(pair % WIDE, hot, slice(i * LANES, (i + 2) * LANES))
        labels.append(pair // WIDE)
    lane = lax.broadcasted_iota(i32, (rows, LANES), 1)
    copies = []
    for first in range(0, STEPS, groups):
        for row in range(TALL):
            for half in range(2):
                at = (2 * row + half) * STEPS + first
                to = first * TALL + row * groups
                lanes = slice(half * LANES, (half + 1) * LANES)
                whole[to : to + groups, lanes] = returned[at : at + groups]
        own = whole[first * TALL : (first + groups) * TALL]
        table = jnp.concatenate(in_two(own), axis=0)
        for i in range(0, rows, 2):
            lanes = slice(i * LANES, (i + 2) * LANES)
            found = look_up(table, labels[i // 2], hot[:, lanes], groups)
            series[pl.ds(first * rows + i, groups, stride=rows)] = found[:, :LANES]
            series[pl.ds(first * rows + i + 1, groups, stride=rows)] = found[:, LANES:]
        number = first // groups
        for g in range(groups):
            result = jnp.zeros((rows, LANES), f32)
            for place in range(groups):
                at = (first + place) * rows
                part = turn(series[at : at + rows], (place - g) * MPB)
                result = jnp.where(lane // MPB == place, part, result)
            block[number, g * rows : (g + 1) * rows] = result
        to = level_out.at[:, pl.ds(number * LANES, LANES)]
        copies.append(pltpu.make_async_copy(block.at[number], to, departures.at[number]))
        copies[-1].start()
    for copy in copies:
        copy.wait()


def shape(*dims, dtype=f32):
    return jax.ShapeDtypeStruct(dims, dtype)


def in_hbm(*arrays):
    return [pltpu.with_memory_space_constraint(whole, pltpu.HBM) for whole in arrays]


def swap(values, tall, devices, capacity):
    per = LANES // capacity
    if per > 1:
        values = values.reshape(devices // per, tall, per, capacity).transpose(0, 2, 1, 3)
    values = values.reshape(devices, 1, tall * capacity)
    values = lax.all_to_all(values, ("river", "coast"), split_axis=0, concat_axis=0, tiled=True)
    if per > 1:
        values = values.reshape(devices // per, per, tall, capacity).transpose(0, 2, 1, 3)
    return values.reshape(devices // per * tall, LANES)


def with_neighbours(odd, even, axis):
    size = lax.axis_size(axis)
    routes = [
        [(i + k, i + 1 - k) for i in range(start, size - 1, 2) for k in range(2)]
        for start in (1, 0)
    ]
    return lax.ppermute(odd, axis, routes[0]), lax.ppermute(even, axis, routes[1])


def per_device(
    reach_depth,
    reach_flow,
    reach_bed,
    reach_width,
    reach_length,
    runoff,
    flows_into,
    mouth_prev,
    mouth_tile,
    mouth_cell,
    sea_level,
    sea_bed,
    wet_mask,
    flux_east,
    flux_north,
):
    devices = lax.axis_size("river") * lax.axis_size("coast")
    blocks = reach_depth.shape[0]
    tile_rows, tile_cols = sea_level.shape
    mouths = blocks * MPB
    capacity = max(2, 2 * mouths // devices)
    groups = devices * capacity // LANES
    rows = mouths // LANES
    height = tile_rows + 2 * HALO

    depth_after, sending, address = pl.pallas_call(
        functools.partial(river_kernel, devices, capacity),
        name="river",
        out_shape=(
            shape(blocks, RB),
            shape(groups * SENT, LANES),
            shape(rows, LANES, dtype=i32),
        ),
        in_specs=[pl.BlockSpec(memory_space=pltpu.HBM)] * 10,
        out_specs=(
            pl.BlockSpec(memory_space=pltpu.HBM),
            pl.BlockSpec(memory_space=pltpu.VMEM),
            pl.BlockSpec(memory_space=pltpu.VMEM),
        ),
        scratch_shapes=[pltpu.VMEM((blocks, RB), f32)] * 6
        + [
            pltpu.VMEM((blocks, RB), i32),
            pltpu.VMEM((MPB, blocks), f32),
            pltpu.VMEM((MPB, blocks), i32),
            pltpu.VMEM((MPB, blocks), i32),
            pltpu.SemaphoreType.DMA((11,)),
            pltpu.VMEM((blocks, RB), f32),
            pltpu.VMEM((reach_offsets, blocks, RB), f32),
            pltpu.VMEM((SENT * rows, LANES), f32),
            pltpu.VMEM((RB, LANES), f32),
            pltpu.VMEM((rows, LANES), i32),
            pltpu.VMEM((rows * devices, LANES), bf16),
            *[pltpu.VMEM((TALL * steps, LANES), bf16) for _, steps in PARTS],
            pltpu.VMEM((2 * TALL * (PARTS[0][1] + 1), mouths), bf16),
            pltpu.VMEM((2 * TALL * PARTS[1][1], mouths), bf16),
            pltpu.VMEM((mouths, WIDE), bf16),
        ],
        compiler_params=PARAMS,
    )(
        *in_hbm(
            reach_depth,
            reach_flow,
            reach_bed,
            reach_width,
            reach_length,
            runoff,
            flows_into,
            mouth_prev.T,
            mouth_tile[:, :, 0].T,
            mouth_cell.T,
        )
    )
    arrived = swap(sending, SENT, devices, capacity)

    fields, odd, even, hot = pl.pallas_call(
        source_kernel,
        name="sources",
        out_shape=(
            shape(FIELDS * tile_rows, LANES),
            shape(ROWS_SENT, LANES),
            shape(ROWS_SENT, LANES),
            shape(WIDE, groups * LANES, dtype=bf16),
        ),
        in_specs=[pl.BlockSpec(memory_space=pltpu.VMEM)]
        + [pl.BlockSpec(memory_space=pltpu.HBM)] * 5,
        scratch_shapes=[
            pltpu.VMEM((tile_rows, tile_cols), f32),
            pltpu.VMEM((tile_rows, tile_cols), f32),
            pltpu.VMEM((tile_rows, tile_cols), i32),
            pltpu.VMEM((tile_rows, tile_cols), f32),
            pltpu.VMEM((tile_rows, tile_cols), f32),
            pltpu.SemaphoreType.DMA((5,)),
            pltpu.VMEM((TALL * STEPS, LANES), bf16),
            pltpu.VMEM((2 * TALL * STEPS, groups * LANES), bf16),
            pltpu.VMEM((2 * TALL * STEPS, LANES), f32),
        ],
        compiler_params=PARAMS,
    )(arrived, *in_hbm(sea_level, sea_bed, wet_mask, flux_east, flux_north))
    from_odd, from_even = with_neighbours(odd, even, "river")

    tall, odd, even = pl.pallas_call(
        strip_kernel,
        name="strips",
        out_shape=(shape(FIELDS * height, LANES), shape(height, LANES), shape(height, LANES)),
        compiler_params=PARAMS,
    )(fields, from_odd, from_even)
    from_odd, from_even = with_neighbours(odd, even, "coast")

    level_after, replies = pl.pallas_call(
        functools.partial(ocean_kernel, tile_rows),
        name="ocean",
        out_shape=(shape(tile_rows, tile_cols), shape(groups * STEPS, LANES)),
        scratch_shapes=[
            pltpu.VMEM((STEPS, height, 2 * LANES), f32),
            pltpu.VMEM((2 * TALL * STEPS, LANES), f32),
        ],
        compiler_params=PARAMS,
    )(tall, from_odd, from_even, arrived, hot)
    returned = swap(replies, STEPS, devices, capacity)

    mouth_level = pl.pallas_call(
        mouth_kernel,
        name="mouths",
        out_shape=shape(blocks, STEPS * MPB),
        scratch_shapes=[
            pltpu.VMEM((TALL * STEPS, WIDE), f32),
            pltpu.VMEM((STEPS * rows, LANES), f32),
            pltpu.VMEM((WIDE, mouths), bf16),
            pltpu.VMEM((STEPS * MPB // LANES, blocks, LANES), f32),
            pltpu.SemaphoreType.DMA((STEPS * MPB // LANES,)),
        ],
        out_specs=pl.BlockSpec(memory_space=pltpu.HBM),
        compiler_params=PARAMS,
    )(returned, address)
    return (depth_after, level_after, mouth_level)


def solution(mesh):
    by_block = P(("river", "coast"), None)
    tiled = P("river", "coast")
    return jax.shard_map(
        per_device,
        mesh=mesh,
        in_specs=(by_block,) * 8
        + (P(("river", "coast"), None, None), by_block)
        + (tiled,) * 5,
        out_specs=(by_block, tiled, by_block),
        check_vma=False,
    )
```

```python
import functools
import math

import jax
import jax.numpy as jnp
from jax import lax
from jax.experimental import pallas as pl
from jax.experimental.pallas import tpu as pltpu
from jax.sharding import PartitionSpec as P

RB = 128
MPB = 32
STEPS = 12

gravity = 9.81
step_seconds = 300.0
cell_metres = 3000.0
river_manning = 0.035
ocean_manning = 0.025
depth_floor = 0.05
reach_offsets = 16

LANES = 128
SENT = 13
TALL = 16
WIDE = 256
PARTS = ((0, 8), (8, 2), (10, 2))
LOOKED_UP = ((0, 8), (8, 4))
CHUNK = 8
HALO = 12
FIELDS = 16
f32, bf16, i32 = jnp.float32, jnp.bfloat16, jnp.int32

PARAMS = pltpu.CompilerParams(vmem_limit_bytes=40 * 1024 * 1024)


def flow_after(unit_flow, upper, lower, bed_top, drive, manning):
    face_depth = jnp.maximum(upper, lower) - bed_top
    driving = drive * jnp.maximum(face_depth, 0.0) * (upper - lower)
    power = -7.0 / 3.0 * math.log2(math.e)
    thin = jnp.exp2(jnp.log(jnp.maximum(face_depth, depth_floor)) * power)
    friction = (gravity * step_seconds * manning * manning) * jnp.abs(unit_flow) * thin
    divisor = 1.0 + friction
    inverse = pl.reciprocal(divisor, approx=True)
    return ((unit_flow + driving) * inverse) * (2.0 - divisor * inverse)


def in_two(values):
    high = values.astype(bf16)
    return high, (values - high.astype(f32)).astype(bf16)


def small(labels):
    return jnp.broadcast_to(labels, (TALL, labels.shape[1])).astype(bf16)


def one_hot_columns(columns, place_of, rhs, lanes):
    labels = small(columns)
    one, none = jnp.ones(labels.shape, bf16), jnp.zeros(labels.shape, bf16)
    for part in range(0, WIDE, TALL):
        hit = place_of(labels, part)
        rhs[part : part + TALL, lanes] = jnp.where(hit, one, none)


def row_owners(owner, steps):
    for part in range(0, owner.shape[0], TALL):
        number = part + lax.broadcasted_iota(i32, (TALL, LANES), 0)
        owner[part : part + TALL] = (number // steps).astype(f32).astype(bf16)


def in_turn(series, at, stride, steps, first):
    parts, row = [], first
    while row < first + 8:
        step = row % steps
        count = min(steps - step, first + 8 - row)
        parts.append(series[pl.ds(at + step * stride, count, stride=stride)])
        row += count
    return parts[0] if len(parts) == 1 else jnp.concatenate(parts, axis=0)


def lay_out(series, at, stride, steps, rows, owner, lhs, lanes):
    turns = math.lcm(steps, 8) // 8
    cycle = [in_turn(series, at, stride, steps, 8 * turn) for turn in range(turns)]
    pairs = [(cycle[2 * k % turns], cycle[(2 * k + 1) % turns]) for k in range(turns)]
    halves = [in_two(jnp.concatenate(pair, axis=0)) for pair in pairs]
    labels = small(rows)
    none = jnp.zeros(labels.shape, bf16)
    for part in range(steps):
        at_rows = slice(part * TALL, (part + 1) * TALL)
        hit = labels == owner[at_rows]
        for number, half in enumerate(halves[part % turns]):
            at_rows = slice((number * steps + part) * TALL, (number * steps + part + 1) * TALL)
            lhs[at_rows, lanes] = jnp.where(hit, half, none)


def look_up(table, rows, hot, steps):
    found = jnp.dot(table, hot, preferred_element_type=f32)
    per = 2 if steps > 6 else 4
    several = (per * steps, rows.shape[1])
    number = (lax.broadcasted_iota(i32, several, 0) // steps).astype(f32)
    labels = jnp.broadcast_to(rows, several) - number
    total = jnp.zeros(several, f32)
    for row in range(0, TALL, per):
        high = found[row * steps : (row + per) * steps]
        low = found[(TALL + row) * steps : (TALL + row + per) * steps]
        total = total + jnp.where(labels == row, high + low, 0.0)
    result = total[:steps]
    for number in range(1, per):
        result = result + total[number * steps : (number + 1) * steps]
    return result


def split_label(number, size):
    return lax.shift_right_logical(number, size.bit_length() - 1), number & (size - 1)


def cell_labels(cells, tile_cols):
    row, column = split_label(cells, tile_cols)
    upper, row = split_label(row, TALL)
    return row, upper * tile_cols + column


def river_kernel(
    devices,
    coasts,
    capacity,
    *refs,
):
    inputs, (depth_out, send_out, address_out), refs = refs[:10], refs[10:13], refs[13:]
    copies = [
        pltpu.make_async_copy(whole, own, refs[10].at[number])
        for number, (whole, own) in enumerate(zip(inputs, refs[:10]))
    ]
    for copy in copies[::-1]:
        copy.start()
    river_steps(devices, coasts, capacity, copies, *refs[:10], depth_out, send_out, address_out, *refs[10:])


def river_steps(
    devices,
    coasts,
    capacity,
    copies,
    depth_in,
    flow_in,
    bed_in,
    width_in,
    length_in,
    runoff_in,
    into_in,
    prev_in,
    tile_in,
    cell_in,
    depth_out,
    send_out,
    address_out,
    arrivals,
    depth_end,
    enters,
    series,
    turned,
    tiles,
    hots,
    counted,
    high_labels,
    low_labels,
    rhs,
    *parts,
):
    owners, slots = parts[: len(PARTS)], parts[len(PARTS) :]
    blocks = depth_in.shape[0]
    groups = LANES // MPB
    rows = blocks // groups
    inland = RB - MPB
    lane = lax.broadcasted_iota(i32, (blocks, RB), 1)

    for copy in copies:
        copy.wait()

    turned[...] = jnp.zeros_like(turned)
    turned[0:MPB, 0:blocks] = tile_in[...].astype(f32)
    turned[MPB : 2 * MPB, 0:blocks] = cell_in[...].astype(f32)
    turned[inland:RB, 0:blocks] = prev_in[...]
    mouths = jnp.transpose(turned[...])[0:blocks]
    prev = mouths

    def grouped(array, first):
        lanes16 = lax.broadcasted_iota(i32, (rows, LANES), 1)
        result = jnp.zeros((rows, LANES), f32)
        for g in range(groups):
            part = array[g * rows : (g + 1) * rows]
            shift = (g * MPB - first) % LANES
            part = part if shift == 0 else pltpu.roll(part, shift, 1)
            result = jnp.where(lanes16 // MPB == g, part, result)
        return result

    tile = grouped(mouths, 0).astype(i32)
    tiles[...] = tile % coasts * (devices // coasts) + tile // coasts
    series[STEPS * rows :] = grouped(mouths, MPB)

    into = into_in[...]
    at_mouth = lane >= inland
    down = jnp.where(at_mouth, 0, into)
    offset = jnp.where(at_mouth, 0, into - lane)
    bed = bed_in[...]
    bed_top = jnp.where(
        at_mouth, bed, jnp.maximum(bed, jnp.take_along_axis(bed, down, axis=1, mode="promise_in_bounds"))
    )
    drive = gravity * step_seconds / length_in[...]
    width = width_in[...]
    area = step_seconds / (width * length_in[...])
    gain = area * runoff_in[...]
    loss = area * width
    moved = [(turn(offset, 1 + b), turn(width, 1 + b)) for b in range(4)]
    for o in range(reach_offsets):
        where_to, its_width = moved[o % 4]
        weight = its_width * turn(area, -(o - o % 4))
        enters[o] = jnp.where(where_to == o + 1, weight, 0.0)

    def river_turn(substep, depth, flow):
        surface = bed + depth
        below = jnp.where(at_mouth, prev, jnp.take_along_axis(surface, down, axis=1, mode="promise_in_bounds"))
        flow = flow_after(flow, surface, below, bed_top, drive, river_manning)
        moved = [turn(flow, 1 + b) for b in range(4)]
        sums = []
        for a in range(0, reach_offsets, 4):
            one, other = [
                enters[a + b] * moved[b] + enters[a + b + 1] * moved[b + 1] for b in (0, 2)
            ]
            sums.append(turn(one + other, a))
        inflow = (sums[0] + sums[1]) + (sums[2] + sums[3])
        depth = (depth + gain - loss * flow) + inflow
        series[substep * rows : (substep + 1) * rows] = grouped(flow * width, inland)
        return depth, flow

    def count_mouths():
        for i in range(rows):
            names = jnp.broadcast_to(tiles[i : i + 1], (devices, LANES))
            hit = names == lax.broadcasted_iota(i32, (devices, LANES), 0)
            hots[i * devices : (i + 1) * devices] = jnp.where(hit, 1.0, 0.0).astype(bf16)
        shape = (LANES, 2 * LANES)
        earlier = lax.broadcasted_iota(i32, shape, 0) < lax.broadcasted_iota(i32, shape, 1)
        counted[...] = jnp.dot(
            hots[...], jnp.where(earlier, 1.0, 0.0).astype(bf16), preferred_element_type=f32
        )

    def rank_mouths():
        before = jnp.zeros((devices, LANES), f32)
        for i in range(rows):
            part = slice(i * devices, (i + 1) * devices)
            ranks = (counted[part, :LANES] + before) * hots[part].astype(f32)
            rank = jnp.sum(ranks, axis=0, keepdims=True).astype(i32)
            address_out[i : i + 1] = tiles[i : i + 1] * capacity + rank
            before = before + counted[part, LANES:]

    one, none = jnp.ones((LANES, LANES), bf16), jnp.zeros((LANES, LANES), bf16)
    number = lax.broadcasted_iota(i32, (TALL, LANES), 0).astype(f32)

    def label_mouths():
        high, low = split_label(address_out[...], WIDE)
        high_labels[...] = high.astype(f32)
        low_labels[...] = jnp.transpose(low.astype(f32))

    def slot_columns(group):
        place = lax.broadcasted_iota(i32, (LANES, LANES), 1).astype(f32).astype(bf16)
        for i in range(group * rows // 4, (group + 1) * rows // 4):
            lanes = slice(i * LANES, (i + 1) * LANES)
            column = jnp.broadcast_to(low_labels[:, i : i + 1], (LANES, LANES)).astype(bf16)
            for half in range(2):
                hit = column - half * LANES == place
                rhs[lanes, half * LANES : (half + 1) * LANES] = jnp.where(hit, one, none)

    def place_series(part, group):
        first, steps = PARTS[part]
        owner, lhs = owners[part], slots[part]
        for i in range(group * rows // 4, (group + 1) * rows // 4):
            lanes = slice(i * LANES, (i + 1) * LANES)
            labels = high_labels[i : i + 1]
            lay_out(series, first * rows + i, rows, steps, labels, owner, lhs, lanes)
            if part == 0:
                cells = series[STEPS * rows + i : STEPS * rows + i + 1]
                cells = jnp.where(number == labels, cells, 0.0)
                for half, value in enumerate(in_two(cells)):
                    at = 2 * TALL * steps + half * TALL
                    lhs[at : at + TALL, lanes] = value

    def pack(part):
        first, steps = PARTS[part]
        high_rows = TALL * steps
        lhs = slots[part]
        both = jnp.dot(lhs[...], rhs[...], preferred_element_type=f32)
        packed = both[:high_rows] + both[high_rows : 2 * high_rows]
        for half in range(2):
            lanes = slice(half * LANES, (half + 1) * LANES)
            for row in range(TALL):
                at = (2 * row + half) * SENT + first
                send_out[at : at + steps] = packed[row * steps : (row + 1) * steps, lanes]
            if part == 0:
                cells = both[2 * high_rows : 2 * high_rows + TALL] + both[2 * high_rows + TALL :]
                send_out[pl.ds(half * SENT + STEPS, TALL, stride=2 * SENT)] = cells[:, lanes]

    beside = {0: [count_mouths], 1: [rank_mouths], 2: [label_mouths]}
    beside |= {3 + group: [functools.partial(slot_columns, group)] for group in range(4)}
    beside |= {8: [functools.partial(place_series, 0, group) for group in range(2)]}
    beside |= {9: [functools.partial(place_series, 0, group) for group in range(2, 4)]}
    beside |= {10: [functools.partial(pack, 0)]}
    beside[10] += [functools.partial(place_series, 1, group) for group in range(4)]
    beside |= {11: [functools.partial(pack, 1)]}
    for owner, (_, steps) in zip(owners, PARTS):
        row_owners(owner, steps)
    depth, flow = depth_in[...], flow_in[...]
    for substep in range(STEPS):
        depth, flow = river_turn(substep, depth, flow)
        for work in beside.get(substep, []):
            work()
    depth_end[...] = depth
    finished = pltpu.make_async_copy(depth_end, depth_out, arrivals.at[len(copies)])
    finished.start()
    for group in range(4):
        place_series(2, group)
    pack(2)
    finished.wait()


def reach_of(field):
    return STEPS - 1 - field if field < STEPS else HALO


def turn(value, lanes):
    lanes %= value.shape[1]
    return value if lanes == 0 else pltpu.roll(value, lanes, 1)


ROW_AT = [sum(reach_of(f) for f in range(field)) for field in range(FIELDS + 1)]
ROWS_SENT = -(-ROW_AT[FIELDS] // 8) * 8


def source_kernel(arrived, *refs):
    inputs, (fields, odd, even, rhs, label_out), refs = refs[:5], refs[5:10], refs[10:]
    first_of_pair = lax.axis_index("river") % 2 == 0
    sea_level, sea_bed, wet_mask, flux_east, flux_north, arrivals, owner, places, labels, lhs, sums = refs
    copies = [
        pltpu.make_async_copy(whole, own, arrivals.at[number])
        for number, (whole, own) in enumerate(zip(inputs, refs[:5]))
    ]
    for copy in copies:
        copy.start()
    groups = arrived.shape[0] // SENT
    tile_rows, tile_cols = sea_level.shape

    high_rows = TALL * STEPS
    row_owners(owner, STEPS)
    row_owners(places, 1)

    def place_of(label, part):
        return label == places[part : part + TALL]

    cells = arrived[pl.ds(STEPS, groups, stride=SENT)].astype(i32)
    for number, label in enumerate(cell_labels(cells, tile_cols)):
        labels[number * groups : (number + 1) * groups] = label.astype(f32)
    label_out[...] = labels[:groups]

    def place(chunk):
        for s in range(chunk, chunk + CHUNK):
            lanes = slice(s * LANES, (s + 1) * LANES)
            lay_out(arrived, s * SENT, 1, STEPS, labels[s : s + 1], owner, lhs, lanes)
            one_hot_columns(labels[groups + s : groups + s + 1], place_of, rhs, lanes)

    both = jnp.zeros((2 * high_rows, WIDE), f32)
    place(0)
    for chunk in range(0, groups, CHUNK):
        if chunk + CHUNK < groups:
            place(chunk + CHUNK)
        lanes = slice(chunk * LANES, (chunk + CHUNK) * LANES)
        both = both + lax.dot_general(
            lhs[:, lanes], rhs[:, lanes], (((1,), (1,)), ((), ())), preferred_element_type=f32
        )
    total = both[:high_rows] + both[high_rows:]
    for half in range(2):
        part = slice(half * high_rows, (half + 1) * high_rows)
        sums[part] = total[:, half * LANES : (half + 1) * LANES]
    for copy in copies:
        copy.wait()
    bed = sea_bed[...]
    level = jnp.where(wet_mask[...] == 1, jnp.maximum(sea_level[...], bed), bed)

    def put(field, value):
        fields[field * tile_rows : (field + 1) * tile_rows] = value
        reach = reach_of(field)
        if reach:
            last, first = value[tile_rows - reach :], value[:reach]
            part = slice(ROW_AT[field], ROW_AT[field] + reach)
            odd[part] = jnp.where(first_of_pair, first, last)
            even[part] = jnp.where(first_of_pair, last, first)

    for swap_out in (odd, even):
        swap_out[ROWS_SENT - 8 :] = jnp.zeros((8, LANES), f32)
    for step in range(STEPS):
        halves = [sums[pl.ds(half * high_rows + step, TALL, stride=STEPS)] for half in range(2)]
        put(step, jnp.concatenate(halves, axis=0))
    for number, value in enumerate((level, bed, flux_east[...], flux_north[...])):
        put(STEPS + number, value)


def strip_kernel(fields, from_odd, from_even, tall, odd, even):
    upper = lax.axis_index("river") % 2 == 0
    first_of_pair = lax.axis_index("coast") % 2 == 0
    from_before = jnp.where(upper, from_odd[...], from_even[...])
    from_after = jnp.where(upper, from_even[...], from_odd[...])
    tile_rows = fields.shape[0] // FIELDS
    height = tall.shape[0] // FIELDS
    lane = lax.broadcasted_iota(i32, (height, LANES), 1)
    ends = jnp.zeros((height, LANES), f32)
    starts = jnp.zeros((height, LANES), f32)
    for field in range(FIELDS):
        reach, at = reach_of(field), ROW_AT[field]
        parts = [fields[field * tile_rows : (field + 1) * tile_rows]]
        if reach:
            parts.append(from_after[at : at + reach])
        if reach < HALO:
            parts.append(jnp.zeros((2 * HALO - 2 * reach, LANES), f32))
        if reach:
            parts.append(from_before[at : at + reach])
        value = jnp.concatenate(parts, axis=0)
        tall[field * height : (field + 1) * height] = value
        if reach:
            here = (lane >= at) & (lane < at + reach)
            ends = jnp.where(here, turn(value, at + reach - LANES), ends)
            starts = jnp.where(here, turn(value, at), starts)
    odd[...] = jnp.where(first_of_pair, starts, ends)
    even[...] = jnp.where(first_of_pair, ends, starts)


def ocean_kernel(
    tile_rows, tall, from_odd, from_even, row_labels, hot, level_out, replies, history
):
    height = tall.shape[0] // FIELDS
    width = 2 * LANES
    river, coast = lax.axis_index("river"), lax.axis_index("coast")
    rivers, coasts = lax.axis_size("river"), lax.axis_size("coast")
    lane = lax.broadcasted_iota(i32, (height, LANES), 1)
    from_left = jnp.where(coast % 2 == 0, from_odd[...], from_even[...])
    from_right = jnp.where(coast % 2 == 0, from_even[...], from_odd[...])

    def whole(field):
        reach, at = reach_of(field), ROW_AT[field]
        beside = jnp.zeros((height, LANES), f32)
        if reach:
            beside = jnp.where(lane < reach, turn(from_right, -at), beside)
            beside = jnp.where(lane >= LANES - reach, turn(from_left, -at - reach), beside)
        return jnp.concatenate([tall[field * height : (field + 1) * height], beside], axis=1)

    level, bed, east, north = [whole(STEPS + number) for number in range(4)]

    row = lax.broadcasted_iota(i32, (height, width), 0)
    column = lax.broadcasted_iota(i32, (height, width), 1)
    row_in = jnp.where(
        row < tile_rows, 1, jnp.where(row < tile_rows + HALO, (river < rivers - 1).astype(i32), (river > 0).astype(i32))
    )
    column_in = jnp.where(
        column < LANES, 1, jnp.where(column < LANES + LANES // 2, (coast < coasts - 1).astype(i32), (coast > 0).astype(i32))
    )
    inside = row_in * column_in == 1

    def next_row(value):
        return pltpu.roll(value, height - 1, 0)

    def next_column(value):
        return pltpu.roll(value, width - 1, 1)

    bed_east = jnp.maximum(bed, next_row(bed))
    bed_north = jnp.maximum(bed, next_column(bed))
    drive = gravity * step_seconds / cell_metres

    def ocean_turn(first, steps, step, level, east, north):
        source = whole(step) * (step_seconds / (cell_metres * cell_metres))
        east = flow_after(east, level, next_row(level), bed_east, drive, ocean_manning)
        north = flow_after(north, level, next_column(level), bed_north, drive, ocean_manning)
        spread = east - pltpu.roll(east, 1, 0) + north - pltpu.roll(north, 1, 1)
        level = level - step_seconds / cell_metres * spread + source
        level = jnp.where(inside, level, 0.0)
        for half in range(2):
            part = level[half * TALL : (half + 1) * TALL, :LANES]
            at = TALL * (2 * first + half * steps) + step - first
            history[pl.ds(at, TALL, stride=steps)] = part
        return level, east, north

    def table_of(first, steps):
        high_rows, at = TALL * steps, 2 * TALL * first
        halves = [history[at + half * high_rows : at + (half + 1) * high_rows] for half in range(2)]
        return jnp.concatenate(in_two(jnp.concatenate(halves, axis=1)), axis=0)

    def reply(table, first, steps, group, of):
        count = replies.shape[0] // STEPS // of
        for s in range(group * count, (group + 1) * count, 2):
            rows = jnp.concatenate([row_labels[s : s + 1], row_labels[s + 1 : s + 2]], axis=1)
            found = look_up(table, rows, hot[:, s * LANES : (s + 2) * LANES], steps)
            for half in range(2):
                at = (s + half) * STEPS + first
                replies[at : at + steps] = found[:, half * LANES : (half + 1) * LANES]

    waiting = []
    for part, (first, steps) in enumerate(LOOKED_UP):
        for step in range(first, first + steps):
            level, east, north = ocean_turn(first, steps, step, level, east, north)
            if waiting:
                reply(*waiting, step - first, steps)
        if part == len(LOOKED_UP) - 1:
            level_out[...] = level[:tile_rows, :LANES]
        waiting = [table_of(first, steps), first, steps]
    reply(*waiting, 0, 1)


def mouth_kernel(returned, address, level_out, whole, series, hot, block, departures):
    rows = address.shape[0]
    groups = LANES // MPB
    place = lax.broadcasted_iota(i32, (TALL, 2 * LANES), 0).astype(f32).astype(bf16)

    def place_of(label, part):
        return label - part == place

    labels = []
    for i in range(0, rows, 2):
        pair = jnp.concatenate([address[i : i + 1], address[i + 1 : i + 2]], axis=1)
        high, low = [label.astype(f32) for label in split_label(pair, WIDE)]
        one_hot_columns(low, place_of, hot, slice(i * LANES, (i + 2) * LANES))
        labels.append(high)
    lane = lax.broadcasted_iota(i32, (rows, LANES), 1)
    copies = []
    for first in range(0, STEPS, groups):
        for row in range(TALL):
            for half in range(2):
                at = (2 * row + half) * STEPS + first
                to = first * TALL + row * groups
                lanes = slice(half * LANES, (half + 1) * LANES)
                whole[to : to + groups, lanes] = returned[at : at + groups]
        own = whole[first * TALL : (first + groups) * TALL]
        table = jnp.concatenate(in_two(own), axis=0)
        for i in range(0, rows, 2):
            lanes = slice(i * LANES, (i + 2) * LANES)
            found = look_up(table, labels[i // 2], hot[:, lanes], groups)
            series[pl.ds(first * rows + i, groups, stride=rows)] = found[:, :LANES]
            series[pl.ds(first * rows + i + 1, groups, stride=rows)] = found[:, LANES:]
        number = first // groups
        for g in range(groups):
            result = jnp.zeros((rows, LANES), f32)
            for place in range(groups):
                at = (first + place) * rows
                part = turn(series[at : at + rows], (place - g) * MPB)
                result = jnp.where(lane // MPB == place, part, result)
            block[number, g * rows : (g + 1) * rows] = result
        to = level_out.at[:, pl.ds(number * LANES, LANES)]
        copies.append(pltpu.make_async_copy(block.at[number], to, departures.at[number]))
        copies[-1].start()
    for copy in copies:
        copy.wait()


def shape(*dims, dtype=f32):
    return jax.ShapeDtypeStruct(dims, dtype)


def in_hbm(*arrays):
    return [pltpu.with_memory_space_constraint(whole, pltpu.HBM) for whole in arrays]


def swap(values, tall, devices, capacity):
    per = LANES // capacity
    if per > 1:
        values = values.reshape(devices // per, tall, per, capacity).transpose(0, 2, 1, 3)
    values = values.reshape(devices, 1, tall * capacity)
    values = lax.all_to_all(values, ("coast", "river"), split_axis=0, concat_axis=0, tiled=True)
    if per > 1:
        values = values.reshape(devices // per, per, tall, capacity).transpose(0, 2, 1, 3)
    return values.reshape(devices // per * tall, LANES)


def with_neighbours(odd, even, axis):
    size = lax.axis_size(axis)
    routes = [
        [(i + k, i + 1 - k) for i in range(start, size - 1, 2) for k in range(2)]
        for start in (1, 0)
    ]
    return lax.ppermute(odd, axis, routes[0]), lax.ppermute(even, axis, routes[1])


def per_device(
    reach_depth,
    reach_flow,
    reach_bed,
    reach_width,
    reach_length,
    runoff,
    flows_into,
    mouth_prev,
    mouth_tile,
    mouth_cell,
    sea_level,
    sea_bed,
    wet_mask,
    flux_east,
    flux_north,
):
    devices = lax.axis_size("river") * lax.axis_size("coast")
    blocks = reach_depth.shape[0]
    tile_rows, tile_cols = sea_level.shape
    mouths = blocks * MPB
    capacity = max(2, 2 * mouths // devices)
    groups = devices * capacity // LANES
    rows = mouths // LANES
    height = tile_rows + 2 * HALO

    depth_after, sending, address = pl.pallas_call(
        functools.partial(river_kernel, devices, lax.axis_size("coast"), capacity),
        name="river",
        out_shape=(
            shape(blocks, RB),
            shape(groups * SENT, LANES),
            shape(rows, LANES, dtype=i32),
        ),
        in_specs=[pl.BlockSpec(memory_space=pltpu.HBM)] * 10,
        out_specs=(
            pl.BlockSpec(memory_space=pltpu.HBM),
            pl.BlockSpec(memory_space=pltpu.VMEM),
            pl.BlockSpec(memory_space=pltpu.VMEM),
        ),
        scratch_shapes=[pltpu.VMEM((blocks, RB), f32)] * 6
        + [
            pltpu.VMEM((blocks, RB), i32),
            pltpu.VMEM((MPB, blocks), f32),
            pltpu.VMEM((MPB, blocks), i32),
            pltpu.VMEM((MPB, blocks), i32),
            pltpu.SemaphoreType.DMA((11,)),
            pltpu.VMEM((blocks, RB), f32),
            pltpu.VMEM((reach_offsets, blocks, RB), f32),
            pltpu.VMEM((SENT * rows, LANES), f32),
            pltpu.VMEM((RB, LANES), f32),
            pltpu.VMEM((rows, LANES), i32),
            pltpu.VMEM((rows * devices, LANES), bf16),
            pltpu.VMEM((rows * devices, 2 * LANES), f32),
            pltpu.VMEM((rows, LANES), f32),
            pltpu.VMEM((LANES, rows), f32),
            pltpu.VMEM((mouths, WIDE), bf16),
            *[pltpu.VMEM((TALL * steps, LANES), bf16) for _, steps in PARTS],
            *[
                pltpu.VMEM((2 * TALL * (steps + (first == 0)), mouths), bf16)
                for first, steps in PARTS
            ],
        ],
        compiler_params=PARAMS,
    )(
        *in_hbm(
            reach_depth,
            reach_flow,
            reach_bed,
            reach_width,
            reach_length,
            runoff,
            flows_into,
            mouth_prev.T,
            mouth_tile[:, :, 0].T,
            mouth_cell.T,
        )
    )
    arrived = swap(sending, SENT, devices, capacity)

    fields, odd, even, hot, labels = pl.pallas_call(
        source_kernel,
        name="sources",
        out_shape=(
            shape(FIELDS * tile_rows, LANES),
            shape(ROWS_SENT, LANES),
            shape(ROWS_SENT, LANES),
            shape(WIDE, groups * LANES, dtype=bf16),
            shape(groups, LANES),
        ),
        in_specs=[pl.BlockSpec(memory_space=pltpu.VMEM)]
        + [pl.BlockSpec(memory_space=pltpu.HBM)] * 5,
        scratch_shapes=[
            pltpu.VMEM((tile_rows, tile_cols), f32),
            pltpu.VMEM((tile_rows, tile_cols), f32),
            pltpu.VMEM((tile_rows, tile_cols), i32),
            pltpu.VMEM((tile_rows, tile_cols), f32),
            pltpu.VMEM((tile_rows, tile_cols), f32),
            pltpu.SemaphoreType.DMA((5,)),
            pltpu.VMEM((TALL * STEPS, LANES), bf16),
            pltpu.VMEM((WIDE, LANES), bf16),
            pltpu.VMEM((2 * groups, LANES), f32),
            pltpu.VMEM((2 * TALL * STEPS, groups * LANES), bf16),
            pltpu.VMEM((2 * TALL * STEPS, LANES), f32),
        ],
        compiler_params=PARAMS,
    )(arrived, *in_hbm(sea_level, sea_bed, wet_mask, flux_east, flux_north))
    from_odd, from_even = with_neighbours(odd, even, "river")

    tall, odd, even = pl.pallas_call(
        strip_kernel,
        name="strips",
        out_shape=(shape(FIELDS * height, LANES), shape(height, LANES), shape(height, LANES)),
        compiler_params=PARAMS,
    )(fields, from_odd, from_even)
    from_odd, from_even = with_neighbours(odd, even, "coast")

    level_after, replies = pl.pallas_call(
        functools.partial(ocean_kernel, tile_rows),
        name="ocean",
        out_shape=(shape(tile_rows, tile_cols), shape(groups * STEPS, LANES)),
        scratch_shapes=[
            pltpu.VMEM((2 * TALL * STEPS, LANES), f32),
        ],
        compiler_params=PARAMS,
    )(tall, from_odd, from_even, labels, hot)
    returned = swap(replies, STEPS, devices, capacity)

    mouth_level = pl.pallas_call(
        mouth_kernel,
        name="mouths",
        out_shape=shape(blocks, STEPS * MPB),
        scratch_shapes=[
            pltpu.VMEM((TALL * STEPS, WIDE), f32),
            pltpu.VMEM((STEPS * rows, LANES), f32),
            pltpu.VMEM((WIDE, mouths), bf16),
            pltpu.VMEM((STEPS * MPB // LANES, blocks, LANES), f32),
            pltpu.SemaphoreType.DMA((STEPS * MPB // LANES,)),
        ],
        out_specs=pl.BlockSpec(memory_space=pltpu.HBM),
        compiler_params=PARAMS,
    )(returned, address)
    return (depth_after, level_after, mouth_level)


def solution(mesh):
    by_block = P(("river", "coast"), None)
    tiled = P("river", "coast")
    return jax.shard_map(
        per_device,
        mesh=mesh,
        in_specs=(by_block,) * 8
        + (P(("river", "coast"), None, None), by_block)
        + (tiled,) * 5,
        out_specs=(by_block, tiled, by_block),
        check_vma=False,
    )
```

```python
import functools
import math

import jax
import jax.numpy as jnp
from jax import lax
from jax.experimental import pallas as pl
from jax.experimental.pallas import tpu as pltpu
from jax.sharding import PartitionSpec as P

RB = 128
MPB = 32
STEPS = 12

gravity = 9.81
step_seconds = 300.0
cell_metres = 3000.0
river_manning = 0.035
ocean_manning = 0.025
depth_floor = 0.05
reach_offsets = 16

LANES = 128
SENT = 13
TALL = 16
WIDE = 256
PARTS = ((0, 8), (8, 2), (10, 2))
LOOKED_UP = ((0, 8), (8, 4))
CHUNK = 8
HALO = 12
FIELDS = 16
f32, bf16, i32 = jnp.float32, jnp.bfloat16, jnp.int32

PARAMS = pltpu.CompilerParams(vmem_limit_bytes=40 * 1024 * 1024)


def flow_after(unit_flow, upper, lower, bed_top, drive, manning):
    face_depth = jnp.maximum(upper, lower) - bed_top
    driving = drive * jnp.maximum(face_depth, 0.0) * (upper - lower)
    power = -7.0 / 3.0 * math.log2(math.e)
    thin = jnp.exp2(jnp.log(jnp.maximum(face_depth, depth_floor)) * power)
    friction = (gravity * step_seconds * manning * manning) * jnp.abs(unit_flow) * thin
    divisor = 1.0 + friction
    inverse = pl.reciprocal(divisor, approx=True)
    return ((unit_flow + driving) * inverse) * (2.0 - divisor * inverse)


def in_two(values):
    high = values.astype(bf16)
    return high, (values - high.astype(f32)).astype(bf16)


def small(labels):
    return jnp.broadcast_to(labels, (TALL, labels.shape[1])).astype(bf16)


def one_hot_columns(columns, place_of, rhs, lanes):
    labels = small(columns)
    one, none = jnp.ones(labels.shape, bf16), jnp.zeros(labels.shape, bf16)
    for part in range(0, WIDE, TALL):
        hit = place_of(labels, part)
        rhs[part : part + TALL, lanes] = jnp.where(hit, one, none)


def row_owners(owner, steps):
    for part in range(0, owner.shape[0], TALL):
        number = part + lax.broadcasted_iota(i32, (TALL, LANES), 0)
        owner[part : part + TALL] = (number // steps).astype(f32).astype(bf16)


def in_turn(series, at, stride, steps, first):
    parts, row = [], first
    while row < first + 8:
        step = row % steps
        count = min(steps - step, first + 8 - row)
        parts.append(series[pl.ds(at + step * stride, count, stride=stride)])
        row += count
    return parts[0] if len(parts) == 1 else jnp.concatenate(parts, axis=0)


def lay_out(series, at, stride, steps, rows, owner, lhs, lanes):
    turns = math.lcm(steps, 8) // 8
    cycle = [in_turn(series, at, stride, steps, 8 * turn) for turn in range(turns)]
    pairs = [(cycle[2 * k % turns], cycle[(2 * k + 1) % turns]) for k in range(turns)]
    halves = [in_two(jnp.concatenate(pair, axis=0)) for pair in pairs]
    labels = small(rows)
    none = jnp.zeros(labels.shape, bf16)
    for part in range(steps):
        at_rows = slice(part * TALL, (part + 1) * TALL)
        hit = labels == owner[at_rows]
        for number, half in enumerate(halves[part % turns]):
            at_rows = slice((number * steps + part) * TALL, (number * steps + part + 1) * TALL)
            lhs[at_rows, lanes] = jnp.where(hit, half, none)


def look_up(table, rows, hot, steps):
    found = jnp.dot(table, hot, preferred_element_type=f32)
    per = 2 if steps > 6 else 4
    several = (per * steps, rows.shape[1])
    number = (lax.broadcasted_iota(i32, several, 0) // steps).astype(f32)
    labels = jnp.broadcast_to(rows, several) - number
    total = jnp.zeros(several, f32)
    for row in range(0, TALL, per):
        high = found[row * steps : (row + per) * steps]
        low = found[(TALL + row) * steps : (TALL + row + per) * steps]
        total = total + jnp.where(labels == row, high + low, 0.0)
    result = total[:steps]
    for number in range(1, per):
        result = result + total[number * steps : (number + 1) * steps]
    return result


def split_label(number, size):
    return lax.shift_right_logical(number, size.bit_length() - 1), number & (size - 1)


def cell_labels(cells, tile_cols):
    row, column = split_label(cells, tile_cols)
    upper, row = split_label(row, TALL)
    return row, upper * tile_cols + column


def river_kernel(
    devices,
    coasts,
    capacity,
    *refs,
):
    inputs, (depth_out, send_out, address_out), refs = refs[:10], refs[10:13], refs[13:]
    copies = [
        pltpu.make_async_copy(whole, own, refs[10].at[number])
        for number, (whole, own) in enumerate(zip(inputs, refs[:10]))
    ]
    for copy in copies[::-1]:
        copy.start()
    river_steps(devices, coasts, capacity, copies, *refs[:10], depth_out, send_out, address_out, *refs[10:])


def river_steps(
    devices,
    coasts,
    capacity,
    copies,
    depth_in,
    flow_in,
    bed_in,
    width_in,
    length_in,
    runoff_in,
    into_in,
    prev_in,
    tile_in,
    cell_in,
    depth_out,
    send_out,
    address_out,
    arrivals,
    depth_end,
    enters,
    series,
    turned,
    tiles,
    hots,
    counted,
    high_labels,
    low_labels,
    rhs,
    *parts,
):
    owners, slots = parts[: len(PARTS)], parts[len(PARTS) :]
    blocks = depth_in.shape[0]
    groups = LANES // MPB
    rows = blocks // groups
    inland = RB - MPB
    lane = lax.broadcasted_iota(i32, (blocks, RB), 1)

    for copy in copies:
        copy.wait()

    turned[...] = jnp.zeros_like(turned)
    turned[0:MPB, 0:blocks] = tile_in[...].astype(f32)
    turned[MPB : 2 * MPB, 0:blocks] = cell_in[...].astype(f32)
    turned[inland:RB, 0:blocks] = prev_in[...]
    mouths = jnp.transpose(turned[...])[0:blocks]
    prev = mouths

    def grouped(array, first):
        lanes16 = lax.broadcasted_iota(i32, (rows, LANES), 1)
        result = jnp.zeros((rows, LANES), f32)
        for g in range(groups):
            part = array[g * rows : (g + 1) * rows]
            shift = (g * MPB - first) % LANES
            part = part if shift == 0 else pltpu.roll(part, shift, 1)
            result = jnp.where(lanes16 // MPB == g, part, result)
        return result

    tile = grouped(mouths, 0).astype(i32)
    tiles[...] = tile % coasts * (devices // coasts) + tile // coasts
    series[STEPS * rows :] = grouped(mouths, MPB)

    into = into_in[...]
    at_mouth = lane >= inland
    down = jnp.where(at_mouth, 0, into)
    offset = jnp.where(at_mouth, 0, into - lane)
    bed = bed_in[...]

    sources = [(down - 4 * a) & (RB - 1) for a in range(reach_offsets // 4)]

    def below_of(value, a=0):
        return jnp.take_along_axis(value, sources[a], axis=1, mode="promise_in_bounds")

    bed_below = below_of(bed)
    bed_top = jnp.where(at_mouth, bed, jnp.maximum(bed, bed_below))
    drive = gravity * step_seconds / length_in[...]
    width = width_in[...]
    area = step_seconds / (width * length_in[...])
    gain = area * runoff_in[...]
    loss = area * width
    moved = [(turn(offset, 1 + b), turn(width, 1 + b)) for b in range(4)]
    for o in range(reach_offsets):
        where_to, its_width = moved[o % 4]
        weight = its_width * turn(area, -(o - o % 4))
        enters[o] = jnp.where(where_to == o + 1, weight, 0.0)

    def river_turn(substep, depth, flow, below):
        below = jnp.where(at_mouth, prev, below)
        flow = flow_after(flow, bed + depth, below, bed_top, drive, river_manning)
        moved = [turn(flow, 1 + b) for b in range(4)]
        sums = []
        for a in range(0, reach_offsets, 4):
            one, other = [
                enters[a + b] * moved[b] + enters[a + b + 1] * moved[b + 1] for b in (0, 2)
            ]
            sums.append(one + other)
        sums[0] = sums[0] + (depth + gain - loss * flow)
        depth, below = [
            (places[0] + places[1]) + (places[2] + places[3])
            for places in (
                [turn(value, 4 * a) for a, value in enumerate(sums)],
                [below_of(value, a) for a, value in enumerate(sums)],
            )
        ]
        series[substep * rows : (substep + 1) * rows] = grouped(flow * width, inland)
        return depth, flow, bed_below + below

    def count_mouths():
        for i in range(rows):
            names = jnp.broadcast_to(tiles[i : i + 1], (devices, LANES))
            hit = names == lax.broadcasted_iota(i32, (devices, LANES), 0)
            hots[i * devices : (i + 1) * devices] = jnp.where(hit, 1.0, 0.0).astype(bf16)
        shape = (LANES, 2 * LANES)
        earlier = lax.broadcasted_iota(i32, shape, 0) < lax.broadcasted_iota(i32, shape, 1)
        counted[...] = jnp.dot(
            hots[...], jnp.where(earlier, 1.0, 0.0).astype(bf16), preferred_element_type=f32
        )

    def rank_mouths():
        before = jnp.zeros((devices, LANES), f32)
        for i in range(rows):
            part = slice(i * devices, (i + 1) * devices)
            ranks = (counted[part, :LANES] + before) * hots[part].astype(f32)
            rank = jnp.sum(ranks, axis=0, keepdims=True).astype(i32)
            address_out[i : i + 1] = tiles[i : i + 1] * capacity + rank
            before = before + counted[part, LANES:]

    one, none = jnp.ones((LANES, LANES), bf16), jnp.zeros((LANES, LANES), bf16)
    number = lax.broadcasted_iota(i32, (TALL, LANES), 0).astype(f32)

    def label_mouths():
        high, low = split_label(address_out[...], WIDE)
        high_labels[...] = high.astype(f32)
        low_labels[...] = jnp.transpose(low.astype(f32))

    def slot_columns(group):
        place = lax.broadcasted_iota(i32, (LANES, LANES), 1).astype(f32).astype(bf16)
        for i in range(group * rows // 4, (group + 1) * rows // 4):
            lanes = slice(i * LANES, (i + 1) * LANES)
            column = jnp.broadcast_to(low_labels[:, i : i + 1], (LANES, LANES)).astype(bf16)
            for half in range(2):
                hit = column - half * LANES == place
                rhs[lanes, half * LANES : (half + 1) * LANES] = jnp.where(hit, one, none)

    def place_series(part, group):
        first, steps = PARTS[part]
        owner, lhs = owners[part], slots[part]
        for i in range(group * rows // 4, (group + 1) * rows // 4):
            lanes = slice(i * LANES, (i + 1) * LANES)
            labels = high_labels[i : i + 1]
            lay_out(series, first * rows + i, rows, steps, labels, owner, lhs, lanes)
            if part == 0:
                cells = series[STEPS * rows + i : STEPS * rows + i + 1]
                cells = jnp.where(number == labels, cells, 0.0)
                for half, value in enumerate(in_two(cells)):
                    at = 2 * TALL * steps + half * TALL
                    lhs[at : at + TALL, lanes] = value

    def pack(part):
        first, steps = PARTS[part]
        high_rows = TALL * steps
        lhs = slots[part]
        both = jnp.dot(lhs[...], rhs[...], preferred_element_type=f32)
        packed = both[:high_rows] + both[high_rows : 2 * high_rows]
        for half in range(2):
            lanes = slice(half * LANES, (half + 1) * LANES)
            for row in range(TALL):
                at = (2 * row + half) * SENT + first
                send_out[at : at + steps] = packed[row * steps : (row + 1) * steps, lanes]
            if part == 0:
                cells = both[2 * high_rows : 2 * high_rows + TALL] + both[2 * high_rows + TALL :]
                send_out[pl.ds(half * SENT + STEPS, TALL, stride=2 * SENT)] = cells[:, lanes]

    beside = {0: [count_mouths], 1: [rank_mouths], 2: [label_mouths]}
    beside |= {3 + group: [functools.partial(slot_columns, group)] for group in range(4)}
    beside |= {8: [functools.partial(place_series, 0, group) for group in range(2)]}
    beside |= {9: [functools.partial(place_series, 0, group) for group in range(2, 4)]}
    beside |= {10: [functools.partial(pack, 0)]}
    beside[10] += [functools.partial(place_series, 1, group) for group in range(4)]
    beside |= {11: [functools.partial(pack, 1)]}
    for owner, (_, steps) in zip(owners, PARTS):
        row_owners(owner, steps)
    depth, flow = depth_in[...], flow_in[...]
    below = bed_below + below_of(depth)
    for substep in range(STEPS):
        depth, flow, below = river_turn(substep, depth, flow, below)
        for work in beside.get(substep, []):
            work()
    depth_end[...] = depth
    finished = pltpu.make_async_copy(depth_end, depth_out, arrivals.at[len(copies)])
    finished.start()
    for group in range(4):
        place_series(2, group)
    pack(2)
    finished.wait()


def reach_of(field):
    return STEPS - 1 - field if field < STEPS else HALO


def turn(value, lanes):
    lanes %= value.shape[1]
    return value if lanes == 0 else pltpu.roll(value, lanes, 1)


ROW_AT = [sum(reach_of(f) for f in range(field)) for field in range(FIELDS + 1)]
ROWS_SENT = -(-ROW_AT[FIELDS] // 8) * 8


def source_kernel(arrived, *refs):
    inputs, (fields, odd, even, rhs, label_out), refs = refs[:5], refs[5:10], refs[10:]
    first_of_pair = lax.axis_index("river") % 2 == 0
    sea_level, sea_bed, wet_mask, flux_east, flux_north, arrivals, owner, places, labels, lhs, sums = refs
    copies = [
        pltpu.make_async_copy(whole, own, arrivals.at[number])
        for number, (whole, own) in enumerate(zip(inputs, refs[:5]))
    ]
    for copy in copies:
        copy.start()
    groups = arrived.shape[0] // SENT
    tile_rows, tile_cols = sea_level.shape

    high_rows = TALL * STEPS
    row_owners(owner, STEPS)
    row_owners(places, 1)

    def place_of(label, part):
        return label == places[part : part + TALL]

    cells = arrived[pl.ds(STEPS, groups, stride=SENT)].astype(i32)
    for number, label in enumerate(cell_labels(cells, tile_cols)):
        labels[number * groups : (number + 1) * groups] = label.astype(f32)
    label_out[...] = labels[:groups]

    def place(chunk):
        for s in range(chunk, chunk + CHUNK):
            lanes = slice(s * LANES, (s + 1) * LANES)
            lay_out(arrived, s * SENT, 1, STEPS, labels[s : s + 1], owner, lhs, lanes)
            one_hot_columns(labels[groups + s : groups + s + 1], place_of, rhs, lanes)

    both = jnp.zeros((2 * high_rows, WIDE), f32)
    place(0)
    for chunk in range(0, groups, CHUNK):
        if chunk + CHUNK < groups:
            place(chunk + CHUNK)
        lanes = slice(chunk * LANES, (chunk + CHUNK) * LANES)
        both = both + lax.dot_general(
            lhs[:, lanes], rhs[:, lanes], (((1,), (1,)), ((), ())), preferred_element_type=f32
        )
    total = both[:high_rows] + both[high_rows:]
    for half in range(2):
        part = slice(half * high_rows, (half + 1) * high_rows)
        sums[part] = total[:, half * LANES : (half + 1) * LANES]
    for copy in copies:
        copy.wait()
    bed = sea_bed[...]
    level = jnp.where(wet_mask[...] == 1, jnp.maximum(sea_level[...], bed), bed)

    def put(field, value):
        fields[field * tile_rows : (field + 1) * tile_rows] = value
        reach = reach_of(field)
        if reach:
            last, first = value[tile_rows - reach :], value[:reach]
            part = slice(ROW_AT[field], ROW_AT[field] + reach)
            odd[part] = jnp.where(first_of_pair, first, last)
            even[part] = jnp.where(first_of_pair, last, first)

    for swap_out in (odd, even):
        swap_out[ROWS_SENT - 8 :] = jnp.zeros((8, LANES), f32)
    for step in range(STEPS):
        halves = [sums[pl.ds(half * high_rows + step, TALL, stride=STEPS)] for half in range(2)]
        put(step, jnp.concatenate(halves, axis=0))
    for number, value in enumerate((level, bed, flux_east[...], flux_north[...])):
        put(STEPS + number, value)


def strip_kernel(fields, from_odd, from_even, tall, odd, even):
    upper = lax.axis_index("river") % 2 == 0
    first_of_pair = lax.axis_index("coast") % 2 == 0
    from_before = jnp.where(upper, from_odd[...], from_even[...])
    from_after = jnp.where(upper, from_even[...], from_odd[...])
    tile_rows = fields.shape[0] // FIELDS
    height = tall.shape[0] // FIELDS
    lane = lax.broadcasted_iota(i32, (height, LANES), 1)
    ends = jnp.zeros((height, LANES), f32)
    starts = jnp.zeros((height, LANES), f32)
    for field in range(FIELDS):
        reach, at = reach_of(field), ROW_AT[field]
        parts = [fields[field * tile_rows : (field + 1) * tile_rows]]
        if reach:
            parts.append(from_after[at : at + reach])
        if reach < HALO:
            parts.append(jnp.zeros((2 * HALO - 2 * reach, LANES), f32))
        if reach:
            parts.append(from_before[at : at + reach])
        value = jnp.concatenate(parts, axis=0)
        tall[field * height : (field + 1) * height] = value
        if reach:
            here = (lane >= at) & (lane < at + reach)
            ends = jnp.where(here, turn(value, at + reach - LANES), ends)
            starts = jnp.where(here, turn(value, at), starts)
    odd[...] = jnp.where(first_of_pair, starts, ends)
    even[...] = jnp.where(first_of_pair, ends, starts)


def ocean_kernel(
    tile_rows, tall, from_odd, from_even, row_labels, hot, level_out, replies, history, level_end, departure
):
    height = tall.shape[0] // FIELDS
    width = 2 * LANES
    river, coast = lax.axis_index("river"), lax.axis_index("coast")
    rivers, coasts = lax.axis_size("river"), lax.axis_size("coast")
    lane = lax.broadcasted_iota(i32, (height, LANES), 1)
    from_left = jnp.where(coast % 2 == 0, from_odd[...], from_even[...])
    from_right = jnp.where(coast % 2 == 0, from_even[...], from_odd[...])

    def whole(field):
        reach, at = reach_of(field), ROW_AT[field]
        beside = jnp.zeros((height, LANES), f32)
        if reach:
            beside = jnp.where(lane < reach, turn(from_right, -at), beside)
            beside = jnp.where(lane >= LANES - reach, turn(from_left, -at - reach), beside)
        return jnp.concatenate([tall[field * height : (field + 1) * height], beside], axis=1)

    level, bed, east, north = [whole(STEPS + number) for number in range(4)]

    row = lax.broadcasted_iota(i32, (height, width), 0)
    column = lax.broadcasted_iota(i32, (height, width), 1)
    row_in = jnp.where(
        row < tile_rows, 1, jnp.where(row < tile_rows + HALO, (river < rivers - 1).astype(i32), (river > 0).astype(i32))
    )
    column_in = jnp.where(
        column < LANES, 1, jnp.where(column < LANES + LANES // 2, (coast < coasts - 1).astype(i32), (coast > 0).astype(i32))
    )
    inside = row_in * column_in == 1

    def next_row(value):
        return pltpu.roll(value, height - 1, 0)

    def next_column(value):
        return pltpu.roll(value, width - 1, 1)

    bed_east = jnp.maximum(bed, next_row(bed))
    bed_north = jnp.maximum(bed, next_column(bed))
    drive = gravity * step_seconds / cell_metres

    def ocean_turn(first, steps, step, level, east, north):
        source = whole(step) * (step_seconds / (cell_metres * cell_metres))
        east = flow_after(east, level, next_row(level), bed_east, drive, ocean_manning)
        north = flow_after(north, level, next_column(level), bed_north, drive, ocean_manning)
        spread = east - pltpu.roll(east, 1, 0) + north - pltpu.roll(north, 1, 1)
        level = level - step_seconds / cell_metres * spread + source
        level = jnp.where(inside, level, 0.0)
        for half in range(2):
            part = level[half * TALL : (half + 1) * TALL, :LANES]
            at = TALL * (2 * first + half * steps) + step - first
            history[pl.ds(at, TALL, stride=steps)] = part
        return level, east, north

    def table_of(first, steps):
        high_rows, at = TALL * steps, 2 * TALL * first
        halves = [history[at + half * high_rows : at + (half + 1) * high_rows] for half in range(2)]
        return jnp.concatenate(in_two(jnp.concatenate(halves, axis=1)), axis=0)

    def reply(table, first, steps, group, of):
        count = replies.shape[0] // STEPS // of
        for s in range(group * count, (group + 1) * count, 2):
            rows = jnp.concatenate([row_labels[s : s + 1], row_labels[s + 1 : s + 2]], axis=1)
            found = look_up(table, rows, hot[:, s * LANES : (s + 2) * LANES], steps)
            for half in range(2):
                at = (s + half) * STEPS + first
                replies[at : at + steps] = found[:, half * LANES : (half + 1) * LANES]

    waiting = []
    for part, (first, steps) in enumerate(LOOKED_UP):
        for step in range(first, first + steps):
            level, east, north = ocean_turn(first, steps, step, level, east, north)
            if waiting:
                reply(*waiting, step - first, steps)
        if part == len(LOOKED_UP) - 1:
            level_end[...] = level[:tile_rows, :LANES]
            finished = pltpu.make_async_copy(level_end, level_out, departure)
            finished.start()
        waiting = [table_of(first, steps), first, steps]
    reply(*waiting, 0, 1)
    finished.wait()


def mouth_kernel(returned, address, level_out, whole, series, hot, block, departures):
    rows = address.shape[0]
    groups = LANES // MPB
    place = lax.broadcasted_iota(i32, (TALL, 2 * LANES), 0).astype(f32).astype(bf16)

    def place_of(label, part):
        return label - part == place

    labels = []
    for i in range(0, rows, 2):
        pair = jnp.concatenate([address[i : i + 1], address[i + 1 : i + 2]], axis=1)
        high, low = [label.astype(f32) for label in split_label(pair, WIDE)]
        one_hot_columns(low, place_of, hot, slice(i * LANES, (i + 2) * LANES))
        labels.append(high)
    lane = lax.broadcasted_iota(i32, (rows, LANES), 1)
    copies = []
    for first, steps in LOOKED_UP:
        for row in range(TALL):
            for half in range(2):
                at = (2 * row + half) * STEPS + first
                to = first * TALL + row * steps
                lanes = slice(half * LANES, (half + 1) * LANES)
                whole[to : to + steps, lanes] = returned[at : at + steps]
        own = whole[first * TALL : (first + steps) * TALL]
        table = jnp.concatenate(in_two(own), axis=0)
        for i in range(0, rows, 2):
            lanes = slice(i * LANES, (i + 2) * LANES)
            found = look_up(table, labels[i // 2], hot[:, lanes], steps)
            series[pl.ds(first * rows + i, steps, stride=rows)] = found[:, :LANES]
            series[pl.ds(first * rows + i + 1, steps, stride=rows)] = found[:, LANES:]
        for number in range(first // groups, (first + steps) // groups):
            for g in range(groups):
                result = jnp.zeros((rows, LANES), f32)
                for place in range(groups):
                    at = (number * groups + place) * rows
                    part = turn(series[at : at + rows], (place - g) * MPB)
                    result = jnp.where(lane // MPB == place, part, result)
                block[number, g * rows : (g + 1) * rows] = result
            to = level_out.at[:, pl.ds(number * LANES, LANES)]
            copies.append(pltpu.make_async_copy(block.at[number], to, departures.at[number]))
            copies[-1].start()
    for copy in copies:
        copy.wait()


def shape(*dims, dtype=f32):
    return jax.ShapeDtypeStruct(dims, dtype)


def in_hbm(*arrays):
    return [pltpu.with_memory_space_constraint(whole, pltpu.HBM) for whole in arrays]


def swap(values, tall, devices, capacity):
    per = LANES // capacity
    if per > 1:
        values = values.reshape(devices // per, tall, per, capacity).transpose(0, 2, 1, 3)
    values = values.reshape(devices, 1, tall * capacity)
    values = lax.all_to_all(values, ("coast", "river"), split_axis=0, concat_axis=0, tiled=True)
    if per > 1:
        values = values.reshape(devices // per, per, tall, capacity).transpose(0, 2, 1, 3)
    return values.reshape(devices // per * tall, LANES)


def with_neighbours(odd, even, axis):
    size = lax.axis_size(axis)
    routes = [
        [(i + k, i + 1 - k) for i in range(start, size - 1, 2) for k in range(2)]
        for start in (1, 0)
    ]
    return lax.ppermute(odd, axis, routes[0]), lax.ppermute(even, axis, routes[1])


def per_device(
    reach_depth,
    reach_flow,
    reach_bed,
    reach_width,
    reach_length,
    runoff,
    flows_into,
    mouth_prev,
    mouth_tile,
    mouth_cell,
    sea_level,
    sea_bed,
    wet_mask,
    flux_east,
    flux_north,
):
    devices = lax.axis_size("river") * lax.axis_size("coast")
    blocks = reach_depth.shape[0]
    tile_rows, tile_cols = sea_level.shape
    mouths = blocks * MPB
    capacity = max(2, 2 * mouths // devices)
    groups = devices * capacity // LANES
    rows = mouths // LANES
    height = tile_rows + 2 * HALO

    depth_after, sending, address = pl.pallas_call(
        functools.partial(river_kernel, devices, lax.axis_size("coast"), capacity),
        name="river",
        out_shape=(
            shape(blocks, RB),
            shape(groups * SENT, LANES),
            shape(rows, LANES, dtype=i32),
        ),
        in_specs=[pl.BlockSpec(memory_space=pltpu.HBM)] * 10,
        out_specs=(
            pl.BlockSpec(memory_space=pltpu.HBM),
            pl.BlockSpec(memory_space=pltpu.VMEM),
            pl.BlockSpec(memory_space=pltpu.VMEM),
        ),
        scratch_shapes=[pltpu.VMEM((blocks, RB), f32)] * 6
        + [
            pltpu.VMEM((blocks, RB), i32),
            pltpu.VMEM((MPB, blocks), f32),
            pltpu.VMEM((MPB, blocks), i32),
            pltpu.VMEM((MPB, blocks), i32),
            pltpu.SemaphoreType.DMA((11,)),
            pltpu.VMEM((blocks, RB), f32),
            pltpu.VMEM((reach_offsets, blocks, RB), f32),
            pltpu.VMEM((SENT * rows, LANES), f32),
            pltpu.VMEM((RB, LANES), f32),
            pltpu.VMEM((rows, LANES), i32),
            pltpu.VMEM((rows * devices, LANES), bf16),
            pltpu.VMEM((rows * devices, 2 * LANES), f32),
            pltpu.VMEM((rows, LANES), f32),
            pltpu.VMEM((LANES, rows), f32),
            pltpu.VMEM((mouths, WIDE), bf16),
            *[pltpu.VMEM((TALL * steps, LANES), bf16) for _, steps in PARTS],
            *[
                pltpu.VMEM((2 * TALL * (steps + (first == 0)), mouths), bf16)
                for first, steps in PARTS
            ],
        ],
        compiler_params=PARAMS,
    )(
        *in_hbm(
            reach_depth,
            reach_flow,
            reach_bed,
            reach_width,
            reach_length,
            runoff,
            flows_into,
            mouth_prev.T,
            mouth_tile[:, :, 0].T,
            mouth_cell.T,
        )
    )
    arrived = swap(sending, SENT, devices, capacity)

    fields, odd, even, hot, labels = pl.pallas_call(
        source_kernel,
        name="sources",
        out_shape=(
            shape(FIELDS * tile_rows, LANES),
            shape(ROWS_SENT, LANES),
            shape(ROWS_SENT, LANES),
            shape(WIDE, groups * LANES, dtype=bf16),
            shape(groups, LANES),
        ),
        in_specs=[pl.BlockSpec(memory_space=pltpu.VMEM)]
        + [pl.BlockSpec(memory_space=pltpu.HBM)] * 5,
        scratch_shapes=[
            pltpu.VMEM((tile_rows, tile_cols), f32),
            pltpu.VMEM((tile_rows, tile_cols), f32),
            pltpu.VMEM((tile_rows, tile_cols), i32),
            pltpu.VMEM((tile_rows, tile_cols), f32),
            pltpu.VMEM((tile_rows, tile_cols), f32),
            pltpu.SemaphoreType.DMA((5,)),
            pltpu.VMEM((TALL * STEPS, LANES), bf16),
            pltpu.VMEM((WIDE, LANES), bf16),
            pltpu.VMEM((2 * groups, LANES), f32),
            pltpu.VMEM((2 * TALL * STEPS, groups * LANES), bf16),
            pltpu.VMEM((2 * TALL * STEPS, LANES), f32),
        ],
        compiler_params=PARAMS,
    )(arrived, *in_hbm(sea_level, sea_bed, wet_mask, flux_east, flux_north))
    from_odd, from_even = with_neighbours(odd, even, "river")

    tall, odd, even = pl.pallas_call(
        strip_kernel,
        name="strips",
        out_shape=(shape(FIELDS * height, LANES), shape(height, LANES), shape(height, LANES)),
        compiler_params=PARAMS,
    )(fields, from_odd, from_even)
    from_odd, from_even = with_neighbours(odd, even, "coast")

    level_after, replies = pl.pallas_call(
        functools.partial(ocean_kernel, tile_rows),
        name="ocean",
        out_shape=(shape(tile_rows, tile_cols), shape(groups * STEPS, LANES)),
        scratch_shapes=[
            pltpu.VMEM((2 * TALL * STEPS, LANES), f32),
            pltpu.VMEM((tile_rows, tile_cols), f32),
            pltpu.SemaphoreType.DMA,
        ],
        out_specs=(
            pl.BlockSpec(memory_space=pltpu.HBM),
            pl.BlockSpec(memory_space=pltpu.VMEM),
        ),
        compiler_params=PARAMS,
    )(tall, from_odd, from_even, labels, hot)
    returned = swap(replies, STEPS, devices, capacity)

    mouth_level = pl.pallas_call(
        mouth_kernel,
        name="mouths",
        out_shape=shape(blocks, STEPS * MPB),
        scratch_shapes=[
            pltpu.VMEM((TALL * STEPS, WIDE), f32),
            pltpu.VMEM((STEPS * rows, LANES), f32),
            pltpu.VMEM((WIDE, mouths), bf16),
            pltpu.VMEM((STEPS * MPB // LANES, blocks, LANES), f32),
            pltpu.SemaphoreType.DMA((STEPS * MPB // LANES,)),
        ],
        out_specs=pl.BlockSpec(memory_space=pltpu.HBM),
        compiler_params=PARAMS,
    )(returned, address)
    return (depth_after, level_after, mouth_level)


def solution(mesh):
    by_block = P(("river", "coast"), None)
    tiled = P("river", "coast")
    return jax.shard_map(
        per_device,
        mesh=mesh,
        in_specs=(by_block,) * 8
        + (P(("river", "coast"), None, None), by_block)
        + (tiled,) * 5,
        out_specs=(by_block, tiled, by_block),
        check_vma=False,
    )
```

```python
import functools
import math

import jax
import jax.numpy as jnp
from jax import lax
from jax.experimental import pallas as pl
from jax.experimental.pallas import tpu as pltpu
from jax.sharding import PartitionSpec as P

RB = 128
MPB = 32
STEPS = 12

gravity = 9.81
step_seconds = 300.0
cell_metres = 3000.0
river_manning = 0.035
ocean_manning = 0.025
depth_floor = 0.05
reach_offsets = 16

LANES = 128
SENT = 13
TALL = 16
WIDE = 256
PARTS = ((0, 8), (8, 2), (10, 2))
LOOKED_UP = ((0, 8), (8, 4))
CHUNK = 8
HALO = 12
FIELDS = 16
f32, bf16, i32 = jnp.float32, jnp.bfloat16, jnp.int32

PARAMS = pltpu.CompilerParams(vmem_limit_bytes=40 * 1024 * 1024)


def flow_after(unit_flow, upper, lower, bed_top, drive, manning):
    face_depth = jnp.maximum(upper, lower) - bed_top
    driving = drive * jnp.maximum(face_depth, 0.0) * (upper - lower)
    power = -7.0 / 3.0 * math.log2(math.e)
    thin = jnp.exp2(jnp.log(jnp.maximum(face_depth, depth_floor)) * power)
    friction = (gravity * step_seconds * manning * manning) * jnp.abs(unit_flow) * thin
    divisor = 1.0 + friction
    inverse = pl.reciprocal(divisor, approx=True)
    return ((unit_flow + driving) * inverse) * (2.0 - divisor * inverse)


def in_two(values):
    high = values.astype(bf16)
    return high, (values - high.astype(f32)).astype(bf16)


def small(labels):
    return jnp.broadcast_to(labels, (TALL, labels.shape[1])).astype(bf16)


def one_hot_columns(columns, place_of, rhs, lanes):
    labels = small(columns)
    one, none = jnp.ones(labels.shape, bf16), jnp.zeros(labels.shape, bf16)
    for part in range(0, WIDE, TALL):
        hit = place_of(labels, part)
        rhs[part : part + TALL, lanes] = jnp.where(hit, one, none)


def row_owners(owner, steps):
    for part in range(0, owner.shape[0], TALL):
        number = part + lax.broadcasted_iota(i32, (TALL, LANES), 0)
        owner[part : part + TALL] = (number // steps).astype(f32).astype(bf16)


def in_turn(series, at, stride, steps, first):
    parts, row = [], first
    while row < first + 8:
        step = row % steps
        count = min(steps - step, first + 8 - row)
        parts.append(series[pl.ds(at + step * stride, count, stride=stride)])
        row += count
    return parts[0] if len(parts) == 1 else jnp.concatenate(parts, axis=0)


def lay_out(series, at, stride, steps, rows, owner, lhs, lanes):
    turns = math.lcm(steps, 8) // 8
    cycle = [in_turn(series, at, stride, steps, 8 * turn) for turn in range(turns)]
    pairs = [(cycle[2 * k % turns], cycle[(2 * k + 1) % turns]) for k in range(turns)]
    halves = [in_two(jnp.concatenate(pair, axis=0)) for pair in pairs]
    labels = small(rows)
    none = jnp.zeros(labels.shape, bf16)
    high_rows = owner.shape[0]
    for part in range(0, high_rows, TALL):
        hit = labels == owner[part : part + TALL]
        for number, half in enumerate(halves[part // TALL % turns]):
            at_rows = slice(number * high_rows + part, number * high_rows + part + TALL)
            lhs[at_rows, lanes] = jnp.where(hit, half, none)


def look_up(table, rows, hot, steps):
    found = jnp.dot(table, hot, preferred_element_type=f32)
    per = 2 if steps > 6 else 4
    several = (per * steps, rows.shape[1])
    number = (lax.broadcasted_iota(i32, several, 0) // steps).astype(f32)
    labels = jnp.broadcast_to(rows, several) - number
    total = jnp.zeros(several, f32)
    for row in range(0, TALL, per):
        high = found[row * steps : (row + per) * steps]
        low = found[(TALL + row) * steps : (TALL + row + per) * steps]
        total = total + jnp.where(labels == row, high + low, 0.0)
    result = total[:steps]
    for number in range(1, per):
        result = result + total[number * steps : (number + 1) * steps]
    return result


def split_label(number, size):
    return lax.shift_right_logical(number, size.bit_length() - 1), number & (size - 1)


def cell_labels(cells, tile_cols):
    row, column = split_label(cells, tile_cols)
    upper, row = split_label(row, TALL)
    return row, upper * tile_cols + column


def river_kernel(
    devices,
    coasts,
    capacity,
    *refs,
):
    inputs, (depth_out, send_out, address_out), refs = refs[:10], refs[10:13], refs[13:]
    copies = [
        pltpu.make_async_copy(whole, own, refs[10].at[number])
        for number, (whole, own) in enumerate(zip(inputs, refs[:10]))
    ]
    for copy in copies[::-1]:
        copy.start()
    river_steps(devices, coasts, capacity, copies, *refs[:10], depth_out, send_out, address_out, *refs[10:])


def river_steps(
    devices,
    coasts,
    capacity,
    copies,
    depth_in,
    flow_in,
    bed_in,
    width_in,
    length_in,
    runoff_in,
    into_in,
    prev_in,
    tile_in,
    cell_in,
    depth_out,
    send_out,
    address_out,
    arrivals,
    depth_end,
    enters,
    series,
    turned,
    tiles,
    hots,
    counted,
    high_labels,
    low_labels,
    rhs,
    *parts,
):
    owners, slots = parts[: len(PARTS)], parts[len(PARTS) :]
    blocks = depth_in.shape[0]
    groups = LANES // MPB
    rows = blocks // groups
    inland = RB - MPB
    lane = lax.broadcasted_iota(i32, (blocks, RB), 1)

    for copy in copies:
        copy.wait()

    turned[...] = jnp.zeros_like(turned)
    turned[0:MPB, 0:blocks] = tile_in[...].astype(f32)
    turned[MPB : 2 * MPB, 0:blocks] = cell_in[...].astype(f32)
    turned[inland:RB, 0:blocks] = prev_in[...]
    mouths = jnp.transpose(turned[...])[0:blocks]
    prev = mouths

    def grouped(array, first):
        lanes16 = lax.broadcasted_iota(i32, (rows, LANES), 1)
        result = jnp.zeros((rows, LANES), f32)
        for g in range(groups):
            part = array[g * rows : (g + 1) * rows]
            shift = (g * MPB - first) % LANES
            part = part if shift == 0 else pltpu.roll(part, shift, 1)
            result = jnp.where(lanes16 // MPB == g, part, result)
        return result

    tile = grouped(mouths, 0).astype(i32)
    tiles[...] = tile % coasts * (devices // coasts) + tile // coasts
    series[STEPS * rows :] = grouped(mouths, MPB)

    into = into_in[...]
    at_mouth = lane >= inland
    down = jnp.where(at_mouth, 0, into)
    offset = jnp.where(at_mouth, 0, into - lane)
    bed = bed_in[...]

    sources = [(down - 4 * a) & (RB - 1) for a in range(reach_offsets // 4)]

    def below_of(value, a=0):
        return jnp.take_along_axis(value, sources[a], axis=1, mode="promise_in_bounds")

    bed_below = below_of(bed)
    bed_top = jnp.where(at_mouth, bed, jnp.maximum(bed, bed_below))
    drive = gravity * step_seconds / length_in[...]
    width = width_in[...]
    area = step_seconds / (width * length_in[...])
    gain = area * runoff_in[...]
    loss = area * width
    moved = [(turn(offset, 1 + b), turn(width, 1 + b)) for b in range(4)]
    for o in range(reach_offsets):
        where_to, its_width = moved[o % 4]
        weight = its_width * turn(area, -(o - o % 4))
        enters[o] = jnp.where(where_to == o + 1, weight, 0.0)

    def river_turn(substep, depth, flow, below):
        below = jnp.where(at_mouth, prev, below)
        flow = flow_after(flow, bed + depth, below, bed_top, drive, river_manning)
        moved = [turn(flow, 1 + b) for b in range(4)]
        sums = []
        for a in range(0, reach_offsets, 4):
            one, other = [
                enters[a + b] * moved[b] + enters[a + b + 1] * moved[b + 1] for b in (0, 2)
            ]
            sums.append(one + other)
        sums[0] = sums[0] + (depth + gain - loss * flow)
        depth, below = [
            (places[0] + places[1]) + (places[2] + places[3])
            for places in (
                [turn(value, 4 * a) for a, value in enumerate(sums)],
                [below_of(value, a) for a, value in enumerate(sums)],
            )
        ]
        series[substep * rows : (substep + 1) * rows] = grouped(flow * width, inland)
        return depth, flow, bed_below + below

    def count_mouths():
        for i in range(rows):
            names = jnp.broadcast_to(tiles[i : i + 1], (devices, LANES))
            hit = names == lax.broadcasted_iota(i32, (devices, LANES), 0)
            hots[i * devices : (i + 1) * devices] = jnp.where(hit, 1.0, 0.0).astype(bf16)
        shape = (LANES, 2 * LANES)
        earlier = lax.broadcasted_iota(i32, shape, 0) < lax.broadcasted_iota(i32, shape, 1)
        counted[...] = jnp.dot(
            hots[...], jnp.where(earlier, 1.0, 0.0).astype(bf16), preferred_element_type=f32
        )

    def rank_mouths():
        before = jnp.zeros((devices, LANES), f32)
        for i in range(rows):
            part = slice(i * devices, (i + 1) * devices)
            ranks = (counted[part, :LANES] + before) * hots[part].astype(f32)
            rank = jnp.sum(ranks, axis=0, keepdims=True).astype(i32)
            address_out[i : i + 1] = tiles[i : i + 1] * capacity + rank
            before = before + counted[part, LANES:]

    one, none = jnp.ones((LANES, LANES), bf16), jnp.zeros((LANES, LANES), bf16)
    number = lax.broadcasted_iota(i32, (TALL, LANES), 0).astype(f32)

    def label_mouths():
        high, low = split_label(address_out[...], WIDE)
        high_labels[...] = high.astype(f32)
        low_labels[...] = jnp.transpose(low.astype(f32))

    def slot_columns(group):
        place = lax.broadcasted_iota(i32, (LANES, LANES), 1).astype(f32).astype(bf16)
        for i in range(group * rows // 4, (group + 1) * rows // 4):
            lanes = slice(i * LANES, (i + 1) * LANES)
            column = jnp.broadcast_to(low_labels[:, i : i + 1], (LANES, LANES)).astype(bf16)
            for half in range(2):
                hit = column - half * LANES == place
                rhs[lanes, half * LANES : (half + 1) * LANES] = jnp.where(hit, one, none)

    def place_series(part, group):
        first, steps = PARTS[part]
        owner, lhs = owners[part], slots[part]
        for i in range(group * rows // 4, (group + 1) * rows // 4):
            lanes = slice(i * LANES, (i + 1) * LANES)
            labels = high_labels[i : i + 1]
            lay_out(series, first * rows + i, rows, steps, labels, owner, lhs, lanes)
            if part == 0:
                cells = series[STEPS * rows + i : STEPS * rows + i + 1]
                cells = jnp.where(number == labels, cells, 0.0)
                for half, value in enumerate(in_two(cells)):
                    at = 2 * TALL * steps + half * TALL
                    lhs[at : at + TALL, lanes] = value

    def pack(part):
        first, steps = PARTS[part]
        high_rows = TALL * steps
        lhs = slots[part]
        both = jnp.dot(lhs[...], rhs[...], preferred_element_type=f32)
        packed = both[:high_rows] + both[high_rows : 2 * high_rows]
        for half in range(2):
            lanes = slice(half * LANES, (half + 1) * LANES)
            for row in range(TALL):
                at = (2 * row + half) * SENT + first
                send_out[at : at + steps] = packed[row * steps : (row + 1) * steps, lanes]
            if part == 0:
                cells = both[2 * high_rows : 2 * high_rows + TALL] + both[2 * high_rows + TALL :]
                send_out[pl.ds(half * SENT + STEPS, TALL, stride=2 * SENT)] = cells[:, lanes]

    beside = {0: [count_mouths], 1: [rank_mouths], 2: [label_mouths]}
    beside |= {3 + group: [functools.partial(slot_columns, group)] for group in range(4)}
    beside |= {8: [functools.partial(place_series, 0, group) for group in range(2)]}
    beside |= {9: [functools.partial(place_series, 0, group) for group in range(2, 4)]}
    beside |= {10: [functools.partial(pack, 0)]}
    beside[10] += [functools.partial(place_series, 1, group) for group in range(4)]
    beside |= {11: [functools.partial(pack, 1)]}
    for owner, (_, steps) in zip(owners, PARTS):
        row_owners(owner, steps)
    depth, flow = depth_in[...], flow_in[...]
    below = bed_below + below_of(depth)
    for substep in range(STEPS):
        depth, flow, below = river_turn(substep, depth, flow, below)
        for work in beside.get(substep, []):
            work()
    depth_end[...] = depth
    finished = pltpu.make_async_copy(depth_end, depth_out, arrivals.at[len(copies)])
    finished.start()
    for group in range(4):
        place_series(2, group)
    pack(2)
    finished.wait()


def reach_of(field):
    return STEPS - 1 - field if field < STEPS else HALO


def turn(value, lanes):
    lanes %= value.shape[1]
    return value if lanes == 0 else pltpu.roll(value, lanes, 1)


ROW_AT = [sum(reach_of(f) for f in range(field)) for field in range(FIELDS + 1)]
ROWS_SENT = -(-ROW_AT[FIELDS] // 8) * 8


def add_in_chunks(arrived, row_labels, column_labels, owner, places, lhs, rhs):
    row_owners(owner, STEPS)
    row_owners(places, 1)
    groups = arrived.shape[0] // SENT

    def place_of(label, part):
        return label == places[part : part + TALL]

    def place(chunk):
        for s in range(chunk, chunk + CHUNK):
            lanes = slice(s * LANES, (s + 1) * LANES)
            lay_out(arrived, s * SENT, 1, STEPS, row_labels[s : s + 1], owner, lhs, lanes)
            one_hot_columns(column_labels[s : s + 1], place_of, rhs, lanes)

    both = jnp.zeros((lhs.shape[0], WIDE), f32)
    place(0)
    for chunk in range(0, groups, CHUNK):
        if chunk + CHUNK < groups:
            place(chunk + CHUNK)
        lanes = slice(chunk * LANES, (chunk + CHUNK) * LANES)
        both = both + lax.dot_general(
            lhs[:, lanes], rhs[:, lanes], (((1,), (1,)), ((), ())), preferred_element_type=f32
        )
    half = lhs.shape[0] // 2
    return both[:half] + both[half:]


def edge_kernel(arrived, *refs):
    inputs, (odd, sea), refs = refs[:5], refs[5:7], refs[7:]
    sea_level, sea_bed, wet_mask, flux_east, flux_north, arrivals = refs[:6]
    owner, places, row_labels, column_labels, lhs, rhs, sums = refs[6:]
    first_of_pair = lax.axis_index("river") % 2 == 0
    copies = [
        pltpu.make_async_copy(whole, own, arrivals.at[number])
        for number, (whole, own) in enumerate(zip(inputs, refs[:5]))
    ]
    for copy in copies:
        copy.start()
    groups = arrived.shape[0] // SENT
    tile_rows, tile_cols = sea_level.shape

    cells = arrived[pl.ds(STEPS, groups, stride=SENT)].astype(i32)
    row, column = split_label(cells, tile_cols)
    row = row - jnp.where(first_of_pair, 0, tile_rows - HALO)
    upper = jnp.where(row >= HALO // 2, 1, 0)
    inside = (row >= 0) & (row < HALO)
    row_labels[...] = jnp.where(inside, row - upper * (HALO // 2), WIDE - 1).astype(f32)
    column_labels[...] = (column + upper * tile_cols).astype(f32)
    total = add_in_chunks(arrived, row_labels, column_labels, owner, places, lhs, rhs)
    high_rows = total.shape[0]
    for half in range(2):
        part = slice(half * high_rows, (half + 1) * high_rows)
        sums[part] = total[:, half * LANES : (half + 1) * LANES]

    def put(field, start, end):
        reach = reach_of(field)
        if reach:
            last, first = end[end.shape[0] - reach :], start[:reach]
            part = slice(ROW_AT[field], ROW_AT[field] + reach)
            odd[part] = jnp.where(first_of_pair, first, last)

    odd[ROWS_SENT - 8 :] = jnp.zeros((8, LANES), f32)
    for step in range(STEPS):
        halves = [
            sums[pl.ds(half * high_rows + step, HALO // 2, stride=STEPS)] for half in range(2)
        ]
        rows = jnp.concatenate(halves, axis=0)
        put(step, rows, rows)
    for copy in copies:
        copy.wait()
    bed = sea_bed[...]
    level = jnp.where(wet_mask[...] == 1, jnp.maximum(sea_level[...], bed), bed)
    for number, value in enumerate((level, bed, flux_east[...], flux_north[...])):
        sea[number * tile_rows : (number + 1) * tile_rows] = value
        put(STEPS + number, value, value)


def source_kernel(arrived, sea, fields, even, rhs, label_out, *refs):
    owner, places, column_labels, lhs, sums = refs
    first_of_pair = lax.axis_index("river") % 2 == 0
    groups = arrived.shape[0] // SENT
    tile_rows, tile_cols = sea.shape[0] // 4, sea.shape[1]

    cells = arrived[pl.ds(STEPS, groups, stride=SENT)].astype(i32)
    row, column = cell_labels(cells, tile_cols)
    label_out[...] = row.astype(f32)
    column_labels[...] = column.astype(f32)
    total = add_in_chunks(arrived, label_out, column_labels, owner, places, lhs, rhs)
    high_rows = total.shape[0]
    for half in range(2):
        part = slice(half * high_rows, (half + 1) * high_rows)
        sums[part] = total[:, half * LANES : (half + 1) * LANES]

    def put(field, value):
        fields[field * tile_rows : (field + 1) * tile_rows] = value
        reach = reach_of(field)
        if reach:
            last, first = value[tile_rows - reach :], value[:reach]
            part = slice(ROW_AT[field], ROW_AT[field] + reach)
            even[part] = jnp.where(first_of_pair, last, first)

    even[ROWS_SENT - 8 :] = jnp.zeros((8, LANES), f32)
    for step in range(STEPS):
        halves = [sums[pl.ds(half * high_rows + step, TALL, stride=STEPS)] for half in range(2)]
        put(step, jnp.concatenate(halves, axis=0))
    for number in range(4):
        put(STEPS + number, sea[number * tile_rows : (number + 1) * tile_rows])


def strip_kernel(fields, from_odd, from_even, tall, odd, even):
    upper = lax.axis_index("river") % 2 == 0
    first_of_pair = lax.axis_index("coast") % 2 == 0
    from_before = jnp.where(upper, from_odd[...], from_even[...])
    from_after = jnp.where(upper, from_even[...], from_odd[...])
    tile_rows = fields.shape[0] // FIELDS
    height = tall.shape[0] // FIELDS
    lane = lax.broadcasted_iota(i32, (height, LANES), 1)
    ends = jnp.zeros((height, LANES), f32)
    starts = jnp.zeros((height, LANES), f32)
    for field in range(FIELDS):
        reach, at = reach_of(field), ROW_AT[field]
        parts = [fields[field * tile_rows : (field + 1) * tile_rows]]
        if reach:
            parts.append(from_after[at : at + reach])
        if reach < HALO:
            parts.append(jnp.zeros((2 * HALO - 2 * reach, LANES), f32))
        if reach:
            parts.append(from_before[at : at + reach])
        value = jnp.concatenate(parts, axis=0)
        tall[field * height : (field + 1) * height] = value
        if reach:
            here = (lane >= at) & (lane < at + reach)
            ends = jnp.where(here, turn(value, at + reach - LANES), ends)
            starts = jnp.where(here, turn(value, at), starts)
    odd[...] = jnp.where(first_of_pair, starts, ends)
    even[...] = jnp.where(first_of_pair, ends, starts)


def ocean_kernel(
    tile_rows, tall, from_odd, from_even, row_labels, hot, level_out, replies, history, level_end, departure
):
    height = tall.shape[0] // FIELDS
    width = 2 * LANES
    river, coast = lax.axis_index("river"), lax.axis_index("coast")
    rivers, coasts = lax.axis_size("river"), lax.axis_size("coast")
    lane = lax.broadcasted_iota(i32, (height, LANES), 1)
    from_left = jnp.where(coast % 2 == 0, from_odd[...], from_even[...])
    from_right = jnp.where(coast % 2 == 0, from_even[...], from_odd[...])

    def whole(field):
        reach, at = reach_of(field), ROW_AT[field]
        beside = jnp.zeros((height, LANES), f32)
        if reach:
            beside = jnp.where(lane < reach, turn(from_right, -at), beside)
            beside = jnp.where(lane >= LANES - reach, turn(from_left, -at - reach), beside)
        return jnp.concatenate([tall[field * height : (field + 1) * height], beside], axis=1)

    level, bed, east, north = [whole(STEPS + number) for number in range(4)]

    row = lax.broadcasted_iota(i32, (height, width), 0)
    column = lax.broadcasted_iota(i32, (height, width), 1)
    row_in = jnp.where(
        row < tile_rows, 1, jnp.where(row < tile_rows + HALO, (river < rivers - 1).astype(i32), (river > 0).astype(i32))
    )
    column_in = jnp.where(
        column < LANES, 1, jnp.where(column < LANES + LANES // 2, (coast < coasts - 1).astype(i32), (coast > 0).astype(i32))
    )
    inside = row_in * column_in == 1

    def next_row(value):
        return pltpu.roll(value, height - 1, 0)

    def next_column(value):
        return pltpu.roll(value, width - 1, 1)

    bed_east = jnp.maximum(bed, next_row(bed))
    bed_north = jnp.maximum(bed, next_column(bed))
    drive = gravity * step_seconds / cell_metres

    def ocean_turn(first, steps, step, level, east, north):
        source = whole(step) * (step_seconds / (cell_metres * cell_metres))
        east = flow_after(east, level, next_row(level), bed_east, drive, ocean_manning)
        north = flow_after(north, level, next_column(level), bed_north, drive, ocean_manning)
        spread = east - pltpu.roll(east, 1, 0) + north - pltpu.roll(north, 1, 1)
        level = level - step_seconds / cell_metres * spread + source
        level = jnp.where(inside, level, 0.0)
        for half in range(2):
            part = level[half * TALL : (half + 1) * TALL, :LANES]
            at = TALL * (2 * first + half * steps) + step - first
            history[pl.ds(at, TALL, stride=steps)] = part
        return level, east, north

    def table_of(first, steps):
        high_rows, at = TALL * steps, 2 * TALL * first
        halves = [history[at + half * high_rows : at + (half + 1) * high_rows] for half in range(2)]
        return jnp.concatenate(in_two(jnp.concatenate(halves, axis=1)), axis=0)

    def reply(table, first, steps, group, of):
        count = replies.shape[0] // STEPS // of
        for s in range(group * count, (group + 1) * count, 2):
            rows = jnp.concatenate([row_labels[s : s + 1], row_labels[s + 1 : s + 2]], axis=1)
            found = look_up(table, rows, hot[:, s * LANES : (s + 2) * LANES], steps)
            for half in range(2):
                at = (s + half) * STEPS + first
                replies[at : at + steps] = found[:, half * LANES : (half + 1) * LANES]

    waiting = []
    for part, (first, steps) in enumerate(LOOKED_UP):
        for step in range(first, first + steps):
            level, east, north = ocean_turn(first, steps, step, level, east, north)
            if waiting:
                reply(*waiting, step - first, steps)
        if part == len(LOOKED_UP) - 1:
            level_end[...] = level[:tile_rows, :LANES]
            finished = pltpu.make_async_copy(level_end, level_out, departure)
            finished.start()
        waiting = [table_of(first, steps), first, steps]
    reply(*waiting, 0, 1)
    finished.wait()


def mouth_kernel(returned, address, level_out, whole, series, hot, block, departures):
    rows = address.shape[0]
    groups = LANES // MPB
    place = lax.broadcasted_iota(i32, (TALL, 2 * LANES), 0).astype(f32).astype(bf16)

    def place_of(label, part):
        return label - part == place

    labels = []
    for i in range(0, rows, 2):
        pair = jnp.concatenate([address[i : i + 1], address[i + 1 : i + 2]], axis=1)
        high, low = [label.astype(f32) for label in split_label(pair, WIDE)]
        one_hot_columns(low, place_of, hot, slice(i * LANES, (i + 2) * LANES))
        labels.append(high)
    lane = lax.broadcasted_iota(i32, (rows, LANES), 1)
    copies = []
    for first, steps in LOOKED_UP:
        for row in range(TALL):
            for half in range(2):
                at = (2 * row + half) * STEPS + first
                to = first * TALL + row * steps
                lanes = slice(half * LANES, (half + 1) * LANES)
                whole[to : to + steps, lanes] = returned[at : at + steps]
        own = whole[first * TALL : (first + steps) * TALL]
        table = jnp.concatenate(in_two(own), axis=0)
        for i in range(0, rows, 2):
            lanes = slice(i * LANES, (i + 2) * LANES)
            found = look_up(table, labels[i // 2], hot[:, lanes], steps)
            series[pl.ds(first * rows + i, steps, stride=rows)] = found[:, :LANES]
            series[pl.ds(first * rows + i + 1, steps, stride=rows)] = found[:, LANES:]
        for number in range(first // groups, (first + steps) // groups):
            for g in range(groups):
                result = jnp.zeros((rows, LANES), f32)
                for place in range(groups):
                    at = (number * groups + place) * rows
                    part = turn(series[at : at + rows], (place - g) * MPB)
                    result = jnp.where(lane // MPB == place, part, result)
                block[number, g * rows : (g + 1) * rows] = result
            to = level_out.at[:, pl.ds(number * LANES, LANES)]
            copies.append(pltpu.make_async_copy(block.at[number], to, departures.at[number]))
            copies[-1].start()
    for copy in copies:
        copy.wait()


def shape(*dims, dtype=f32):
    return jax.ShapeDtypeStruct(dims, dtype)


def cost(products):
    return pl.CostEstimate(flops=2 * products, bytes_accessed=8 << 20, transcendentals=0)


def in_hbm(*arrays):
    return [pltpu.with_memory_space_constraint(whole, pltpu.HBM) for whole in arrays]


def swap(values, tall, devices, capacity):
    per = LANES // capacity
    if per > 1:
        values = values.reshape(devices // per, tall, per, capacity).transpose(0, 2, 1, 3)
    values = values.reshape(devices, 1, tall * capacity)
    values = lax.all_to_all(values, ("coast", "river"), split_axis=0, concat_axis=0, tiled=True)
    if per > 1:
        values = values.reshape(devices // per, per, tall, capacity).transpose(0, 2, 1, 3)
    return values.reshape(devices // per * tall, LANES)


def with_neighbour(value, axis, start):
    pairs = range(start, lax.axis_size(axis) - 1, 2)
    return lax.ppermute(value, axis, [(i + k, i + 1 - k) for i in pairs for k in range(2)])


def per_device(
    reach_depth,
    reach_flow,
    reach_bed,
    reach_width,
    reach_length,
    runoff,
    flows_into,
    mouth_prev,
    mouth_tile,
    mouth_cell,
    sea_level,
    sea_bed,
    wet_mask,
    flux_east,
    flux_north,
):
    devices = lax.axis_size("river") * lax.axis_size("coast")
    blocks = reach_depth.shape[0]
    tile_rows, tile_cols = sea_level.shape
    mouths = blocks * MPB
    capacity = max(2, 2 * mouths // devices)
    groups = devices * capacity // LANES
    rows = mouths // LANES
    height = tile_rows + 2 * HALO

    depth_after, sending, address = pl.pallas_call(
        functools.partial(river_kernel, devices, lax.axis_size("coast"), capacity),
        name="river",
        out_shape=(
            shape(blocks, RB),
            shape(groups * SENT, LANES),
            shape(rows, LANES, dtype=i32),
        ),
        in_specs=[pl.BlockSpec(memory_space=pltpu.HBM)] * 10,
        out_specs=(
            pl.BlockSpec(memory_space=pltpu.HBM),
            pl.BlockSpec(memory_space=pltpu.VMEM),
            pl.BlockSpec(memory_space=pltpu.VMEM),
        ),
        scratch_shapes=[pltpu.VMEM((blocks, RB), f32)] * 6
        + [
            pltpu.VMEM((blocks, RB), i32),
            pltpu.VMEM((MPB, blocks), f32),
            pltpu.VMEM((MPB, blocks), i32),
            pltpu.VMEM((MPB, blocks), i32),
            pltpu.SemaphoreType.DMA((11,)),
            pltpu.VMEM((blocks, RB), f32),
            pltpu.VMEM((reach_offsets, blocks, RB), f32),
            pltpu.VMEM((SENT * rows, LANES), f32),
            pltpu.VMEM((RB, LANES), f32),
            pltpu.VMEM((rows, LANES), i32),
            pltpu.VMEM((rows * devices, LANES), bf16),
            pltpu.VMEM((rows * devices, 2 * LANES), f32),
            pltpu.VMEM((rows, LANES), f32),
            pltpu.VMEM((LANES, rows), f32),
            pltpu.VMEM((mouths, WIDE), bf16),
            *[pltpu.VMEM((TALL * steps, LANES), bf16) for _, steps in PARTS],
            *[
                pltpu.VMEM((2 * TALL * (steps + (first == 0)), mouths), bf16)
                for first, steps in PARTS
            ],
        ],
        compiler_params=PARAMS,
    )(
        *in_hbm(
            reach_depth,
            reach_flow,
            reach_bed,
            reach_width,
            reach_length,
            runoff,
            flows_into,
            mouth_prev.T,
            mouth_tile[:, :, 0].T,
            mouth_cell.T,
        )
    )
    arrived = swap(sending, SENT, devices, capacity)

    edge_rows = -(-HALO // 2 * STEPS // TALL) * TALL
    odd, sea = pl.pallas_call(
        edge_kernel,
        name="edges",
        out_shape=(shape(ROWS_SENT, LANES), shape(4 * tile_rows, tile_cols)),
        in_specs=[pl.BlockSpec(memory_space=pltpu.VMEM)]
        + [pl.BlockSpec(memory_space=pltpu.HBM)] * 5,
        scratch_shapes=[
            pltpu.VMEM((tile_rows, tile_cols), f32),
            pltpu.VMEM((tile_rows, tile_cols), f32),
            pltpu.VMEM((tile_rows, tile_cols), i32),
            pltpu.VMEM((tile_rows, tile_cols), f32),
            pltpu.VMEM((tile_rows, tile_cols), f32),
            pltpu.SemaphoreType.DMA((5,)),
            pltpu.VMEM((edge_rows, LANES), bf16),
            pltpu.VMEM((WIDE, LANES), bf16),
            pltpu.VMEM((groups, LANES), f32),
            pltpu.VMEM((groups, LANES), f32),
            pltpu.VMEM((2 * edge_rows, groups * LANES), bf16),
            pltpu.VMEM((WIDE, groups * LANES), bf16),
            pltpu.VMEM((2 * edge_rows, LANES), f32),
        ],
        cost_estimate=cost(2 * edge_rows * WIDE * groups * LANES),
        compiler_params=PARAMS,
    )(arrived, *in_hbm(sea_level, sea_bed, wet_mask, flux_east, flux_north))
    from_odd = with_neighbour(odd, "river", 1)

    fields, even, hot, labels = pl.pallas_call(
        source_kernel,
        name="sources",
        out_shape=(
            shape(FIELDS * tile_rows, LANES),
            shape(ROWS_SENT, LANES),
            shape(WIDE, groups * LANES, dtype=bf16),
            shape(groups, LANES),
        ),
        scratch_shapes=[
            pltpu.VMEM((TALL * STEPS, LANES), bf16),
            pltpu.VMEM((WIDE, LANES), bf16),
            pltpu.VMEM((groups, LANES), f32),
            pltpu.VMEM((2 * TALL * STEPS, groups * LANES), bf16),
            pltpu.VMEM((2 * TALL * STEPS, LANES), f32),
        ],
        cost_estimate=cost(2 * TALL * STEPS * WIDE * groups * LANES),
        compiler_params=PARAMS,
    )(arrived, sea)
    from_even = with_neighbour(even, "river", 0)

    tall, odd, even = pl.pallas_call(
        strip_kernel,
        name="strips",
        out_shape=(shape(FIELDS * height, LANES), shape(height, LANES), shape(height, LANES)),
        compiler_params=PARAMS,
    )(fields, from_odd, from_even)
    from_odd, from_even = with_neighbour(odd, "coast", 1), with_neighbour(even, "coast", 0)

    level_after, replies = pl.pallas_call(
        functools.partial(ocean_kernel, tile_rows),
        name="ocean",
        out_shape=(shape(tile_rows, tile_cols), shape(groups * STEPS, LANES)),
        scratch_shapes=[
            pltpu.VMEM((2 * TALL * STEPS, LANES), f32),
            pltpu.VMEM((tile_rows, tile_cols), f32),
            pltpu.SemaphoreType.DMA,
        ],
        out_specs=(
            pl.BlockSpec(memory_space=pltpu.HBM),
            pl.BlockSpec(memory_space=pltpu.VMEM),
        ),
        compiler_params=PARAMS,
    )(tall, from_odd, from_even, labels, hot)
    returned = swap(replies, STEPS, devices, capacity)

    mouth_level = pl.pallas_call(
        mouth_kernel,
        name="mouths",
        out_shape=shape(blocks, STEPS * MPB),
        scratch_shapes=[
            pltpu.VMEM((TALL * STEPS, WIDE), f32),
            pltpu.VMEM((STEPS * rows, LANES), f32),
            pltpu.VMEM((WIDE, mouths), bf16),
            pltpu.VMEM((STEPS * MPB // LANES, blocks, LANES), f32),
            pltpu.SemaphoreType.DMA((STEPS * MPB // LANES,)),
        ],
        out_specs=pl.BlockSpec(memory_space=pltpu.HBM),
        compiler_params=PARAMS,
    )(returned, address)
    return (depth_after, level_after, mouth_level)


def solution(mesh):
    by_block = P(("river", "coast"), None)
    tiled = P("river", "coast")
    return jax.shard_map(
        per_device,
        mesh=mesh,
        in_specs=(by_block,) * 8
        + (P(("river", "coast"), None, None), by_block)
        + (tiled,) * 5,
        out_specs=(by_block, tiled, by_block),
        check_vma=False,
    )
```

```python
import functools
import math

import jax
import jax.numpy as jnp
from jax import lax
from jax.experimental import pallas as pl
from jax.experimental.pallas import tpu as pltpu
from jax.sharding import PartitionSpec as P

RB = 128
MPB = 32
STEPS = 12

gravity = 9.81
step_seconds = 300.0
cell_metres = 3000.0
river_manning = 0.035
ocean_manning = 0.025
depth_floor = 0.05
reach_offsets = 16

LANES = 128
SENT = 13
TALL = 16
WIDE = 256
PARTS = ((0, 8), (8, 2), (10, 2))
LOOKED_UP = ((0, 8), (8, 4))
CHUNK = 8
HALO = 12
FIELDS = 16
f32, bf16, i32 = jnp.float32, jnp.bfloat16, jnp.int32

PARAMS = pltpu.CompilerParams(vmem_limit_bytes=40 * 1024 * 1024)


def flow_after(unit_flow, upper, lower, bed_top, drive, manning):
    face_depth = jnp.maximum(upper, lower) - bed_top
    driving = drive * jnp.maximum(face_depth, 0.0) * (upper - lower)
    power = -7.0 / 3.0 * math.log2(math.e)
    thin = jnp.exp2(jnp.log(jnp.maximum(face_depth, depth_floor)) * power)
    friction = (gravity * step_seconds * manning * manning) * jnp.abs(unit_flow) * thin
    divisor = 1.0 + friction
    inverse = pl.reciprocal(divisor, approx=True)
    return ((unit_flow + driving) * inverse) * (2.0 - divisor * inverse)


def in_two(values):
    high = values.astype(bf16)
    return high, (values - high.astype(f32)).astype(bf16)


def small(labels):
    return jnp.broadcast_to(labels, (TALL, labels.shape[1])).astype(bf16)


def one_hot_columns(columns, place_of, rhs, lanes):
    labels = small(columns)
    one, none = jnp.ones(labels.shape, bf16), jnp.zeros(labels.shape, bf16)
    for part in range(0, WIDE, TALL):
        hit = place_of(labels, part)
        rhs[part : part + TALL, lanes] = jnp.where(hit, one, none)


def row_owners(owner, steps):
    for part in range(0, owner.shape[0], TALL):
        number = part + lax.broadcasted_iota(i32, (TALL, LANES), 0)
        owner[part : part + TALL] = (number // steps).astype(f32).astype(bf16)


def in_turn(series, at, stride, steps, first):
    parts, row = [], first
    while row < first + 8:
        step = row % steps
        count = min(steps - step, first + 8 - row)
        parts.append(series[pl.ds(at + step * stride, count, stride=stride)])
        row += count
    return parts[0] if len(parts) == 1 else jnp.concatenate(parts, axis=0)


def lay_out(series, at, stride, steps, rows, owner, lhs, lanes):
    turns = math.lcm(steps, 8) // 8
    cycle = [in_turn(series, at, stride, steps, 8 * turn) for turn in range(turns)]
    pairs = [(cycle[2 * k % turns], cycle[(2 * k + 1) % turns]) for k in range(turns)]
    halves = [in_two(jnp.concatenate(pair, axis=0)) for pair in pairs]
    labels = small(rows)
    none = jnp.zeros(labels.shape, bf16)
    high_rows = owner.shape[0]
    for part in range(0, high_rows, TALL):
        hit = labels == owner[part : part + TALL]
        for number, half in enumerate(halves[part // TALL % turns]):
            at_rows = slice(number * high_rows + part, number * high_rows + part + TALL)
            lhs[at_rows, lanes] = jnp.where(hit, half, none)


def look_up(table, rows, hot, steps):
    found = jnp.dot(table, hot, preferred_element_type=f32)
    per = 2 if steps > 6 else 4
    several = (per * steps, rows.shape[1])
    number = (lax.broadcasted_iota(i32, several, 0) // steps).astype(f32)
    labels = jnp.broadcast_to(rows, several) - number
    total = jnp.zeros(several, f32)
    for row in range(0, TALL, per):
        high = found[row * steps : (row + per) * steps]
        low = found[(TALL + row) * steps : (TALL + row + per) * steps]
        total = total + jnp.where(labels == row, high + low, 0.0)
    result = total[:steps]
    for number in range(1, per):
        result = result + total[number * steps : (number + 1) * steps]
    return result


def split_label(number, size):
    return lax.shift_right_logical(number, size.bit_length() - 1), number & (size - 1)


def cell_labels(cells, tile_cols):
    row, column = split_label(cells, tile_cols)
    upper, row = split_label(row, TALL)
    return row, upper * tile_cols + column


def river_kernel(
    devices,
    coasts,
    capacity,
    *refs,
):
    inputs, (depth_out, send_out, address_out, sea_out), refs = refs[:15], refs[15:19], refs[19:]
    arrivals = refs[15]
    copies = [
        pltpu.make_async_copy(whole, own, arrivals.at[number])
        for number, (whole, own) in enumerate(zip(inputs, refs[:15]))
    ]
    copies, of_sea = copies[:10], copies[10:]
    for copy in copies[::-1] + of_sea:
        copy.start()
    outputs = (depth_out, send_out, address_out)
    finished = river_steps(
        devices, coasts, capacity, copies, *refs[:10], *outputs, arrivals, *refs[16:]
    )

    sea_level, sea_bed, wet_mask, flux_east, flux_north = refs[10:15]
    tile_rows = sea_level.shape[0]
    for copy in of_sea:
        copy.wait()
    bed = sea_bed[...]
    level = jnp.where(wet_mask[...] == 1, jnp.maximum(sea_level[...], bed), bed)
    for number, value in enumerate((level, bed, flux_east[...], flux_north[...])):
        sea_out[number * tile_rows : (number + 1) * tile_rows] = value
    finished.wait()


def river_steps(
    devices,
    coasts,
    capacity,
    copies,
    depth_in,
    flow_in,
    bed_in,
    width_in,
    length_in,
    runoff_in,
    into_in,
    prev_in,
    tile_in,
    cell_in,
    depth_out,
    send_out,
    address_out,
    arrivals,
    depth_end,
    enters,
    series,
    turned,
    tiles,
    hots,
    counted,
    high_labels,
    low_labels,
    rhs,
    *parts,
):
    owners, slots = parts[: len(PARTS)], parts[len(PARTS) :]
    blocks = depth_in.shape[0]
    groups = LANES // MPB
    rows = blocks // groups
    inland = RB - MPB
    lane = lax.broadcasted_iota(i32, (blocks, RB), 1)

    for copy in copies[7:]:
        copy.wait()

    turned[...] = jnp.zeros_like(turned)
    turned[0:MPB, 0:blocks] = tile_in[...].astype(f32)
    turned[MPB : 2 * MPB, 0:blocks] = cell_in[...].astype(f32)
    turned[inland:RB, 0:blocks] = prev_in[...]
    mouths = jnp.transpose(turned[...])[0:blocks]
    prev = mouths

    def grouped(array, first):
        lanes16 = lax.broadcasted_iota(i32, (rows, LANES), 1)
        result = jnp.zeros((rows, LANES), f32)
        for g in range(groups):
            part = array[g * rows : (g + 1) * rows]
            shift = (g * MPB - first) % LANES
            part = part if shift == 0 else pltpu.roll(part, shift, 1)
            result = jnp.where(lanes16 // MPB == g, part, result)
        return result

    tile = grouped(mouths, 0).astype(i32)
    tiles[...] = tile % coasts * (devices // coasts) + tile // coasts
    series[STEPS * rows :] = grouped(mouths, MPB)
    for copy in copies[:7]:
        copy.wait()

    into = into_in[...]
    at_mouth = lane >= inland
    down = jnp.where(at_mouth, 0, into)
    offset = jnp.where(at_mouth, 0, into - lane)
    bed = bed_in[...]

    sources = [(down - 4 * a) & (RB - 1) for a in range(reach_offsets // 4)]

    def below_of(value, a=0):
        return jnp.take_along_axis(value, sources[a], axis=1, mode="promise_in_bounds")

    bed_below = below_of(bed)
    bed_top = jnp.where(at_mouth, bed, jnp.maximum(bed, bed_below))
    drive = gravity * step_seconds / length_in[...]
    width = width_in[...]
    area = step_seconds / (width * length_in[...])
    gain = area * runoff_in[...]
    loss = area * width
    moved = [(turn(offset, 1 + b), turn(width, 1 + b)) for b in range(4)]
    for o in range(reach_offsets):
        where_to, its_width = moved[o % 4]
        weight = its_width * turn(area, -(o - o % 4))
        enters[o] = jnp.where(where_to == o + 1, weight, 0.0)

    def river_turn(substep, depth, flow, below):
        below = jnp.where(at_mouth, prev, below)
        flow = flow_after(flow, bed + depth, below, bed_top, drive, river_manning)
        moved = [turn(flow, 1 + b) for b in range(4)]
        sums = []
        for a in range(0, reach_offsets, 4):
            one, other = [
                enters[a + b] * moved[b] + enters[a + b + 1] * moved[b + 1] for b in (0, 2)
            ]
            sums.append(one + other)
        sums[0] = sums[0] + (depth + gain - loss * flow)
        depth, below = [
            (places[0] + places[1]) + (places[2] + places[3])
            for places in (
                [turn(value, 4 * a) for a, value in enumerate(sums)],
                [below_of(value, a) for a, value in enumerate(sums)],
            )
        ]
        series[substep * rows : (substep + 1) * rows] = grouped(flow * width, inland)
        return depth, flow, bed_below + below

    def count_mouths():
        for i in range(rows):
            names = jnp.broadcast_to(tiles[i : i + 1], (devices, LANES))
            hit = names == lax.broadcasted_iota(i32, (devices, LANES), 0)
            hots[i * devices : (i + 1) * devices] = jnp.where(hit, 1.0, 0.0).astype(bf16)
        shape = (LANES, 2 * LANES)
        earlier = lax.broadcasted_iota(i32, shape, 0) < lax.broadcasted_iota(i32, shape, 1)
        counted[...] = jnp.dot(
            hots[...], jnp.where(earlier, 1.0, 0.0).astype(bf16), preferred_element_type=f32
        )

    def rank_mouths():
        before = jnp.zeros((devices, LANES), f32)
        for i in range(rows):
            part = slice(i * devices, (i + 1) * devices)
            ranks = (counted[part, :LANES] + before) * hots[part].astype(f32)
            rank = jnp.sum(ranks, axis=0, keepdims=True).astype(i32)
            address_out[i : i + 1] = tiles[i : i + 1] * capacity + rank
            before = before + counted[part, LANES:]

    one, none = jnp.ones((LANES, LANES), bf16), jnp.zeros((LANES, LANES), bf16)
    number = lax.broadcasted_iota(i32, (TALL, LANES), 0).astype(f32)

    def label_mouths():
        high, low = split_label(address_out[...], WIDE)
        high_labels[...] = high.astype(f32)
        low_labels[...] = jnp.transpose(low.astype(f32))

    def slot_columns(group):
        place = lax.broadcasted_iota(i32, (LANES, LANES), 1).astype(f32).astype(bf16)
        for i in range(group * rows // 4, (group + 1) * rows // 4):
            lanes = slice(i * LANES, (i + 1) * LANES)
            column = jnp.broadcast_to(low_labels[:, i : i + 1], (LANES, LANES)).astype(bf16)
            for half in range(2):
                hit = column - half * LANES == place
                rhs[lanes, half * LANES : (half + 1) * LANES] = jnp.where(hit, one, none)

    def place_series(part, group):
        first, steps = PARTS[part]
        owner, lhs = owners[part], slots[part]
        for i in range(group * rows // 4, (group + 1) * rows // 4):
            lanes = slice(i * LANES, (i + 1) * LANES)
            labels = high_labels[i : i + 1]
            lay_out(series, first * rows + i, rows, steps, labels, owner, lhs, lanes)
            if part == 0:
                cells = series[STEPS * rows + i : STEPS * rows + i + 1]
                cells = jnp.where(number == labels, cells, 0.0)
                for half, value in enumerate(in_two(cells)):
                    at = 2 * TALL * steps + half * TALL
                    lhs[at : at + TALL, lanes] = value

    def pack(part):
        first, steps = PARTS[part]
        high_rows = TALL * steps
        lhs = slots[part]
        both = jnp.dot(lhs[...], rhs[...], preferred_element_type=f32)
        packed = both[:high_rows] + both[high_rows : 2 * high_rows]
        for half in range(2):
            lanes = slice(half * LANES, (half + 1) * LANES)
            for row in range(TALL):
                at = (2 * row + half) * SENT + first
                send_out[at : at + steps] = packed[row * steps : (row + 1) * steps, lanes]
            if part == 0:
                cells = both[2 * high_rows : 2 * high_rows + TALL] + both[2 * high_rows + TALL :]
                send_out[pl.ds(half * SENT + STEPS, TALL, stride=2 * SENT)] = cells[:, lanes]

    beside = {0: [count_mouths], 1: [rank_mouths], 2: [label_mouths]}
    beside |= {3 + group: [functools.partial(slot_columns, group)] for group in range(4)}
    beside |= {8: [functools.partial(place_series, 0, group) for group in range(2)]}
    beside |= {9: [functools.partial(place_series, 0, group) for group in range(2, 4)]}
    beside |= {10: [functools.partial(pack, 0)]}
    beside[10] += [functools.partial(place_series, 1, group) for group in range(4)]
    beside |= {11: [functools.partial(pack, 1)]}
    for owner, (_, steps) in zip(owners, PARTS):
        row_owners(owner, steps)
    depth, flow = depth_in[...], flow_in[...]
    below = bed_below + below_of(depth)
    for substep in range(STEPS):
        depth, flow, below = river_turn(substep, depth, flow, below)
        for work in beside.get(substep, []):
            work()
    depth_end[...] = depth
    finished = pltpu.make_async_copy(depth_end, depth_out, arrivals.at[15])
    finished.start()
    for group in range(4):
        place_series(2, group)
    pack(2)
    return finished


def reach_of(field):
    return STEPS - 1 - field if field < STEPS else HALO


def turn(value, lanes):
    lanes %= value.shape[1]
    return value if lanes == 0 else pltpu.roll(value, lanes, 1)


ROW_AT = [sum(reach_of(f) for f in range(field)) for field in range(FIELDS + 1)]
ROWS_SENT = -(-ROW_AT[FIELDS] // 8) * 8


def add_in_chunks(arrived, row_labels, column_labels, owner, places, lhs, rhs):
    row_owners(owner, STEPS)
    row_owners(places, 1)
    groups = arrived.shape[0] // SENT

    def place_of(label, part):
        return label == places[part : part + TALL]

    def place(chunk):
        for s in range(chunk, chunk + CHUNK):
            lanes = slice(s * LANES, (s + 1) * LANES)
            lay_out(arrived, s * SENT, 1, STEPS, row_labels[s : s + 1], owner, lhs, lanes)
            one_hot_columns(column_labels[s : s + 1], place_of, rhs, lanes)

    both = jnp.zeros((lhs.shape[0], WIDE), f32)
    place(0)
    for chunk in range(0, groups, CHUNK):
        if chunk + CHUNK < groups:
            place(chunk + CHUNK)
        lanes = slice(chunk * LANES, (chunk + CHUNK) * LANES)
        both = both + lax.dot_general(
            lhs[:, lanes], rhs[:, lanes], (((1,), (1,)), ((), ())), preferred_element_type=f32
        )
    half = lhs.shape[0] // 2
    return both[:half] + both[half:]


def edge_kernel(arrived, sea, odd, sea_out, *refs):
    owner, places, row_labels, column_labels, lhs, rhs, sums = refs
    first_of_pair = lax.axis_index("river") % 2 == 0
    groups = arrived.shape[0] // SENT
    tile_rows, tile_cols = sea.shape[0] // 4, sea.shape[1]
    sea_out[...] = sea[...]

    cells = arrived[pl.ds(STEPS, groups, stride=SENT)].astype(i32)
    row, column = split_label(cells, tile_cols)
    row = row - jnp.where(first_of_pair, 0, tile_rows - HALO)
    upper = jnp.where(row >= HALO // 2, 1, 0)
    inside = (row >= 0) & (row < HALO)
    row_labels[...] = jnp.where(inside, row - upper * (HALO // 2), WIDE - 1).astype(f32)
    column_labels[...] = (column + upper * tile_cols).astype(f32)
    total = add_in_chunks(arrived, row_labels, column_labels, owner, places, lhs, rhs)
    high_rows = total.shape[0]
    for half in range(2):
        part = slice(half * high_rows, (half + 1) * high_rows)
        sums[part] = total[:, half * LANES : (half + 1) * LANES]

    def put(field, start, end):
        reach = reach_of(field)
        if reach:
            last, first = end[end.shape[0] - reach :], start[:reach]
            part = slice(ROW_AT[field], ROW_AT[field] + reach)
            odd[part] = jnp.where(first_of_pair, first, last)

    odd[ROWS_SENT - 8 :] = jnp.zeros((8, LANES), f32)
    for step in range(STEPS):
        halves = [
            sums[pl.ds(half * high_rows + step, HALO // 2, stride=STEPS)] for half in range(2)
        ]
        rows = jnp.concatenate(halves, axis=0)
        put(step, rows, rows)
    for number in range(4):
        value = sea[number * tile_rows : (number + 1) * tile_rows]
        put(STEPS + number, value, value)


def source_kernel(arrived, sea, fields, even, rhs, label_out, *refs):
    owner, places, column_labels, lhs, sums = refs
    first_of_pair = lax.axis_index("river") % 2 == 0
    groups = arrived.shape[0] // SENT
    tile_rows, tile_cols = sea.shape[0] // 4, sea.shape[1]

    cells = arrived[pl.ds(STEPS, groups, stride=SENT)].astype(i32)
    row, column = cell_labels(cells, tile_cols)
    label_out[...] = row.astype(f32)
    column_labels[...] = column.astype(f32)
    total = add_in_chunks(arrived, label_out, column_labels, owner, places, lhs, rhs)
    high_rows = total.shape[0]
    for half in range(2):
        part = slice(half * high_rows, (half + 1) * high_rows)
        sums[part] = total[:, half * LANES : (half + 1) * LANES]

    def put(field, value):
        fields[field * tile_rows : (field + 1) * tile_rows] = value
        reach = reach_of(field)
        if reach:
            last, first = value[tile_rows - reach :], value[:reach]
            part = slice(ROW_AT[field], ROW_AT[field] + reach)
            even[part] = jnp.where(first_of_pair, last, first)

    even[ROWS_SENT - 8 :] = jnp.zeros((8, LANES), f32)
    for step in range(STEPS):
        halves = [sums[pl.ds(half * high_rows + step, TALL, stride=STEPS)] for half in range(2)]
        put(step, jnp.concatenate(halves, axis=0))
    for number in range(4):
        put(STEPS + number, sea[number * tile_rows : (number + 1) * tile_rows])


def strip_kernel(fields, from_odd, from_even, tall, odd, even):
    upper = lax.axis_index("river") % 2 == 0
    first_of_pair = lax.axis_index("coast") % 2 == 0
    from_before = jnp.where(upper, from_odd[...], from_even[...])
    from_after = jnp.where(upper, from_even[...], from_odd[...])
    tile_rows = fields.shape[0] // FIELDS
    height = tall.shape[0] // FIELDS
    lane = lax.broadcasted_iota(i32, (height, LANES), 1)
    ends = jnp.zeros((height, LANES), f32)
    starts = jnp.zeros((height, LANES), f32)
    for field in range(FIELDS):
        reach, at = reach_of(field), ROW_AT[field]
        parts = [fields[field * tile_rows : (field + 1) * tile_rows]]
        if reach:
            parts.append(from_after[at : at + reach])
        if reach < HALO:
            parts.append(jnp.zeros((2 * HALO - 2 * reach, LANES), f32))
        if reach:
            parts.append(from_before[at : at + reach])
        value = jnp.concatenate(parts, axis=0)
        tall[field * height : (field + 1) * height] = value
        if reach:
            here = (lane >= at) & (lane < at + reach)
            ends = jnp.where(here, turn(value, at + reach - LANES), ends)
            starts = jnp.where(here, turn(value, at), starts)
    odd[...] = jnp.where(first_of_pair, starts, ends)
    even[...] = jnp.where(first_of_pair, ends, starts)


def ocean_kernel(
    tile_rows, tall, from_odd, from_even, row_labels, hot, level_out, replies, history, level_end, departure
):
    height = tall.shape[0] // FIELDS
    width = 2 * LANES
    river, coast = lax.axis_index("river"), lax.axis_index("coast")
    rivers, coasts = lax.axis_size("river"), lax.axis_size("coast")
    lane = lax.broadcasted_iota(i32, (height, LANES), 1)
    from_left = jnp.where(coast % 2 == 0, from_odd[...], from_even[...])
    from_right = jnp.where(coast % 2 == 0, from_even[...], from_odd[...])

    def whole(field):
        reach, at = reach_of(field), ROW_AT[field]
        beside = jnp.zeros((height, LANES), f32)
        if reach:
            beside = jnp.where(lane < reach, turn(from_right, -at), beside)
            beside = jnp.where(lane >= LANES - reach, turn(from_left, -at - reach), beside)
        return jnp.concatenate([tall[field * height : (field + 1) * height], beside], axis=1)

    level, bed, east, north = [whole(STEPS + number) for number in range(4)]

    row = lax.broadcasted_iota(i32, (height, width), 0)
    column = lax.broadcasted_iota(i32, (height, width), 1)
    row_in = jnp.where(
        row < tile_rows, 1, jnp.where(row < tile_rows + HALO, (river < rivers - 1).astype(i32), (river > 0).astype(i32))
    )
    column_in = jnp.where(
        column < LANES, 1, jnp.where(column < LANES + LANES // 2, (coast < coasts - 1).astype(i32), (coast > 0).astype(i32))
    )
    inside = row_in * column_in == 1

    def next_row(value):
        return pltpu.roll(value, height - 1, 0)

    def next_column(value):
        return pltpu.roll(value, width - 1, 1)

    bed_east = jnp.maximum(bed, next_row(bed))
    bed_north = jnp.maximum(bed, next_column(bed))
    drive = gravity * step_seconds / cell_metres

    def ocean_turn(first, steps, step, level, east, north):
        source = whole(step) * (step_seconds / (cell_metres * cell_metres))
        east = flow_after(east, level, next_row(level), bed_east, drive, ocean_manning)
        north = flow_after(north, level, next_column(level), bed_north, drive, ocean_manning)
        spread = east - pltpu.roll(east, 1, 0) + north - pltpu.roll(north, 1, 1)
        level = level - step_seconds / cell_metres * spread + source
        level = jnp.where(inside, level, 0.0)
        for half in range(2):
            part = level[half * TALL : (half + 1) * TALL, :LANES]
            at = TALL * (2 * first + half * steps) + step - first
            history[pl.ds(at, TALL, stride=steps)] = part
        return level, east, north

    def table_of(first, steps):
        high_rows, at = TALL * steps, 2 * TALL * first
        halves = [history[at + half * high_rows : at + (half + 1) * high_rows] for half in range(2)]
        return jnp.concatenate(in_two(jnp.concatenate(halves, axis=1)), axis=0)

    def reply(table, first, steps, group, of):
        count = replies.shape[0] // STEPS // of
        for s in range(group * count, (group + 1) * count, 2):
            rows = jnp.concatenate([row_labels[s : s + 1], row_labels[s + 1 : s + 2]], axis=1)
            found = look_up(table, rows, hot[:, s * LANES : (s + 2) * LANES], steps)
            for half in range(2):
                at = (s + half) * STEPS + first
                replies[at : at + steps] = found[:, half * LANES : (half + 1) * LANES]

    waiting = []
    for part, (first, steps) in enumerate(LOOKED_UP):
        for step in range(first, first + steps):
            level, east, north = ocean_turn(first, steps, step, level, east, north)
            if waiting:
                reply(*waiting, step - first, steps)
        if part == len(LOOKED_UP) - 1:
            level_end[...] = level[:tile_rows, :LANES]
            finished = pltpu.make_async_copy(level_end, level_out, departure)
            finished.start()
        waiting = [table_of(first, steps), first, steps]
    reply(*waiting, 0, 1)
    finished.wait()


def column_kernel(address, _, hot, labels):
    place = lax.broadcasted_iota(i32, (TALL, 2 * LANES), 0).astype(f32).astype(bf16)

    def place_of(label, part):
        return label - part == place

    for i in range(0, address.shape[0], 2):
        pair = jnp.concatenate([address[i : i + 1], address[i + 1 : i + 2]], axis=1)
        high, low = [label.astype(f32) for label in split_label(pair, WIDE)]
        one_hot_columns(low, place_of, hot, slice(i * LANES, (i + 2) * LANES))
        labels[i // 2 : i // 2 + 1] = high


def mouth_kernel(returned, hot, labels, level_out, whole, series, block, departures):
    rows = hot.shape[1] // LANES
    groups = LANES // MPB
    lane = lax.broadcasted_iota(i32, (rows, LANES), 1)
    copies = []
    for first, steps in LOOKED_UP:
        for row in range(TALL):
            for half in range(2):
                at = (2 * row + half) * STEPS + first
                to = first * TALL + row * steps
                lanes = slice(half * LANES, (half + 1) * LANES)
                whole[to : to + steps, lanes] = returned[at : at + steps]
        own = whole[first * TALL : (first + steps) * TALL]
        table = jnp.concatenate(in_two(own), axis=0)
        for i in range(0, rows, 2):
            lanes = slice(i * LANES, (i + 2) * LANES)
            found = look_up(table, labels[i // 2 : i // 2 + 1], hot[:, lanes], steps)
            series[pl.ds(first * rows + i, steps, stride=rows)] = found[:, :LANES]
            series[pl.ds(first * rows + i + 1, steps, stride=rows)] = found[:, LANES:]
        for number in range(first // groups, (first + steps) // groups):
            for g in range(groups):
                result = jnp.zeros((rows, LANES), f32)
                for place in range(groups):
                    at = (number * groups + place) * rows
                    part = turn(series[at : at + rows], (place - g) * MPB)
                    result = jnp.where(lane // MPB == place, part, result)
                block[number, g * rows : (g + 1) * rows] = result
            to = level_out.at[:, pl.ds(number * LANES, LANES)]
            copies.append(pltpu.make_async_copy(block.at[number], to, departures.at[number]))
            copies[-1].start()
    for copy in copies:
        copy.wait()


def shape(*dims, dtype=f32):
    return jax.ShapeDtypeStruct(dims, dtype)


def cost(products):
    return pl.CostEstimate(flops=2 * products, bytes_accessed=8 << 20, transcendentals=0)


def in_hbm(*arrays):
    return [pltpu.with_memory_space_constraint(whole, pltpu.HBM) for whole in arrays]


def swap(values, tall, devices, capacity):
    per = LANES // capacity
    if per > 1:
        values = values.reshape(devices // per, tall, per, capacity).transpose(0, 2, 1, 3)
    values = values.reshape(devices, 1, tall * capacity)
    values = lax.all_to_all(values, ("coast", "river"), split_axis=0, concat_axis=0, tiled=True)
    if per > 1:
        values = values.reshape(devices // per, per, tall, capacity).transpose(0, 2, 1, 3)
    return values.reshape(devices // per * tall, LANES)


def with_neighbour(value, axis, start):
    pairs = range(start, lax.axis_size(axis) - 1, 2)
    return lax.ppermute(value, axis, [(i + k, i + 1 - k) for i in pairs for k in range(2)])


def per_device(
    reach_depth,
    reach_flow,
    reach_bed,
    reach_width,
    reach_length,
    runoff,
    flows_into,
    mouth_prev,
    mouth_tile,
    mouth_cell,
    sea_level,
    sea_bed,
    wet_mask,
    flux_east,
    flux_north,
):
    devices = lax.axis_size("river") * lax.axis_size("coast")
    blocks = reach_depth.shape[0]
    tile_rows, tile_cols = sea_level.shape
    mouths = blocks * MPB
    capacity = max(2, 2 * mouths // devices)
    groups = devices * capacity // LANES
    rows = mouths // LANES
    height = tile_rows + 2 * HALO

    depth_after, sending, address, sea = pl.pallas_call(
        functools.partial(river_kernel, devices, lax.axis_size("coast"), capacity),
        name="river",
        out_shape=(
            shape(blocks, RB),
            shape(groups * SENT, LANES),
            shape(rows, LANES, dtype=i32),
            shape(4 * tile_rows, tile_cols),
        ),
        in_specs=[pl.BlockSpec(memory_space=pltpu.HBM)] * 15,
        out_specs=(
            pl.BlockSpec(memory_space=pltpu.HBM),
            pl.BlockSpec(memory_space=pltpu.VMEM),
            pl.BlockSpec(memory_space=pltpu.VMEM),
            pl.BlockSpec(memory_space=pltpu.VMEM),
        ),
        scratch_shapes=[pltpu.VMEM((blocks, RB), f32)] * 6
        + [
            pltpu.VMEM((blocks, RB), i32),
            pltpu.VMEM((MPB, blocks), f32),
            pltpu.VMEM((MPB, blocks), i32),
            pltpu.VMEM((MPB, blocks), i32),
            pltpu.VMEM((tile_rows, tile_cols), f32),
            pltpu.VMEM((tile_rows, tile_cols), f32),
            pltpu.VMEM((tile_rows, tile_cols), i32),
            pltpu.VMEM((tile_rows, tile_cols), f32),
            pltpu.VMEM((tile_rows, tile_cols), f32),
            pltpu.SemaphoreType.DMA((16,)),
            pltpu.VMEM((blocks, RB), f32),
            pltpu.VMEM((reach_offsets, blocks, RB), f32),
            pltpu.VMEM((SENT * rows, LANES), f32),
            pltpu.VMEM((RB, LANES), f32),
            pltpu.VMEM((rows, LANES), i32),
            pltpu.VMEM((rows * devices, LANES), bf16),
            pltpu.VMEM((rows * devices, 2 * LANES), f32),
            pltpu.VMEM((rows, LANES), f32),
            pltpu.VMEM((LANES, rows), f32),
            pltpu.VMEM((mouths, WIDE), bf16),
            *[pltpu.VMEM((TALL * steps, LANES), bf16) for _, steps in PARTS],
            *[
                pltpu.VMEM((2 * TALL * (steps + (first == 0)), mouths), bf16)
                for first, steps in PARTS
            ],
        ],
        compiler_params=PARAMS,
    )(
        *in_hbm(
            reach_depth,
            reach_flow,
            reach_bed,
            reach_width,
            reach_length,
            runoff,
            flows_into,
            mouth_prev.T,
            mouth_tile[:, :, 0].T,
            mouth_cell.T,
            sea_level,
            sea_bed,
            wet_mask,
            flux_east,
            flux_north,
        )
    )
    arrived = swap(sending, SENT, devices, capacity)

    edge_rows = -(-HALO // 2 * STEPS // TALL) * TALL
    odd, sea = pl.pallas_call(
        edge_kernel,
        name="edges",
        out_shape=(shape(ROWS_SENT, LANES), shape(4 * tile_rows, tile_cols)),
        scratch_shapes=[
            pltpu.VMEM((edge_rows, LANES), bf16),
            pltpu.VMEM((WIDE, LANES), bf16),
            pltpu.VMEM((groups, LANES), f32),
            pltpu.VMEM((groups, LANES), f32),
            pltpu.VMEM((2 * edge_rows, groups * LANES), bf16),
            pltpu.VMEM((WIDE, groups * LANES), bf16),
            pltpu.VMEM((2 * edge_rows, LANES), f32),
        ],
        cost_estimate=cost(2 * edge_rows * WIDE * groups * LANES),
        compiler_params=PARAMS,
    )(arrived, sea)
    from_odd = with_neighbour(odd, "river", 1)

    fields, even, hot, labels = pl.pallas_call(
        source_kernel,
        name="sources",
        out_shape=(
            shape(FIELDS * tile_rows, LANES),
            shape(ROWS_SENT, LANES),
            shape(WIDE, groups * LANES, dtype=bf16),
            shape(groups, LANES),
        ),
        scratch_shapes=[
            pltpu.VMEM((TALL * STEPS, LANES), bf16),
            pltpu.VMEM((WIDE, LANES), bf16),
            pltpu.VMEM((groups, LANES), f32),
            pltpu.VMEM((2 * TALL * STEPS, groups * LANES), bf16),
            pltpu.VMEM((2 * TALL * STEPS, LANES), f32),
        ],
        cost_estimate=cost(2 * TALL * STEPS * WIDE * groups * LANES),
        compiler_params=PARAMS,
    )(arrived, sea)
    from_even = with_neighbour(even, "river", 0)

    slot_hot, slot_labels = pl.pallas_call(
        column_kernel,
        name="columns",
        out_shape=(shape(WIDE, mouths, dtype=bf16), shape(rows // 2, 2 * LANES)),
        in_specs=[
            pl.BlockSpec(memory_space=pltpu.VMEM),
            pl.BlockSpec(memory_space=pl.ANY),
        ],
        cost_estimate=cost(WIDE * mouths * LANES),
        compiler_params=PARAMS,
    )(address, labels)

    tall, odd, even = pl.pallas_call(
        strip_kernel,
        name="strips",
        out_shape=(shape(FIELDS * height, LANES), shape(height, LANES), shape(height, LANES)),
        compiler_params=PARAMS,
    )(fields, from_odd, from_even)
    from_odd, from_even = with_neighbour(odd, "coast", 1), with_neighbour(even, "coast", 0)

    level_after, replies = pl.pallas_call(
        functools.partial(ocean_kernel, tile_rows),
        name="ocean",
        out_shape=(shape(tile_rows, tile_cols), shape(groups * STEPS, LANES)),
        scratch_shapes=[
            pltpu.VMEM((2 * TALL * STEPS, LANES), f32),
            pltpu.VMEM((tile_rows, tile_cols), f32),
            pltpu.SemaphoreType.DMA,
        ],
        out_specs=(
            pl.BlockSpec(memory_space=pltpu.HBM),
            pl.BlockSpec(memory_space=pltpu.VMEM),
        ),
        compiler_params=PARAMS,
    )(tall, from_odd, from_even, labels, hot)
    returned = swap(replies, STEPS, devices, capacity)

    mouth_level = pl.pallas_call(
        mouth_kernel,
        name="mouths",
        out_shape=shape(blocks, STEPS * MPB),
        scratch_shapes=[
            pltpu.VMEM((TALL * STEPS, WIDE), f32),
            pltpu.VMEM((STEPS * rows, LANES), f32),
            pltpu.VMEM((STEPS * MPB // LANES, blocks, LANES), f32),
            pltpu.SemaphoreType.DMA((STEPS * MPB // LANES,)),
        ],
        out_specs=pl.BlockSpec(memory_space=pltpu.HBM),
        compiler_params=PARAMS,
    )(returned, slot_hot, slot_labels)
    return (depth_after, level_after, mouth_level)


def solution(mesh):
    by_block = P(("river", "coast"), None)
    tiled = P("river", "coast")
    return jax.shard_map(
        per_device,
        mesh=mesh,
        in_specs=(by_block,) * 8
        + (P(("river", "coast"), None, None), by_block)
        + (tiled,) * 5,
        out_specs=(by_block, tiled, by_block),
        check_vma=False,
    )
```

```python
import functools
import math

import jax
import jax.numpy as jnp
from jax import lax
from jax.experimental import pallas as pl
from jax.experimental.pallas import tpu as pltpu
from jax.sharding import PartitionSpec as P

RB = 128
MPB = 32
STEPS = 12

gravity = 9.81
step_seconds = 300.0
cell_metres = 3000.0
river_manning = 0.035
ocean_manning = 0.025
depth_floor = 0.05
reach_offsets = 16

LANES = 128
SENT = 13
TALL = 16
WIDE = 256
PARTS = ((0, 8), (8, 2), (10, 2))
LOOKED_UP = ((0, 8), (8, 4))
CHUNK = 8
HALO = 12
FIELDS = 16
f32, bf16, i32 = jnp.float32, jnp.bfloat16, jnp.int32

PARAMS = pltpu.CompilerParams(vmem_limit_bytes=40 * 1024 * 1024)


def flow_after(unit_flow, upper, lower, bed_top, drive, manning):
    face_depth = jnp.maximum(upper, lower) - bed_top
    driving = drive * jnp.maximum(face_depth, 0.0) * (upper - lower)
    power = -7.0 / 3.0 * math.log2(math.e)
    thin = jnp.exp2(jnp.log(jnp.maximum(face_depth, depth_floor)) * power)
    friction = (gravity * step_seconds * manning * manning) * jnp.abs(unit_flow) * thin
    divisor = 1.0 + friction
    inverse = pl.reciprocal(divisor, approx=True)
    return ((unit_flow + driving) * inverse) * (2.0 - divisor * inverse)


def in_two(values):
    high = values.astype(bf16)
    return high, (values - high.astype(f32)).astype(bf16)


def small(labels):
    return jnp.broadcast_to(labels, (TALL, labels.shape[1])).astype(bf16)


def one_hot_columns(columns, place_of, rhs, lanes):
    labels = small(columns)
    one, none = jnp.ones(labels.shape, bf16), jnp.zeros(labels.shape, bf16)
    for part in range(0, WIDE, TALL):
        hit = place_of(labels, part)
        rhs[part : part + TALL, lanes] = jnp.where(hit, one, none)


def row_owners(owner, steps):
    for part in range(0, owner.shape[0], TALL):
        number = part + lax.broadcasted_iota(i32, (TALL, LANES), 0)
        owner[part : part + TALL] = (number // steps).astype(f32).astype(bf16)


def in_turn(series, at, stride, steps, first):
    parts, row = [], first
    while row < first + 8:
        step = row % steps
        count = min(steps - step, first + 8 - row)
        parts.append(series[pl.ds(at + step * stride, count, stride=stride)])
        row += count
    return parts[0] if len(parts) == 1 else jnp.concatenate(parts, axis=0)


def lay_out(series, at, stride, steps, rows, owner, lhs, lanes):
    turns = math.lcm(steps, 8) // 8
    cycle = [in_turn(series, at, stride, steps, 8 * turn) for turn in range(turns)]
    pairs = [(cycle[2 * k % turns], cycle[(2 * k + 1) % turns]) for k in range(turns)]
    halves = [in_two(jnp.concatenate(pair, axis=0)) for pair in pairs]
    labels = small(rows)
    none = jnp.zeros(labels.shape, bf16)
    high_rows = owner.shape[0]
    for part in range(0, high_rows, TALL):
        hit = labels == owner[part : part + TALL]
        for number, half in enumerate(halves[part // TALL % turns]):
            at_rows = slice(number * high_rows + part, number * high_rows + part + TALL)
            lhs[at_rows, lanes] = jnp.where(hit, half, none)


def look_up(table, rows, hot, steps):
    found = jnp.dot(table, hot, preferred_element_type=f32)
    per = 2 if steps > 6 else 4
    several = (per * steps, rows.shape[1])
    number = (lax.broadcasted_iota(i32, several, 0) // steps).astype(f32)
    labels = jnp.broadcast_to(rows, several) - number
    total = jnp.zeros(several, f32)
    for row in range(0, TALL, per):
        high = found[row * steps : (row + per) * steps]
        low = found[(TALL + row) * steps : (TALL + row + per) * steps]
        total = total + jnp.where(labels == row, high + low, 0.0)
    result = total[:steps]
    for number in range(1, per):
        result = result + total[number * steps : (number + 1) * steps]
    return result


def split_label(number, size):
    return lax.shift_right_logical(number, size.bit_length() - 1), number & (size - 1)


def cell_labels(cells, tile_cols):
    row, column = split_label(cells, tile_cols)
    upper, row = split_label(row, TALL)
    return row, upper * tile_cols + column


def river_kernel(
    devices,
    coasts,
    capacity,
    *refs,
):
    inputs, (depth_out, send_out, address_out, sea_out), refs = refs[:15], refs[15:19], refs[19:]
    arrivals = refs[15]
    copies = [
        pltpu.make_async_copy(whole, own, arrivals.at[number])
        for number, (whole, own) in enumerate(zip(inputs, refs[:15]))
    ]
    copies, of_sea = copies[:10], copies[10:]
    for copy in copies[::-1] + of_sea:
        copy.start()
    outputs = (depth_out, send_out, address_out)
    finished = river_steps(
        devices, coasts, capacity, copies, *refs[:10], *outputs, arrivals, *refs[16:]
    )

    sea_level, sea_bed, wet_mask, flux_east, flux_north = refs[10:15]
    tile_rows = sea_level.shape[0]
    for copy in of_sea:
        copy.wait()
    bed = sea_bed[...]
    level = jnp.where(wet_mask[...] == 1, jnp.maximum(sea_level[...], bed), bed)
    for number, value in enumerate((level, bed, flux_east[...], flux_north[...])):
        sea_out[number * tile_rows : (number + 1) * tile_rows] = value
    finished.wait()


def river_steps(
    devices,
    coasts,
    capacity,
    copies,
    depth_in,
    flow_in,
    bed_in,
    width_in,
    length_in,
    runoff_in,
    into_in,
    prev_in,
    tile_in,
    cell_in,
    depth_out,
    send_out,
    address_out,
    arrivals,
    depth_end,
    enters,
    series,
    turned,
    tiles,
    hots,
    counted,
    high_labels,
    low_labels,
    rhs,
    *parts,
):
    owners, slots = parts[: len(PARTS)], parts[len(PARTS) :]
    blocks = depth_in.shape[0]
    groups = LANES // MPB
    rows = blocks // groups
    inland = RB - MPB
    lane = lax.broadcasted_iota(i32, (blocks, RB), 1)

    for copy in copies:
        copy.wait()

    turned[...] = jnp.zeros_like(turned)
    turned[0:MPB, 0:blocks] = tile_in[...].astype(f32)
    turned[MPB : 2 * MPB, 0:blocks] = cell_in[...].astype(f32)
    turned[inland:RB, 0:blocks] = prev_in[...]
    mouths = jnp.transpose(turned[...])[0:blocks]
    prev = mouths

    def grouped(array, first):
        lanes16 = lax.broadcasted_iota(i32, (rows, LANES), 1)
        result = jnp.zeros((rows, LANES), f32)
        for g in range(groups):
            part = array[g * rows : (g + 1) * rows]
            shift = (g * MPB - first) % LANES
            part = part if shift == 0 else pltpu.roll(part, shift, 1)
            result = jnp.where(lanes16 // MPB == g, part, result)
        return result

    tile = grouped(mouths, 0).astype(i32)
    tiles[...] = tile % coasts * (devices // coasts) + tile // coasts
    series[STEPS * rows :] = grouped(mouths, MPB)

    into = into_in[...]
    at_mouth = lane >= inland
    down = jnp.where(at_mouth, 0, into)
    offset = jnp.where(at_mouth, 0, into - lane)
    bed = bed_in[...]

    sources = [(down - 4 * a) & (RB - 1) for a in range(reach_offsets // 4)]

    def below_of(value, a=0):
        return jnp.take_along_axis(value, sources[a], axis=1, mode="promise_in_bounds")

    bed_below = below_of(bed)
    bed_top = jnp.where(at_mouth, bed, jnp.maximum(bed, bed_below))
    drive = gravity * step_seconds / length_in[...]
    width = width_in[...]
    area = step_seconds / (width * length_in[...])
    gain = area * runoff_in[...]
    loss = area * width
    moved = [(turn(offset, 1 + b), turn(width, 1 + b)) for b in range(4)]
    for o in range(reach_offsets):
        where_to, its_width = moved[o % 4]
        weight = its_width * turn(area, -(o - o % 4))
        enters[o] = jnp.where(where_to == o + 1, weight, 0.0)

    def river_turn(substep, depth, flow, below):
        below = jnp.where(at_mouth, prev, below)
        flow = flow_after(flow, bed + depth, below, bed_top, drive, river_manning)
        moved = [turn(flow, 1 + b) for b in range(4)]
        sums = []
        for a in range(0, reach_offsets, 4):
            one, other = [
                enters[a + b] * moved[b] + enters[a + b + 1] * moved[b + 1] for b in (0, 2)
            ]
            sums.append(one + other)
        sums[0] = sums[0] + (depth + gain - loss * flow)
        depth, below = [
            (places[0] + places[1]) + (places[2] + places[3])
            for places in (
                [turn(value, 4 * a) for a, value in enumerate(sums)],
                [below_of(value, a) for a, value in enumerate(sums)],
            )
        ]
        series[substep * rows : (substep + 1) * rows] = grouped(flow * width, inland)
        return depth, flow, bed_below + below

    def count_mouths():
        for i in range(rows):
            names = jnp.broadcast_to(tiles[i : i + 1], (devices, LANES))
            hit = names == lax.broadcasted_iota(i32, (devices, LANES), 0)
            hots[i * devices : (i + 1) * devices] = jnp.where(hit, 1.0, 0.0).astype(bf16)
        shape = (LANES, 2 * LANES)
        earlier = lax.broadcasted_iota(i32, shape, 0) < lax.broadcasted_iota(i32, shape, 1)
        counted[...] = jnp.dot(
            hots[...], jnp.where(earlier, 1.0, 0.0).astype(bf16), preferred_element_type=f32
        )

    def rank_mouths():
        before = jnp.zeros((devices, LANES), f32)
        for i in range(rows):
            part = slice(i * devices, (i + 1) * devices)
            ranks = (counted[part, :LANES] + before) * hots[part].astype(f32)
            rank = jnp.sum(ranks, axis=0, keepdims=True).astype(i32)
            address_out[i : i + 1] = tiles[i : i + 1] * capacity + rank
            before = before + counted[part, LANES:]

    one, none = jnp.ones((LANES, LANES), bf16), jnp.zeros((LANES, LANES), bf16)
    number = lax.broadcasted_iota(i32, (TALL, LANES), 0).astype(f32)

    def label_mouths():
        high, low = split_label(address_out[...], WIDE)
        high_labels[...] = high.astype(f32)
        low_labels[...] = jnp.transpose(low.astype(f32))

    def slot_columns(group):
        place = lax.broadcasted_iota(i32, (LANES, LANES), 1).astype(f32).astype(bf16)
        for i in range(group * rows // 4, (group + 1) * rows // 4):
            lanes = slice(i * LANES, (i + 1) * LANES)
            column = jnp.broadcast_to(low_labels[:, i : i + 1], (LANES, LANES)).astype(bf16)
            for half in range(2):
                hit = column - half * LANES == place
                rhs[lanes, half * LANES : (half + 1) * LANES] = jnp.where(hit, one, none)

    def place_series(part, group):
        first, steps = PARTS[part]
        owner, lhs = owners[part], slots[part]
        for i in range(group * rows // 4, (group + 1) * rows // 4):
            lanes = slice(i * LANES, (i + 1) * LANES)
            labels = high_labels[i : i + 1]
            lay_out(series, first * rows + i, rows, steps, labels, owner, lhs, lanes)
            if part == 0:
                cells = series[STEPS * rows + i : STEPS * rows + i + 1]
                cells = jnp.where(number == labels, cells, 0.0)
                for half, value in enumerate(in_two(cells)):
                    at = 2 * TALL * steps + half * TALL
                    lhs[at : at + TALL, lanes] = value

    def pack(part):
        first, steps = PARTS[part]
        high_rows = TALL * steps
        lhs = slots[part]
        both = jnp.dot(lhs[...], rhs[...], preferred_element_type=f32)
        packed = both[:high_rows] + both[high_rows : 2 * high_rows]
        for half in range(2):
            lanes = slice(half * LANES, (half + 1) * LANES)
            for row in range(TALL):
                at = (2 * row + half) * SENT + first
                send_out[at : at + steps] = packed[row * steps : (row + 1) * steps, lanes]
            if part == 0:
                cells = both[2 * high_rows : 2 * high_rows + TALL] + both[2 * high_rows + TALL :]
                send_out[pl.ds(half * SENT + STEPS, TALL, stride=2 * SENT)] = cells[:, lanes]

    beside = {0: [count_mouths], 1: [rank_mouths], 2: [label_mouths]}
    beside |= {3 + group: [functools.partial(slot_columns, group)] for group in range(4)}
    beside |= {8: [functools.partial(place_series, 0, group) for group in range(2)]}
    beside |= {9: [functools.partial(place_series, 0, group) for group in range(2, 4)]}
    beside |= {10: [functools.partial(pack, 0)]}
    beside[10] += [functools.partial(place_series, 1, group) for group in range(4)]
    beside |= {11: [functools.partial(pack, 1)]}
    for owner, (_, steps) in zip(owners, PARTS):
        row_owners(owner, steps)
    depth, flow = depth_in[...], flow_in[...]
    below = bed_below + below_of(depth)
    for substep in range(STEPS):
        depth, flow, below = river_turn(substep, depth, flow, below)
        for work in beside.get(substep, []):
            work()
    depth_end[...] = depth
    finished = pltpu.make_async_copy(depth_end, depth_out, arrivals.at[15])
    finished.start()
    for group in range(4):
        place_series(2, group)
    pack(2)
    return finished


def reach_of(field):
    return STEPS - 1 - field if field < STEPS else HALO


def turn(value, lanes):
    lanes %= value.shape[1]
    return value if lanes == 0 else pltpu.roll(value, lanes, 1)


ROW_AT = [sum(reach_of(f) for f in range(field)) for field in range(FIELDS + 1)]
ROWS_SENT = -(-ROW_AT[FIELDS] // 8) * 8


def add_in_chunks(arrived, row_labels, column_labels, owner, places, lhs, rhs):
    row_owners(owner, STEPS)
    row_owners(places, 1)
    groups = arrived.shape[0] // SENT

    def place_of(label, part):
        return label == places[part : part + TALL]

    def place(chunk):
        for s in range(chunk, chunk + CHUNK):
            lanes = slice(s * LANES, (s + 1) * LANES)
            lay_out(arrived, s * SENT, 1, STEPS, row_labels[s : s + 1], owner, lhs, lanes)
            one_hot_columns(column_labels[s : s + 1], place_of, rhs, lanes)

    both = jnp.zeros((lhs.shape[0], WIDE), f32)
    place(0)
    for chunk in range(0, groups, CHUNK):
        if chunk + CHUNK < groups:
            place(chunk + CHUNK)
        lanes = slice(chunk * LANES, (chunk + CHUNK) * LANES)
        both = both + lax.dot_general(
            lhs[:, lanes], rhs[:, lanes], (((1,), (1,)), ((), ())), preferred_element_type=f32
        )
    half = lhs.shape[0] // 2
    return both[:half] + both[half:]


def source_kernel(arrived, sea, fields, odd, even, rhs, label_out, *refs):
    owner, places, column_labels, lhs, sums = refs
    first_of_pair = lax.axis_index("river") % 2 == 0
    groups = arrived.shape[0] // SENT
    tile_rows, tile_cols = sea.shape[0] // 4, sea.shape[1]

    cells = arrived[pl.ds(STEPS, groups, stride=SENT)].astype(i32)
    row, column = cell_labels(cells, tile_cols)
    label_out[...] = row.astype(f32)
    column_labels[...] = column.astype(f32)
    total = add_in_chunks(arrived, label_out, column_labels, owner, places, lhs, rhs)
    high_rows = total.shape[0]
    for half in range(2):
        part = slice(half * high_rows, (half + 1) * high_rows)
        sums[part] = total[:, half * LANES : (half + 1) * LANES]

    def put(field, value):
        fields[field * tile_rows : (field + 1) * tile_rows] = value
        reach = reach_of(field)
        if reach:
            last, first = value[tile_rows - reach :], value[:reach]
            part = slice(ROW_AT[field], ROW_AT[field] + reach)
            odd[part] = jnp.where(first_of_pair, first, last)
            even[part] = jnp.where(first_of_pair, last, first)

    for message in (odd, even):
        message[ROWS_SENT - 8 :] = jnp.zeros((8, LANES), f32)
    for step in range(STEPS):
        halves = [sums[pl.ds(half * high_rows + step, TALL, stride=STEPS)] for half in range(2)]
        put(step, jnp.concatenate(halves, axis=0))
    for number in range(4):
        put(STEPS + number, sea[number * tile_rows : (number + 1) * tile_rows])


def strip_kernel(fields, from_odd, from_even, tall, odd, even):
    upper = lax.axis_index("river") % 2 == 0
    first_of_pair = lax.axis_index("coast") % 2 == 0
    from_before = jnp.where(upper, from_odd[...], from_even[...])
    from_after = jnp.where(upper, from_even[...], from_odd[...])
    tile_rows = fields.shape[0] // FIELDS
    height = tall.shape[0] // FIELDS
    lane = lax.broadcasted_iota(i32, (height, LANES), 1)
    ends = jnp.zeros((height, LANES), f32)
    starts = jnp.zeros((height, LANES), f32)
    for field in range(FIELDS):
        reach, at = reach_of(field), ROW_AT[field]
        parts = [fields[field * tile_rows : (field + 1) * tile_rows]]
        if reach:
            parts.append(from_after[at : at + reach])
        if reach < HALO:
            parts.append(jnp.zeros((2 * HALO - 2 * reach, LANES), f32))
        if reach:
            parts.append(from_before[at : at + reach])
        value = jnp.concatenate(parts, axis=0)
        tall[field * height : (field + 1) * height] = value
        if reach:
            here = (lane >= at) & (lane < at + reach)
            ends = jnp.where(here, turn(value, at + reach - LANES), ends)
            starts = jnp.where(here, turn(value, at), starts)
    odd[...] = jnp.where(first_of_pair, starts, ends)
    even[...] = jnp.where(first_of_pair, ends, starts)


def ocean_kernel(
    tile_rows, tall, from_odd, from_even, row_labels, hot, level_out, replies, history, level_end, departure
):
    height = tall.shape[0] // FIELDS
    width = 2 * LANES
    river, coast = lax.axis_index("river"), lax.axis_index("coast")
    rivers, coasts = lax.axis_size("river"), lax.axis_size("coast")
    lane = lax.broadcasted_iota(i32, (height, LANES), 1)
    from_left = jnp.where(coast % 2 == 0, from_odd[...], from_even[...])
    from_right = jnp.where(coast % 2 == 0, from_even[...], from_odd[...])

    def whole(field):
        reach, at = reach_of(field), ROW_AT[field]
        beside = jnp.zeros((height, LANES), f32)
        if reach:
            beside = jnp.where(lane < reach, turn(from_right, -at), beside)
            beside = jnp.where(lane >= LANES - reach, turn(from_left, -at - reach), beside)
        return jnp.concatenate([tall[field * height : (field + 1) * height], beside], axis=1)

    level, bed, east, north = [whole(STEPS + number) for number in range(4)]

    row = lax.broadcasted_iota(i32, (height, width), 0)
    column = lax.broadcasted_iota(i32, (height, width), 1)
    row_in = jnp.where(
        row < tile_rows, 1, jnp.where(row < tile_rows + HALO, (river < rivers - 1).astype(i32), (river > 0).astype(i32))
    )
    column_in = jnp.where(
        column < LANES, 1, jnp.where(column < LANES + LANES // 2, (coast < coasts - 1).astype(i32), (coast > 0).astype(i32))
    )
    inside = row_in * column_in == 1

    def next_row(value):
        return pltpu.roll(value, height - 1, 0)

    def next_column(value):
        return pltpu.roll(value, width - 1, 1)

    bed_east = jnp.maximum(bed, next_row(bed))
    bed_north = jnp.maximum(bed, next_column(bed))
    drive = gravity * step_seconds / cell_metres

    def ocean_turn(first, steps, step, level, east, north):
        source = whole(step) * (step_seconds / (cell_metres * cell_metres))
        east = flow_after(east, level, next_row(level), bed_east, drive, ocean_manning)
        north = flow_after(north, level, next_column(level), bed_north, drive, ocean_manning)
        spread = east - pltpu.roll(east, 1, 0) + north - pltpu.roll(north, 1, 1)
        level = level - step_seconds / cell_metres * spread + source
        level = jnp.where(inside, level, 0.0)
        for half in range(2):
            part = level[half * TALL : (half + 1) * TALL, :LANES]
            at = TALL * (2 * first + half * steps) + step - first
            history[pl.ds(at, TALL, stride=steps)] = part
        return level, east, north

    def table_of(first, steps):
        high_rows, at = TALL * steps, 2 * TALL * first
        halves = [history[at + half * high_rows : at + (half + 1) * high_rows] for half in range(2)]
        return jnp.concatenate(in_two(jnp.concatenate(halves, axis=1)), axis=0)

    def reply(table, first, steps, group, of):
        count = replies.shape[0] // STEPS // of
        for s in range(group * count, (group + 1) * count, 2):
            rows = jnp.concatenate([row_labels[s : s + 1], row_labels[s + 1 : s + 2]], axis=1)
            found = look_up(table, rows, hot[:, s * LANES : (s + 2) * LANES], steps)
            for half in range(2):
                at = (s + half) * STEPS + first
                replies[at : at + steps] = found[:, half * LANES : (half + 1) * LANES]

    waiting = []
    for part, (first, steps) in enumerate(LOOKED_UP):
        for step in range(first, first + steps):
            level, east, north = ocean_turn(first, steps, step, level, east, north)
            if waiting:
                reply(*waiting, step - first, steps)
        if part == len(LOOKED_UP) - 1:
            level_end[...] = level[:tile_rows, :LANES]
            finished = pltpu.make_async_copy(level_end, level_out, departure)
            finished.start()
        waiting = [table_of(first, steps), first, steps]
    reply(*waiting, 0, 1)
    finished.wait()


def mouth_kernel(returned, address, level_out, whole, series, hot, block, departures):
    rows = address.shape[0]
    groups = LANES // MPB
    place = lax.broadcasted_iota(i32, (TALL, 2 * LANES), 0).astype(f32).astype(bf16)

    def place_of(label, part):
        return label - part == place

    labels = []
    for i in range(0, rows, 2):
        pair = jnp.concatenate([address[i : i + 1], address[i + 1 : i + 2]], axis=1)
        high, low = [label.astype(f32) for label in split_label(pair, WIDE)]
        one_hot_columns(low, place_of, hot, slice(i * LANES, (i + 2) * LANES))
        labels.append(high)
    lane = lax.broadcasted_iota(i32, (rows, LANES), 1)
    copies = []
    for first, steps in LOOKED_UP:
        for row in range(TALL):
            for half in range(2):
                at = (2 * row + half) * STEPS + first
                to = first * TALL + row * steps
                lanes = slice(half * LANES, (half + 1) * LANES)
                whole[to : to + steps, lanes] = returned[at : at + steps]
        own = whole[first * TALL : (first + steps) * TALL]
        table = jnp.concatenate(in_two(own), axis=0)
        for i in range(0, rows, 2):
            lanes = slice(i * LANES, (i + 2) * LANES)
            found = look_up(table, labels[i // 2], hot[:, lanes], steps)
            series[pl.ds(first * rows + i, steps, stride=rows)] = found[:, :LANES]
            series[pl.ds(first * rows + i + 1, steps, stride=rows)] = found[:, LANES:]
        for number in range(first // groups, (first + steps) // groups):
            for g in range(groups):
                result = jnp.zeros((rows, LANES), f32)
                for place in range(groups):
                    at = (number * groups + place) * rows
                    part = turn(series[at : at + rows], (place - g) * MPB)
                    result = jnp.where(lane // MPB == place, part, result)
                block[number, g * rows : (g + 1) * rows] = result
            to = level_out.at[:, pl.ds(number * LANES, LANES)]
            copies.append(pltpu.make_async_copy(block.at[number], to, departures.at[number]))
            copies[-1].start()
    for copy in copies:
        copy.wait()


def shape(*dims, dtype=f32):
    return jax.ShapeDtypeStruct(dims, dtype)


def in_hbm(*arrays):
    return [pltpu.with_memory_space_constraint(whole, pltpu.HBM) for whole in arrays]


def swap(values, tall, devices, capacity):
    per = LANES // capacity
    if per > 1:
        values = values.reshape(devices // per, tall, per, capacity).transpose(0, 2, 1, 3)
    values = values.reshape(devices, 1, tall * capacity)
    values = lax.all_to_all(values, ("coast", "river"), split_axis=0, concat_axis=0, tiled=True)
    if per > 1:
        values = values.reshape(devices // per, per, tall, capacity).transpose(0, 2, 1, 3)
    return values.reshape(devices // per * tall, LANES)


def with_neighbour(value, axis, start):
    pairs = range(start, lax.axis_size(axis) - 1, 2)
    return lax.ppermute(value, axis, [(i + k, i + 1 - k) for i in pairs for k in range(2)])


def per_device(
    reach_depth,
    reach_flow,
    reach_bed,
    reach_width,
    reach_length,
    runoff,
    flows_into,
    mouth_prev,
    mouth_tile,
    mouth_cell,
    sea_level,
    sea_bed,
    wet_mask,
    flux_east,
    flux_north,
):
    devices = lax.axis_size("river") * lax.axis_size("coast")
    blocks = reach_depth.shape[0]
    tile_rows, tile_cols = sea_level.shape
    mouths = blocks * MPB
    capacity = max(2, 2 * mouths // devices)
    groups = devices * capacity // LANES
    rows = mouths // LANES
    height = tile_rows + 2 * HALO

    depth_after, sending, address, sea = pl.pallas_call(
        functools.partial(river_kernel, devices, lax.axis_size("coast"), capacity),
        name="river",
        out_shape=(
            shape(blocks, RB),
            shape(groups * SENT, LANES),
            shape(rows, LANES, dtype=i32),
            shape(4 * tile_rows, tile_cols),
        ),
        in_specs=[pl.BlockSpec(memory_space=pltpu.HBM)] * 15,
        out_specs=(
            pl.BlockSpec(memory_space=pltpu.HBM),
            pl.BlockSpec(memory_space=pltpu.VMEM),
            pl.BlockSpec(memory_space=pltpu.VMEM),
            pl.BlockSpec(memory_space=pltpu.VMEM),
        ),
        scratch_shapes=[pltpu.VMEM((blocks, RB), f32)] * 6
        + [
            pltpu.VMEM((blocks, RB), i32),
            pltpu.VMEM((MPB, blocks), f32),
            pltpu.VMEM((MPB, blocks), i32),
            pltpu.VMEM((MPB, blocks), i32),
            pltpu.VMEM((tile_rows, tile_cols), f32),
            pltpu.VMEM((tile_rows, tile_cols), f32),
            pltpu.VMEM((tile_rows, tile_cols), i32),
            pltpu.VMEM((tile_rows, tile_cols), f32),
            pltpu.VMEM((tile_rows, tile_cols), f32),
            pltpu.SemaphoreType.DMA((16,)),
            pltpu.VMEM((blocks, RB), f32),
            pltpu.VMEM((reach_offsets, blocks, RB), f32),
            pltpu.VMEM((SENT * rows, LANES), f32),
            pltpu.VMEM((RB, LANES), f32),
            pltpu.VMEM((rows, LANES), i32),
            pltpu.VMEM((rows * devices, LANES), bf16),
            pltpu.VMEM((rows * devices, 2 * LANES), f32),
            pltpu.VMEM((rows, LANES), f32),
            pltpu.VMEM((LANES, rows), f32),
            pltpu.VMEM((mouths, WIDE), bf16),
            *[pltpu.VMEM((TALL * steps, LANES), bf16) for _, steps in PARTS],
            *[
                pltpu.VMEM((2 * TALL * (steps + (first == 0)), mouths), bf16)
                for first, steps in PARTS
            ],
        ],
        compiler_params=PARAMS,
    )(
        *in_hbm(
            reach_depth,
            reach_flow,
            reach_bed,
            reach_width,
            reach_length,
            runoff,
            flows_into,
            mouth_prev.T,
            mouth_tile[:, :, 0].T,
            mouth_cell.T,
            sea_level,
            sea_bed,
            wet_mask,
            flux_east,
            flux_north,
        )
    )
    arrived = swap(sending, SENT, devices, capacity)

    fields, odd, even, hot, labels = pl.pallas_call(
        source_kernel,
        name="sources",
        out_shape=(
            shape(FIELDS * tile_rows, LANES),
            shape(ROWS_SENT, LANES),
            shape(ROWS_SENT, LANES),
            shape(WIDE, groups * LANES, dtype=bf16),
            shape(groups, LANES),
        ),
        scratch_shapes=[
            pltpu.VMEM((TALL * STEPS, LANES), bf16),
            pltpu.VMEM((WIDE, LANES), bf16),
            pltpu.VMEM((groups, LANES), f32),
            pltpu.VMEM((2 * TALL * STEPS, groups * LANES), bf16),
            pltpu.VMEM((2 * TALL * STEPS, LANES), f32),
        ],
        compiler_params=PARAMS,
    )(arrived, sea)
    from_odd, from_even = with_neighbour(odd, "river", 1), with_neighbour(even, "river", 0)

    tall, odd, even = pl.pallas_call(
        strip_kernel,
        name="strips",
        out_shape=(shape(FIELDS * height, LANES), shape(height, LANES), shape(height, LANES)),
        compiler_params=PARAMS,
    )(fields, from_odd, from_even)
    from_odd, from_even = with_neighbour(odd, "coast", 1), with_neighbour(even, "coast", 0)

    level_after, replies = pl.pallas_call(
        functools.partial(ocean_kernel, tile_rows),
        name="ocean",
        out_shape=(shape(tile_rows, tile_cols), shape(groups * STEPS, LANES)),
        scratch_shapes=[
            pltpu.VMEM((2 * TALL * STEPS, LANES), f32),
            pltpu.VMEM((tile_rows, tile_cols), f32),
            pltpu.SemaphoreType.DMA,
        ],
        out_specs=(
            pl.BlockSpec(memory_space=pltpu.HBM),
            pl.BlockSpec(memory_space=pltpu.VMEM),
        ),
        compiler_params=PARAMS,
    )(tall, from_odd, from_even, labels, hot)
    returned = swap(replies, STEPS, devices, capacity)

    mouth_level = pl.pallas_call(
        mouth_kernel,
        name="mouths",
        out_shape=shape(blocks, STEPS * MPB),
        scratch_shapes=[
            pltpu.VMEM((TALL * STEPS, WIDE), f32),
            pltpu.VMEM((STEPS * rows, LANES), f32),
            pltpu.VMEM((WIDE, mouths), bf16),
            pltpu.VMEM((STEPS * MPB // LANES, blocks, LANES), f32),
            pltpu.SemaphoreType.DMA((STEPS * MPB // LANES,)),
        ],
        out_specs=pl.BlockSpec(memory_space=pltpu.HBM),
        compiler_params=PARAMS,
    )(returned, address)
    return (depth_after, level_after, mouth_level)


def solution(mesh):
    by_block = P(("river", "coast"), None)
    tiled = P("river", "coast")
    return jax.shard_map(
        per_device,
        mesh=mesh,
        in_specs=(by_block,) * 8
        + (P(("river", "coast"), None, None), by_block)
        + (tiled,) * 5,
        out_specs=(by_block, tiled, by_block),
        check_vma=False,
    )
```

```python
import functools
import math

import jax
import jax.numpy as jnp
from jax import lax
from jax.experimental import pallas as pl
from jax.experimental.pallas import tpu as pltpu
from jax.sharding import PartitionSpec as P

RB = 128
MPB = 32
STEPS = 12

gravity = 9.81
step_seconds = 300.0
cell_metres = 3000.0
river_manning = 0.035
ocean_manning = 0.025
depth_floor = 0.05
reach_offsets = 16

LANES = 128
SENT = 13
TALL = 16
WIDE = 256
PARTS = ((0, 8), (8, 2), (10, 2))
LOOKED_UP = ((0, 8), (8, 4))
CHUNK = 4
HALO = 12
FIELDS = 16
f32, bf16, i32 = jnp.float32, jnp.bfloat16, jnp.int32

PARAMS = pltpu.CompilerParams(vmem_limit_bytes=40 * 1024 * 1024)


def flow_after(unit_flow, upper, lower, bed_top, drive, manning):
    face_depth = jnp.maximum(upper, lower) - bed_top
    driving = drive * jnp.maximum(face_depth, 0.0) * (upper - lower)
    power = -7.0 / 3.0 * math.log2(math.e)
    thin = jnp.exp2(jnp.log(jnp.maximum(face_depth, depth_floor)) * power)
    friction = (gravity * step_seconds * manning * manning) * jnp.abs(unit_flow) * thin
    divisor = 1.0 + friction
    inverse = pl.reciprocal(divisor, approx=True)
    return ((unit_flow + driving) * inverse) * (2.0 - divisor * inverse)


def in_two(values):
    high = values.astype(bf16)
    return high, (values - high.astype(f32)).astype(bf16)


def small(labels):
    return jnp.broadcast_to(labels, (TALL, labels.shape[1])).astype(bf16)


def one_hot_columns(columns, place_of, rhs, lanes):
    labels = small(columns)
    one, none = jnp.ones(labels.shape, bf16), jnp.zeros(labels.shape, bf16)
    for part in range(0, WIDE, TALL):
        hit = place_of(labels, part)
        rhs[part : part + TALL, lanes] = jnp.where(hit, one, none)


def row_owners(owner, steps):
    for part in range(0, owner.shape[0], TALL):
        number = part + lax.broadcasted_iota(i32, (TALL, LANES), 0)
        owner[part : part + TALL] = (number // steps).astype(f32).astype(bf16)


def in_turn(series, at, stride, steps, first):
    parts, row = [], first
    while row < first + 8:
        step = row % steps
        count = min(steps - step, first + 8 - row)
        parts.append(series[pl.ds(at + step * stride, count, stride=stride)])
        row += count
    return parts[0] if len(parts) == 1 else jnp.concatenate(parts, axis=0)


def lay_out(series, at, stride, steps, rows, owner, lhs, lanes):
    turns = math.lcm(steps, 8) // 8
    cycle = [in_turn(series, at, stride, steps, 8 * turn) for turn in range(turns)]
    pairs = [(cycle[2 * k % turns], cycle[(2 * k + 1) % turns]) for k in range(turns)]
    halves = [in_two(jnp.concatenate(pair, axis=0)) for pair in pairs]
    labels = small(rows)
    none = jnp.zeros(labels.shape, bf16)
    high_rows = owner.shape[0]
    for part in range(0, high_rows, TALL):
        hit = labels == owner[part : part + TALL]
        for number, half in enumerate(halves[part // TALL % turns]):
            at_rows = slice(number * high_rows + part, number * high_rows + part + TALL)
            lhs[at_rows, lanes] = jnp.where(hit, half, none)


def look_up(table, rows, hot, steps):
    found = jnp.dot(table, hot, preferred_element_type=f32)
    per = 2 if steps > 6 else 4
    several = (per * steps, rows.shape[1])
    number = (lax.broadcasted_iota(i32, several, 0) // steps).astype(f32)
    labels = jnp.broadcast_to(rows, several) - number
    total = jnp.zeros(several, f32)
    for row in range(0, TALL, per):
        high = found[row * steps : (row + per) * steps]
        low = found[(TALL + row) * steps : (TALL + row + per) * steps]
        total = total + jnp.where(labels == row, high + low, 0.0)
    result = total[:steps]
    for number in range(1, per):
        result = result + total[number * steps : (number + 1) * steps]
    return result


def split_label(number, size):
    return lax.shift_right_logical(number, size.bit_length() - 1), number & (size - 1)


def cell_labels(cells, tile_cols):
    row, column = split_label(cells, tile_cols)
    upper, row = split_label(row, TALL)
    return row, upper * tile_cols + column


def river_kernel(
    devices,
    coasts,
    capacity,
    *refs,
):
    inputs, (depth_out, send_out, address_out, sea_out), refs = refs[:15], refs[15:19], refs[19:]
    arrivals = refs[15]
    copies = [
        pltpu.make_async_copy(whole, own, arrivals.at[number])
        for number, (whole, own) in enumerate(zip(inputs, refs[:15]))
    ]
    copies, of_sea = copies[:10], copies[10:]
    for copy in copies[::-1] + of_sea:
        copy.start()
    outputs = (depth_out, send_out, address_out)
    finished = river_steps(
        devices, coasts, capacity, copies, *refs[:10], *outputs, arrivals, *refs[16:]
    )

    sea_level, sea_bed, wet_mask, flux_east, flux_north = refs[10:15]
    tile_rows = sea_level.shape[0]
    for copy in of_sea:
        copy.wait()
    bed = sea_bed[...]
    level = jnp.where(wet_mask[...] == 1, jnp.maximum(sea_level[...], bed), bed)
    for number, value in enumerate((level, bed, flux_east[...], flux_north[...])):
        sea_out[number * tile_rows : (number + 1) * tile_rows] = value
    finished.wait()


def river_steps(
    devices,
    coasts,
    capacity,
    copies,
    depth_in,
    flow_in,
    bed_in,
    width_in,
    length_in,
    runoff_in,
    into_in,
    prev_in,
    tile_in,
    cell_in,
    depth_out,
    send_out,
    address_out,
    arrivals,
    depth_end,
    enters,
    series,
    turned,
    tiles,
    hots,
    counted,
    high_labels,
    low_labels,
    rhs,
    *parts,
):
    owners, slots = parts[: len(PARTS)], parts[len(PARTS) :]
    blocks = depth_in.shape[0]
    groups = LANES // MPB
    rows = blocks // groups
    inland = RB - MPB
    lane = lax.broadcasted_iota(i32, (blocks, RB), 1)

    for copy in copies:
        copy.wait()

    turned[...] = jnp.zeros_like(turned)
    turned[0:MPB, 0:blocks] = tile_in[...].astype(f32)
    turned[MPB : 2 * MPB, 0:blocks] = cell_in[...].astype(f32)
    turned[inland:RB, 0:blocks] = prev_in[...]
    mouths = jnp.transpose(turned[...])[0:blocks]
    prev = mouths

    def grouped(array, first):
        lanes16 = lax.broadcasted_iota(i32, (rows, LANES), 1)
        result = jnp.zeros((rows, LANES), f32)
        for g in range(groups):
            part = array[g * rows : (g + 1) * rows]
            shift = (g * MPB - first) % LANES
            part = part if shift == 0 else pltpu.roll(part, shift, 1)
            result = jnp.where(lanes16 // MPB == g, part, result)
        return result

    tile = grouped(mouths, 0).astype(i32)
    tiles[...] = tile % coasts * (devices // coasts) + tile // coasts
    series[STEPS * rows :] = grouped(mouths, MPB)

    into = into_in[...]
    at_mouth = lane >= inland
    down = jnp.where(at_mouth, 0, into)
    offset = jnp.where(at_mouth, 0, into - lane)
    bed = bed_in[...]

    sources = [(down - 4 * a) & (RB - 1) for a in range(reach_offsets // 4)]

    def below_of(value, a=0):
        return jnp.take_along_axis(value, sources[a], axis=1, mode="promise_in_bounds")

    bed_below = below_of(bed)
    bed_top = jnp.where(at_mouth, bed, jnp.maximum(bed, bed_below))
    drive = gravity * step_seconds / length_in[...]
    width = width_in[...]
    area = step_seconds / (width * length_in[...])
    gain = area * runoff_in[...]
    loss = area * width
    moved = [(turn(offset, 1 + b), turn(width, 1 + b)) for b in range(4)]
    for o in range(reach_offsets):
        where_to, its_width = moved[o % 4]
        weight = its_width * turn(area, -(o - o % 4))
        enters[o] = jnp.where(where_to == o + 1, weight, 0.0)

    def river_turn(substep, depth, flow, below):
        below = jnp.where(at_mouth, prev, below)
        flow = flow_after(flow, bed + depth, below, bed_top, drive, river_manning)
        moved = [turn(flow, 1 + b) for b in range(4)]
        sums = []
        for a in range(0, reach_offsets, 4):
            one, other = [
                enters[a + b] * moved[b] + enters[a + b + 1] * moved[b + 1] for b in (0, 2)
            ]
            sums.append(one + other)
        sums[0] = sums[0] + (depth + gain - loss * flow)
        depth, below = [
            (places[0] + places[1]) + (places[2] + places[3])
            for places in (
                [turn(value, 4 * a) for a, value in enumerate(sums)],
                [below_of(value, a) for a, value in enumerate(sums)],
            )
        ]
        series[substep * rows : (substep + 1) * rows] = grouped(flow * width, inland)
        return depth, flow, bed_below + below

    def count_mouths():
        for i in range(rows):
            names = jnp.broadcast_to(tiles[i : i + 1], (devices, LANES))
            hit = names == lax.broadcasted_iota(i32, (devices, LANES), 0)
            hots[i * devices : (i + 1) * devices] = jnp.where(hit, 1.0, 0.0).astype(bf16)
        shape = (LANES, 2 * LANES)
        earlier = lax.broadcasted_iota(i32, shape, 0) < lax.broadcasted_iota(i32, shape, 1)
        counted[...] = jnp.dot(
            hots[...], jnp.where(earlier, 1.0, 0.0).astype(bf16), preferred_element_type=f32
        )

    def rank_mouths():
        before = jnp.zeros((devices, LANES), f32)
        for i in range(rows):
            part = slice(i * devices, (i + 1) * devices)
            ranks = (counted[part, :LANES] + before) * hots[part].astype(f32)
            rank = jnp.sum(ranks, axis=0, keepdims=True).astype(i32)
            address_out[i : i + 1] = tiles[i : i + 1] * capacity + rank
            before = before + counted[part, LANES:]

    one, none = jnp.ones((LANES, LANES), bf16), jnp.zeros((LANES, LANES), bf16)
    number = lax.broadcasted_iota(i32, (TALL, LANES), 0).astype(f32)

    def label_mouths():
        high, low = split_label(address_out[...], WIDE)
        high_labels[...] = high.astype(f32)
        low_labels[...] = jnp.transpose(low.astype(f32))

    def slot_columns(group):
        place = lax.broadcasted_iota(i32, (LANES, LANES), 1).astype(f32).astype(bf16)
        for i in range(group * rows // 4, (group + 1) * rows // 4):
            lanes = slice(i * LANES, (i + 1) * LANES)
            column = jnp.broadcast_to(low_labels[:, i : i + 1], (LANES, LANES)).astype(bf16)
            for half in range(2):
                hit = column - half * LANES == place
                rhs[lanes, half * LANES : (half + 1) * LANES] = jnp.where(hit, one, none)

    def place_series(part, group):
        first, steps = PARTS[part]
        owner, lhs = owners[part], slots[part]
        for i in range(group * rows // 4, (group + 1) * rows // 4):
            lanes = slice(i * LANES, (i + 1) * LANES)
            labels = high_labels[i : i + 1]
            lay_out(series, first * rows + i, rows, steps, labels, owner, lhs, lanes)
            if part == 0:
                cells = series[STEPS * rows + i : STEPS * rows + i + 1]
                cells = jnp.where(number == labels, cells, 0.0)
                for half, value in enumerate(in_two(cells)):
                    at = 2 * TALL * steps + half * TALL
                    lhs[at : at + TALL, lanes] = value

    def pack(part):
        first, steps = PARTS[part]
        high_rows = TALL * steps
        lhs = slots[part]
        both = jnp.dot(lhs[...], rhs[...], preferred_element_type=f32)
        packed = both[:high_rows] + both[high_rows : 2 * high_rows]
        for half in range(2):
            lanes = slice(half * LANES, (half + 1) * LANES)
            for row in range(TALL):
                at = (2 * row + half) * SENT + first
                send_out[at : at + steps] = packed[row * steps : (row + 1) * steps, lanes]
            if part == 0:
                cells = both[2 * high_rows : 2 * high_rows + TALL] + both[2 * high_rows + TALL :]
                send_out[pl.ds(half * SENT + STEPS, TALL, stride=2 * SENT)] = cells[:, lanes]

    beside = {0: [count_mouths], 1: [rank_mouths], 2: [label_mouths]}
    beside |= {3 + group: [functools.partial(slot_columns, group)] for group in range(4)}
    beside |= {8: [functools.partial(place_series, 0, group) for group in range(2)]}
    beside |= {9: [functools.partial(place_series, 0, group) for group in range(2, 4)]}
    beside |= {10: [functools.partial(pack, 0)]}
    beside[10] += [functools.partial(place_series, 1, group) for group in range(4)]
    beside |= {11: [functools.partial(pack, 1)]}
    for owner, (_, steps) in zip(owners, PARTS):
        row_owners(owner, steps)
    depth, flow = depth_in[...], flow_in[...]
    below = bed_below + below_of(depth)
    for substep in range(STEPS):
        depth, flow, below = river_turn(substep, depth, flow, below)
        for work in beside.get(substep, []):
            work()
    depth_end[...] = depth
    finished = pltpu.make_async_copy(depth_end, depth_out, arrivals.at[15])
    finished.start()
    for group in range(4):
        place_series(2, group)
    pack(2)
    return finished


def reach_of(field):
    return STEPS - 1 - field if field < STEPS else HALO


def turn(value, lanes):
    lanes %= value.shape[1]
    return value if lanes == 0 else pltpu.roll(value, lanes, 1)


ROW_AT = [sum(reach_of(f) for f in range(field)) for field in range(FIELDS + 1)]
ROWS_SENT = -(-ROW_AT[FIELDS] // 8) * 8


def add_in_chunks(arrived, row_labels, column_labels, owner, places, lhs, rhs):
    row_owners(owner, STEPS)
    row_owners(places, 1)
    groups = arrived.shape[0] // SENT

    def place_of(label, part):
        return label == places[part : part + TALL]

    def place(chunk):
        for s in range(chunk, chunk + CHUNK):
            lanes = slice(s * LANES, (s + 1) * LANES)
            lay_out(arrived, s * SENT, 1, STEPS, row_labels[s : s + 1], owner, lhs, lanes)
            one_hot_columns(column_labels[s : s + 1], place_of, rhs, lanes)

    both = jnp.zeros((lhs.shape[0], WIDE), f32)
    place(0)
    for chunk in range(0, groups, CHUNK):
        if chunk + CHUNK < groups:
            place(chunk + CHUNK)
        lanes = slice(chunk * LANES, (chunk + CHUNK) * LANES)
        both = both + lax.dot_general(
            lhs[:, lanes], rhs[:, lanes], (((1,), (1,)), ((), ())), preferred_element_type=f32
        )
    half = lhs.shape[0] // 2
    return both[:half] + both[half:]


def edge_kernel(arrived, sea, odd, sea_out, *refs):
    owner, places, row_labels, column_labels, lhs, rhs, sums = refs
    first_of_pair = lax.axis_index("river") % 2 == 0
    groups = arrived.shape[0] // SENT
    tile_rows, tile_cols = sea.shape[0] // 4, sea.shape[1]
    sea_out[...] = sea[...]

    cells = arrived[pl.ds(STEPS, groups, stride=SENT)].astype(i32)
    row, column = split_label(cells, tile_cols)
    row = row - jnp.where(first_of_pair, 0, tile_rows - HALO)
    upper = jnp.where(row >= HALO // 2, 1, 0)
    inside = (row >= 0) & (row < HALO)
    row_labels[...] = jnp.where(inside, row - upper * (HALO // 2), WIDE - 1).astype(f32)
    column_labels[...] = (column + upper * tile_cols).astype(f32)
    total = add_in_chunks(arrived, row_labels, column_labels, owner, places, lhs, rhs)
    high_rows = total.shape[0]
    for half in range(2):
        part = slice(half * high_rows, (half + 1) * high_rows)
        sums[part] = total[:, half * LANES : (half + 1) * LANES]

    def put(field, start, end):
        reach = reach_of(field)
        if reach:
            last, first = end[end.shape[0] - reach :], start[:reach]
            part = slice(ROW_AT[field], ROW_AT[field] + reach)
            odd[part] = jnp.where(first_of_pair, first, last)

    odd[ROWS_SENT - 8 :] = jnp.zeros((8, LANES), f32)
    for step in range(STEPS):
        halves = [
            sums[pl.ds(half * high_rows + step, HALO // 2, stride=STEPS)] for half in range(2)
        ]
        rows = jnp.concatenate(halves, axis=0)
        put(step, rows, rows)
    for number in range(4):
        value = sea[number * tile_rows : (number + 1) * tile_rows]
        put(STEPS + number, value, value)


def source_kernel(arrived, sea, fields, even, rhs, label_out, *refs):
    owner, places, column_labels, lhs, sums = refs
    first_of_pair = lax.axis_index("river") % 2 == 0
    groups = arrived.shape[0] // SENT
    tile_rows, tile_cols = sea.shape[0] // 4, sea.shape[1]

    cells = arrived[pl.ds(STEPS, groups, stride=SENT)].astype(i32)
    row, column = cell_labels(cells, tile_cols)
    label_out[...] = row.astype(f32)
    column_labels[...] = column.astype(f32)
    total = add_in_chunks(arrived, label_out, column_labels, owner, places, lhs, rhs)
    high_rows = total.shape[0]
    for half in range(2):
        part = slice(half * high_rows, (half + 1) * high_rows)
        sums[part] = total[:, half * LANES : (half + 1) * LANES]

    def put(field, value):
        fields[field * tile_rows : (field + 1) * tile_rows] = value
        reach = reach_of(field)
        if reach:
            last, first = value[tile_rows - reach :], value[:reach]
            part = slice(ROW_AT[field], ROW_AT[field] + reach)
            even[part] = jnp.where(first_of_pair, last, first)

    even[ROWS_SENT - 8 :] = jnp.zeros((8, LANES), f32)
    for step in range(STEPS):
        halves = [sums[pl.ds(half * high_rows + step, TALL, stride=STEPS)] for half in range(2)]
        put(step, jnp.concatenate(halves, axis=0))
    for number in range(4):
        put(STEPS + number, sea[number * tile_rows : (number + 1) * tile_rows])


def strip_kernel(fields, from_odd, from_even, tall, odd, even):
    upper = lax.axis_index("river") % 2 == 0
    first_of_pair = lax.axis_index("coast") % 2 == 0
    from_before = jnp.where(upper, from_odd[...], from_even[...])
    from_after = jnp.where(upper, from_even[...], from_odd[...])
    tile_rows = fields.shape[0] // FIELDS
    height = tall.shape[0] // FIELDS
    lane = lax.broadcasted_iota(i32, (height, LANES), 1)
    ends = jnp.zeros((height, LANES), f32)
    starts = jnp.zeros((height, LANES), f32)
    for field in range(FIELDS):
        reach, at = reach_of(field), ROW_AT[field]
        parts = [fields[field * tile_rows : (field + 1) * tile_rows]]
        if reach:
            parts.append(from_after[at : at + reach])
        if reach < HALO:
            parts.append(jnp.zeros((2 * HALO - 2 * reach, LANES), f32))
        if reach:
            parts.append(from_before[at : at + reach])
        value = jnp.concatenate(parts, axis=0)
        tall[field * height : (field + 1) * height] = value
        if reach:
            here = (lane >= at) & (lane < at + reach)
            ends = jnp.where(here, turn(value, at + reach - LANES), ends)
            starts = jnp.where(here, turn(value, at), starts)
    odd[...] = jnp.where(first_of_pair, starts, ends)
    even[...] = jnp.where(first_of_pair, ends, starts)


def ocean_kernel(
    tile_rows, tall, from_odd, from_even, row_labels, hot, level_out, replies, history, level_end, departure
):
    height = tall.shape[0] // FIELDS
    width = 2 * LANES
    river, coast = lax.axis_index("river"), lax.axis_index("coast")
    rivers, coasts = lax.axis_size("river"), lax.axis_size("coast")
    lane = lax.broadcasted_iota(i32, (height, LANES), 1)
    from_left = jnp.where(coast % 2 == 0, from_odd[...], from_even[...])
    from_right = jnp.where(coast % 2 == 0, from_even[...], from_odd[...])

    def whole(field):
        reach, at = reach_of(field), ROW_AT[field]
        beside = jnp.zeros((height, LANES), f32)
        if reach:
            beside = jnp.where(lane < reach, turn(from_right, -at), beside)
            beside = jnp.where(lane >= LANES - reach, turn(from_left, -at - reach), beside)
        return jnp.concatenate([tall[field * height : (field + 1) * height], beside], axis=1)

    level, bed, east, north = [whole(STEPS + number) for number in range(4)]

    row = lax.broadcasted_iota(i32, (height, width), 0)
    column = lax.broadcasted_iota(i32, (height, width), 1)
    row_in = jnp.where(
        row < tile_rows, 1, jnp.where(row < tile_rows + HALO, (river < rivers - 1).astype(i32), (river > 0).astype(i32))
    )
    column_in = jnp.where(
        column < LANES, 1, jnp.where(column < LANES + LANES // 2, (coast < coasts - 1).astype(i32), (coast > 0).astype(i32))
    )
    inside = row_in * column_in == 1

    def next_row(value):
        return pltpu.roll(value, height - 1, 0)

    def next_column(value):
        return pltpu.roll(value, width - 1, 1)

    bed_east = jnp.maximum(bed, next_row(bed))
    bed_north = jnp.maximum(bed, next_column(bed))
    drive = gravity * step_seconds / cell_metres

    def ocean_turn(first, steps, step, level, east, north):
        source = whole(step) * (step_seconds / (cell_metres * cell_metres))
        east = flow_after(east, level, next_row(level), bed_east, drive, ocean_manning)
        north = flow_after(north, level, next_column(level), bed_north, drive, ocean_manning)
        spread = east - pltpu.roll(east, 1, 0) + north - pltpu.roll(north, 1, 1)
        level = level - step_seconds / cell_metres * spread + source
        level = jnp.where(inside, level, 0.0)
        for half in range(2):
            part = level[half * TALL : (half + 1) * TALL, :LANES]
            at = TALL * (2 * first + half * steps) + step - first
            history[pl.ds(at, TALL, stride=steps)] = part
        return level, east, north

    def table_of(first, steps):
        high_rows, at = TALL * steps, 2 * TALL * first
        halves = [history[at + half * high_rows : at + (half + 1) * high_rows] for half in range(2)]
        return jnp.concatenate(in_two(jnp.concatenate(halves, axis=1)), axis=0)

    def reply(table, first, steps, group, of):
        count = replies.shape[0] // STEPS // of
        for s in range(group * count, (group + 1) * count, 2):
            rows = jnp.concatenate([row_labels[s : s + 1], row_labels[s + 1 : s + 2]], axis=1)
            found = look_up(table, rows, hot[:, s * LANES : (s + 2) * LANES], steps)
            for half in range(2):
                at = (s + half) * STEPS + first
                replies[at : at + steps] = found[:, half * LANES : (half + 1) * LANES]

    waiting = []
    for part, (first, steps) in enumerate(LOOKED_UP):
        for step in range(first, first + steps):
            level, east, north = ocean_turn(first, steps, step, level, east, north)
            if waiting:
                reply(*waiting, step - first, steps)
        if part == len(LOOKED_UP) - 1:
            level_end[...] = level[:tile_rows, :LANES]
            finished = pltpu.make_async_copy(level_end, level_out, departure)
            finished.start()
        waiting = [table_of(first, steps), first, steps]
    reply(*waiting, 0, 1)
    finished.wait()


def mouth_kernel(returned, address, level_out, whole, series, hot, block, departures):
    rows = address.shape[0]
    groups = LANES // MPB
    place = lax.broadcasted_iota(i32, (TALL, 2 * LANES), 0).astype(f32).astype(bf16)

    def place_of(label, part):
        return label - part == place

    labels = []
    for i in range(0, rows, 2):
        pair = jnp.concatenate([address[i : i + 1], address[i + 1 : i + 2]], axis=1)
        high, low = [label.astype(f32) for label in split_label(pair, WIDE)]
        one_hot_columns(low, place_of, hot, slice(i * LANES, (i + 2) * LANES))
        labels.append(high)
    lane = lax.broadcasted_iota(i32, (rows, LANES), 1)
    copies = []
    for first, steps in LOOKED_UP:
        for row in range(TALL):
            for half in range(2):
                at = (2 * row + half) * STEPS + first
                to = first * TALL + row * steps
                lanes = slice(half * LANES, (half + 1) * LANES)
                whole[to : to + steps, lanes] = returned[at : at + steps]
        own = whole[first * TALL : (first + steps) * TALL]
        table = jnp.concatenate(in_two(own), axis=0)
        for i in range(0, rows, 2):
            lanes = slice(i * LANES, (i + 2) * LANES)
            found = look_up(table, labels[i // 2], hot[:, lanes], steps)
            series[pl.ds(first * rows + i, steps, stride=rows)] = found[:, :LANES]
            series[pl.ds(first * rows + i + 1, steps, stride=rows)] = found[:, LANES:]
        for number in range(first // groups, (first + steps) // groups):
            for g in range(groups):
                result = jnp.zeros((rows, LANES), f32)
                for place in range(groups):
                    at = (number * groups + place) * rows
                    part = turn(series[at : at + rows], (place - g) * MPB)
                    result = jnp.where(lane // MPB == place, part, result)
                block[number, g * rows : (g + 1) * rows] = result
            to = level_out.at[:, pl.ds(number * LANES, LANES)]
            copies.append(pltpu.make_async_copy(block.at[number], to, departures.at[number]))
            copies[-1].start()
    for copy in copies:
        copy.wait()


def shape(*dims, dtype=f32):
    return jax.ShapeDtypeStruct(dims, dtype)


def cost(products):
    return pl.CostEstimate(flops=2 * products, bytes_accessed=8 << 20, transcendentals=0)


def in_hbm(*arrays):
    return [pltpu.with_memory_space_constraint(whole, pltpu.HBM) for whole in arrays]


def swap(values, tall, devices, capacity):
    per = LANES // capacity
    if per > 1:
        values = values.reshape(devices // per, tall, per, capacity).transpose(0, 2, 1, 3)
    values = values.reshape(devices, 1, tall * capacity)
    values = lax.all_to_all(values, ("coast", "river"), split_axis=0, concat_axis=0, tiled=True)
    if per > 1:
        values = values.reshape(devices // per, per, tall, capacity).transpose(0, 2, 1, 3)
    return values.reshape(devices // per * tall, LANES)


def with_neighbour(value, axis, start):
    pairs = range(start, lax.axis_size(axis) - 1, 2)
    return lax.ppermute(value, axis, [(i + k, i + 1 - k) for i in pairs for k in range(2)])


def per_device(
    reach_depth,
    reach_flow,
    reach_bed,
    reach_width,
    reach_length,
    runoff,
    flows_into,
    mouth_prev,
    mouth_tile,
    mouth_cell,
    sea_level,
    sea_bed,
    wet_mask,
    flux_east,
    flux_north,
):
    devices = lax.axis_size("river") * lax.axis_size("coast")
    blocks = reach_depth.shape[0]
    tile_rows, tile_cols = sea_level.shape
    mouths = blocks * MPB
    capacity = max(2, 2 * mouths // devices)
    groups = devices * capacity // LANES
    rows = mouths // LANES
    height = tile_rows + 2 * HALO

    depth_after, sending, address, sea = pl.pallas_call(
        functools.partial(river_kernel, devices, lax.axis_size("coast"), capacity),
        name="river",
        out_shape=(
            shape(blocks, RB),
            shape(groups * SENT, LANES),
            shape(rows, LANES, dtype=i32),
            shape(4 * tile_rows, tile_cols),
        ),
        in_specs=[pl.BlockSpec(memory_space=pltpu.HBM)] * 15,
        out_specs=(
            pl.BlockSpec(memory_space=pltpu.HBM),
            pl.BlockSpec(memory_space=pltpu.VMEM),
            pl.BlockSpec(memory_space=pltpu.VMEM),
            pl.BlockSpec(memory_space=pltpu.VMEM),
        ),
        scratch_shapes=[pltpu.VMEM((blocks, RB), f32)] * 6
        + [
            pltpu.VMEM((blocks, RB), i32),
            pltpu.VMEM((MPB, blocks), f32),
            pltpu.VMEM((MPB, blocks), i32),
            pltpu.VMEM((MPB, blocks), i32),
            pltpu.VMEM((tile_rows, tile_cols), f32),
            pltpu.VMEM((tile_rows, tile_cols), f32),
            pltpu.VMEM((tile_rows, tile_cols), i32),
            pltpu.VMEM((tile_rows, tile_cols), f32),
            pltpu.VMEM((tile_rows, tile_cols), f32),
            pltpu.SemaphoreType.DMA((16,)),
            pltpu.VMEM((blocks, RB), f32),
            pltpu.VMEM((reach_offsets, blocks, RB), f32),
            pltpu.VMEM((SENT * rows, LANES), f32),
            pltpu.VMEM((RB, LANES), f32),
            pltpu.VMEM((rows, LANES), i32),
            pltpu.VMEM((rows * devices, LANES), bf16),
            pltpu.VMEM((rows * devices, 2 * LANES), f32),
            pltpu.VMEM((rows, LANES), f32),
            pltpu.VMEM((LANES, rows), f32),
            pltpu.VMEM((mouths, WIDE), bf16),
            *[pltpu.VMEM((TALL * steps, LANES), bf16) for _, steps in PARTS],
            *[
                pltpu.VMEM((2 * TALL * (steps + (first == 0)), mouths), bf16)
                for first, steps in PARTS
            ],
        ],
        compiler_params=PARAMS,
    )(
        *in_hbm(
            reach_depth,
            reach_flow,
            reach_bed,
            reach_width,
            reach_length,
            runoff,
            flows_into,
            mouth_prev.T,
            mouth_tile[:, :, 0].T,
            mouth_cell.T,
            sea_level,
            sea_bed,
            wet_mask,
            flux_east,
            flux_north,
        )
    )
    arrived = swap(sending, SENT, devices, capacity)

    edge_rows = -(-HALO // 2 * STEPS // TALL) * TALL
    odd, sea = pl.pallas_call(
        edge_kernel,
        name="edges",
        out_shape=(shape(ROWS_SENT, LANES), shape(4 * tile_rows, tile_cols)),
        scratch_shapes=[
            pltpu.VMEM((edge_rows, LANES), bf16),
            pltpu.VMEM((WIDE, LANES), bf16),
            pltpu.VMEM((groups, LANES), f32),
            pltpu.VMEM((groups, LANES), f32),
            pltpu.VMEM((2 * edge_rows, groups * LANES), bf16),
            pltpu.VMEM((WIDE, groups * LANES), bf16),
            pltpu.VMEM((2 * edge_rows, LANES), f32),
        ],
        cost_estimate=cost(2 * edge_rows * WIDE * groups * LANES),
        compiler_params=PARAMS,
    )(arrived, sea)
    from_odd = with_neighbour(odd, "river", 1)

    fields, even, hot, labels = pl.pallas_call(
        source_kernel,
        name="sources",
        out_shape=(
            shape(FIELDS * tile_rows, LANES),
            shape(ROWS_SENT, LANES),
            shape(WIDE, groups * LANES, dtype=bf16),
            shape(groups, LANES),
        ),
        scratch_shapes=[
            pltpu.VMEM((TALL * STEPS, LANES), bf16),
            pltpu.VMEM((WIDE, LANES), bf16),
            pltpu.VMEM((groups, LANES), f32),
            pltpu.VMEM((2 * TALL * STEPS, groups * LANES), bf16),
            pltpu.VMEM((2 * TALL * STEPS, LANES), f32),
        ],
        cost_estimate=cost(2 * TALL * STEPS * WIDE * groups * LANES),
        compiler_params=PARAMS,
    )(arrived, sea)
    from_even = with_neighbour(even, "river", 0)

    tall, odd, even = pl.pallas_call(
        strip_kernel,
        name="strips",
        out_shape=(shape(FIELDS * height, LANES), shape(height, LANES), shape(height, LANES)),
        compiler_params=PARAMS,
    )(fields, from_odd, from_even)
    from_odd, from_even = with_neighbour(odd, "coast", 1), with_neighbour(even, "coast", 0)

    level_after, replies = pl.pallas_call(
        functools.partial(ocean_kernel, tile_rows),
        name="ocean",
        out_shape=(shape(tile_rows, tile_cols), shape(groups * STEPS, LANES)),
        scratch_shapes=[
            pltpu.VMEM((2 * TALL * STEPS, LANES), f32),
            pltpu.VMEM((tile_rows, tile_cols), f32),
            pltpu.SemaphoreType.DMA,
        ],
        out_specs=(
            pl.BlockSpec(memory_space=pltpu.HBM),
            pl.BlockSpec(memory_space=pltpu.VMEM),
        ),
        compiler_params=PARAMS,
    )(tall, from_odd, from_even, labels, hot)
    returned = swap(replies, STEPS, devices, capacity)

    mouth_level = pl.pallas_call(
        mouth_kernel,
        name="mouths",
        out_shape=shape(blocks, STEPS * MPB),
        scratch_shapes=[
            pltpu.VMEM((TALL * STEPS, WIDE), f32),
            pltpu.VMEM((STEPS * rows, LANES), f32),
            pltpu.VMEM((WIDE, mouths), bf16),
            pltpu.VMEM((STEPS * MPB // LANES, blocks, LANES), f32),
            pltpu.SemaphoreType.DMA((STEPS * MPB // LANES,)),
        ],
        out_specs=pl.BlockSpec(memory_space=pltpu.HBM),
        compiler_params=PARAMS,
    )(returned, address)
    return (depth_after, level_after, mouth_level)


def solution(mesh):
    by_block = P(("river", "coast"), None)
    tiled = P("river", "coast")
    return jax.shard_map(
        per_device,
        mesh=mesh,
        in_specs=(by_block,) * 8
        + (P(("river", "coast"), None, None), by_block)
        + (tiled,) * 5,
        out_specs=(by_block, tiled, by_block),
        check_vma=False,
    )
```

```python
import functools
import math

import jax
import jax.numpy as jnp
from jax import lax
from jax.experimental import pallas as pl
from jax.experimental.pallas import tpu as pltpu
from jax.sharding import PartitionSpec as P

RB = 128
MPB = 32
STEPS = 12

gravity = 9.81
step_seconds = 300.0
cell_metres = 3000.0
river_manning = 0.035
ocean_manning = 0.025
depth_floor = 0.05
reach_offsets = 16

LANES = 128
SENT = 13
TALL = 16
WIDE = 256
PARTS = ((0, 8), (8, 2), (10, 2))
LOOKED_UP = ((0, 8), (8, 4))
CHUNK = 8
HALO = 12
FIELDS = 16
f32, bf16, i32 = jnp.float32, jnp.bfloat16, jnp.int32

PARAMS = pltpu.CompilerParams(vmem_limit_bytes=40 * 1024 * 1024)


def flow_after(unit_flow, upper, lower, bed_top, drive, manning):
    face_depth = jnp.maximum(upper, lower) - bed_top
    driving = drive * jnp.maximum(face_depth, 0.0) * (upper - lower)
    power = -7.0 / 3.0 * math.log2(math.e)
    thin = jnp.exp2(jnp.log(jnp.maximum(face_depth, depth_floor)) * power)
    friction = (gravity * step_seconds * manning * manning) * jnp.abs(unit_flow) * thin
    divisor = 1.0 + friction
    inverse = pl.reciprocal(divisor, approx=True)
    return ((unit_flow + driving) * inverse) * (2.0 - divisor * inverse)


def in_two(values):
    high = values.astype(bf16)
    return high, (values - high.astype(f32)).astype(bf16)


def small(labels):
    return jnp.broadcast_to(labels, (TALL, labels.shape[1])).astype(bf16)


def one_hot_columns(columns, place_of, rhs, lanes):
    labels = small(columns)
    one, none = jnp.ones(labels.shape, bf16), jnp.zeros(labels.shape, bf16)
    for part in range(0, WIDE, TALL):
        hit = place_of(labels, part)
        rhs[part : part + TALL, lanes] = jnp.where(hit, one, none)


def row_owners(owner, steps):
    for part in range(0, owner.shape[0], TALL):
        number = part + lax.broadcasted_iota(i32, (TALL, LANES), 0)
        owner[part : part + TALL] = (number // steps).astype(f32).astype(bf16)


def in_turn(series, at, stride, steps, first):
    parts, row = [], first
    while row < first + 8:
        step = row % steps
        count = min(steps - step, first + 8 - row)
        parts.append(series[pl.ds(at + step * stride, count, stride=stride)])
        row += count
    return parts[0] if len(parts) == 1 else jnp.concatenate(parts, axis=0)


def lay_out(series, at, stride, steps, rows, owner, lhs, lanes):
    turns = math.lcm(steps, 8) // 8
    cycle = [in_turn(series, at, stride, steps, 8 * turn) for turn in range(turns)]
    pairs = [(cycle[2 * k % turns], cycle[(2 * k + 1) % turns]) for k in range(turns)]
    halves = [in_two(jnp.concatenate(pair, axis=0)) for pair in pairs]
    labels = small(rows)
    none = jnp.zeros(labels.shape, bf16)
    high_rows = owner.shape[0]
    for part in range(0, high_rows, TALL):
        hit = labels == owner[part : part + TALL]
        for number, half in enumerate(halves[part // TALL % turns]):
            at_rows = slice(number * high_rows + part, number * high_rows + part + TALL)
            lhs[at_rows, lanes] = jnp.where(hit, half, none)


def look_up(table, rows, hot, steps):
    found = jnp.dot(table, hot, preferred_element_type=f32)
    per = 2 if steps > 6 else 4
    several = (per * steps, rows.shape[1])
    number = (lax.broadcasted_iota(i32, several, 0) // steps).astype(f32)
    labels = jnp.broadcast_to(rows, several) - number
    total = jnp.zeros(several, f32)
    for row in range(0, TALL, per):
        high = found[row * steps : (row + per) * steps]
        low = found[(TALL + row) * steps : (TALL + row + per) * steps]
        total = total + jnp.where(labels == row, high + low, 0.0)
    result = total[:steps]
    for number in range(1, per):
        result = result + total[number * steps : (number + 1) * steps]
    return result


def split_label(number, size):
    return lax.shift_right_logical(number, size.bit_length() - 1), number & (size - 1)


def cell_labels(cells, tile_cols):
    row, column = split_label(cells, tile_cols)
    upper, row = split_label(row, TALL)
    return row, upper * tile_cols + column


def river_kernel(
    devices,
    coasts,
    capacity,
    *refs,
):
    inputs, (depth_out, send_out, address_out, sea_out), refs = refs[:15], refs[15:19], refs[19:]
    arrivals = refs[15]
    copies = [
        pltpu.make_async_copy(whole, own, arrivals.at[number])
        for number, (whole, own) in enumerate(zip(inputs, refs[:15]))
    ]
    copies, of_sea = copies[:10], copies[10:]
    for copy in copies[::-1] + of_sea:
        copy.start()
    outputs = (depth_out, send_out, address_out)
    finished = river_steps(
        devices, coasts, capacity, copies, *refs[:10], *outputs, arrivals, *refs[16:]
    )

    sea_level, sea_bed, wet_mask, flux_east, flux_north = refs[10:15]
    tile_rows = sea_level.shape[0]
    for copy in of_sea:
        copy.wait()
    bed = sea_bed[...]
    level = jnp.where(wet_mask[...] == 1, jnp.maximum(sea_level[...], bed), bed)
    for number, value in enumerate((level, bed, flux_east[...], flux_north[...])):
        sea_out[number * tile_rows : (number + 1) * tile_rows] = value
    finished.wait()


def river_steps(
    devices,
    coasts,
    capacity,
    copies,
    depth_in,
    flow_in,
    bed_in,
    width_in,
    length_in,
    runoff_in,
    into_in,
    prev_in,
    tile_in,
    cell_in,
    depth_out,
    send_out,
    address_out,
    arrivals,
    depth_end,
    enters,
    series,
    turned,
    tiles,
    hots,
    counted,
    high_labels,
    low_labels,
    rhs,
    *parts,
):
    owners, slots = parts[: len(PARTS)], parts[len(PARTS) :]
    blocks = depth_in.shape[0]
    groups = LANES // MPB
    rows = blocks // groups
    inland = RB - MPB
    lane = lax.broadcasted_iota(i32, (blocks, RB), 1)

    for copy in copies:
        copy.wait()

    turned[...] = jnp.zeros_like(turned)
    turned[0:MPB, 0:blocks] = tile_in[...].astype(f32)
    turned[MPB : 2 * MPB, 0:blocks] = cell_in[...].astype(f32)
    turned[inland:RB, 0:blocks] = prev_in[...]
    mouths = jnp.transpose(turned[...])[0:blocks]
    prev = mouths

    def grouped(array, first):
        lanes16 = lax.broadcasted_iota(i32, (rows, LANES), 1)
        result = jnp.zeros((rows, LANES), f32)
        for g in range(groups):
            part = array[g * rows : (g + 1) * rows]
            shift = (g * MPB - first) % LANES
            part = part if shift == 0 else pltpu.roll(part, shift, 1)
            result = jnp.where(lanes16 // MPB == g, part, result)
        return result

    tile = grouped(mouths, 0).astype(i32)
    tiles[...] = tile % coasts * (devices // coasts) + tile // coasts
    series[STEPS * rows :] = grouped(mouths, MPB)

    into = into_in[...]
    at_mouth = lane >= inland
    down = jnp.where(at_mouth, 0, into)
    offset = jnp.where(at_mouth, 0, into - lane)
    bed = bed_in[...]

    sources = [(down - 4 * a) & (RB - 1) for a in range(reach_offsets // 4)]

    def below_of(value, a=0):
        return jnp.take_along_axis(value, sources[a], axis=1, mode="promise_in_bounds")

    bed_below = below_of(bed)
    bed_top = jnp.where(at_mouth, bed, jnp.maximum(bed, bed_below))
    drive = gravity * step_seconds / length_in[...]
    width = width_in[...]
    area = step_seconds / (width * length_in[...])
    gain = area * runoff_in[...]
    loss = area * width
    moved = [(turn(offset, 1 + b), turn(width, 1 + b)) for b in range(4)]
    for o in range(reach_offsets):
        where_to, its_width = moved[o % 4]
        weight = its_width * turn(area, -(o - o % 4))
        enters[o] = jnp.where(where_to == o + 1, weight, 0.0)

    def river_turn(substep, depth, flow, below):
        below = jnp.where(at_mouth, prev, below)
        flow = flow_after(flow, bed + depth, below, bed_top, drive, river_manning)
        moved = [turn(flow, 1 + b) for b in range(4)]
        sums = []
        for a in range(0, reach_offsets, 4):
            one, other = [
                enters[a + b] * moved[b] + enters[a + b + 1] * moved[b + 1] for b in (0, 2)
            ]
            sums.append(one + other)
        sums[0] = sums[0] + (depth + gain - loss * flow)
        depth, below = [
            (places[0] + places[1]) + (places[2] + places[3])
            for places in (
                [turn(value, 4 * a) for a, value in enumerate(sums)],
                [below_of(value, a) for a, value in enumerate(sums)],
            )
        ]
        series[substep * rows : (substep + 1) * rows] = grouped(flow * width, inland)
        return depth, flow, bed_below + below

    def count_mouths():
        for i in range(rows):
            names = jnp.broadcast_to(tiles[i : i + 1], (devices, LANES))
            hit = names == lax.broadcasted_iota(i32, (devices, LANES), 0)
            hots[i * devices : (i + 1) * devices] = jnp.where(hit, 1.0, 0.0).astype(bf16)
        shape = (LANES, 2 * LANES)
        earlier = lax.broadcasted_iota(i32, shape, 0) < lax.broadcasted_iota(i32, shape, 1)
        counted[...] = jnp.dot(
            hots[...], jnp.where(earlier, 1.0, 0.0).astype(bf16), preferred_element_type=f32
        )

    def rank_mouths():
        before = jnp.zeros((devices, LANES), f32)
        for i in range(rows):
            part = slice(i * devices, (i + 1) * devices)
            ranks = (counted[part, :LANES] + before) * hots[part].astype(f32)
            rank = jnp.sum(ranks, axis=0, keepdims=True).astype(i32)
            address_out[i : i + 1] = tiles[i : i + 1] * capacity + rank
            before = before + counted[part, LANES:]

    one, none = jnp.ones((LANES, LANES), bf16), jnp.zeros((LANES, LANES), bf16)
    number = lax.broadcasted_iota(i32, (TALL, LANES), 0).astype(f32)

    def label_mouths():
        high, low = split_label(address_out[...], WIDE)
        high_labels[...] = high.astype(f32)
        low_labels[...] = jnp.transpose(low.astype(f32))

    def slot_columns(group):
        place = lax.broadcasted_iota(i32, (LANES, LANES), 1).astype(f32).astype(bf16)
        for i in range(group * rows // 4, (group + 1) * rows // 4):
            lanes = slice(i * LANES, (i + 1) * LANES)
            column = jnp.broadcast_to(low_labels[:, i : i + 1], (LANES, LANES)).astype(bf16)
            for half in range(2):
                hit = column - half * LANES == place
                rhs[lanes, half * LANES : (half + 1) * LANES] = jnp.where(hit, one, none)

    def place_series(part, group):
        first, steps = PARTS[part]
        owner, lhs = owners[part], slots[part]
        for i in range(group * rows // 4, (group + 1) * rows // 4):
            lanes = slice(i * LANES, (i + 1) * LANES)
            labels = high_labels[i : i + 1]
            lay_out(series, first * rows + i, rows, steps, labels, owner, lhs, lanes)
            if part == 0:
                cells = series[STEPS * rows + i : STEPS * rows + i + 1]
                cells = jnp.where(number == labels, cells, 0.0)
                for half, value in enumerate(in_two(cells)):
                    at = 2 * TALL * steps + half * TALL
                    lhs[at : at + TALL, lanes] = value

    def pack(part):
        first, steps = PARTS[part]
        high_rows = TALL * steps
        lhs = slots[part]
        both = jnp.dot(lhs[...], rhs[...], preferred_element_type=f32)
        packed = both[:high_rows] + both[high_rows : 2 * high_rows]
        for half in range(2):
            lanes = slice(half * LANES, (half + 1) * LANES)
            for row in range(TALL):
                at = (2 * row + half) * SENT + first
                send_out[at : at + steps] = packed[row * steps : (row + 1) * steps, lanes]
            if part == 0:
                cells = both[2 * high_rows : 2 * high_rows + TALL] + both[2 * high_rows + TALL :]
                send_out[pl.ds(half * SENT + STEPS, TALL, stride=2 * SENT)] = cells[:, lanes]

    beside = {0: [count_mouths], 1: [rank_mouths], 2: [label_mouths]}
    beside |= {3 + group: [functools.partial(slot_columns, group)] for group in range(4)}
    beside |= {8: [functools.partial(place_series, 0, group) for group in range(2)]}
    beside |= {9: [functools.partial(place_series, 0, group) for group in range(2, 4)]}
    beside |= {10: [functools.partial(pack, 0)]}
    beside[10] += [functools.partial(place_series, 1, group) for group in range(4)]
    beside |= {11: [functools.partial(pack, 1)]}
    for owner, (_, steps) in zip(owners, PARTS):
        row_owners(owner, steps)
    depth, flow = depth_in[...], flow_in[...]
    below = bed_below + below_of(depth)
    for substep in range(STEPS):
        depth, flow, below = river_turn(substep, depth, flow, below)
        for work in beside.get(substep, []):
            work()
    depth_end[...] = depth
    finished = pltpu.make_async_copy(depth_end, depth_out, arrivals.at[15])
    finished.start()
    for group in range(4):
        place_series(2, group)
    pack(2)
    return finished


def reach_of(field):
    return STEPS - 1 - field if field < STEPS else HALO


def turn(value, lanes):
    lanes %= value.shape[1]
    return value if lanes == 0 else pltpu.roll(value, lanes, 1)


ROW_AT = [sum(reach_of(f) for f in range(field)) for field in range(FIELDS + 1)]
ROWS_SENT = -(-ROW_AT[FIELDS] // 8) * 8


def add_in_chunks(arrived, row_labels, column_labels, owner, places, lhs, rhs):
    row_owners(owner, STEPS)
    row_owners(places, 1)
    groups = arrived.shape[0] // SENT

    def place_of(label, part):
        return label == places[part : part + TALL]

    def place(chunk):
        for s in range(chunk, chunk + CHUNK):
            lanes = slice(s * LANES, (s + 1) * LANES)
            lay_out(arrived, s * SENT, 1, STEPS, row_labels[s : s + 1], owner, lhs, lanes)
            one_hot_columns(column_labels[s : s + 1], place_of, rhs, lanes)

    both = jnp.zeros((lhs.shape[0], WIDE), f32)
    place(0)
    for chunk in range(0, groups, CHUNK):
        if chunk + CHUNK < groups:
            place(chunk + CHUNK)
        lanes = slice(chunk * LANES, (chunk + CHUNK) * LANES)
        both = both + lax.dot_general(
            lhs[:, lanes], rhs[:, lanes], (((1,), (1,)), ((), ())), preferred_element_type=f32
        )
    half = lhs.shape[0] // 2
    return both[:half] + both[half:]


def edge_kernel(arrived, sea, odd, sea_out, *refs):
    owner, places, row_labels, column_labels, lhs, rhs, sums = refs
    first_of_pair = lax.axis_index("river") % 2 == 0
    groups = arrived.shape[0] // SENT
    tile_rows, tile_cols = sea.shape[0] // 4, sea.shape[1]
    sea_out[...] = sea[...]

    cells = arrived[pl.ds(STEPS, groups, stride=SENT)].astype(i32)
    row, column = split_label(cells, tile_cols)
    row = row - jnp.where(first_of_pair, 0, tile_rows - HALO)
    upper = jnp.where(row >= HALO // 2, 1, 0)
    inside = (row >= 0) & (row < HALO)
    row_labels[...] = jnp.where(inside, row - upper * (HALO // 2), WIDE - 1).astype(f32)
    column_labels[...] = (column + upper * tile_cols).astype(f32)
    total = add_in_chunks(arrived, row_labels, column_labels, owner, places, lhs, rhs)
    high_rows = total.shape[0]
    for half in range(2):
        part = slice(half * high_rows, (half + 1) * high_rows)
        sums[part] = total[:, half * LANES : (half + 1) * LANES]

    def put(field, start, end):
        reach = reach_of(field)
        if reach:
            last, first = end[end.shape[0] - reach :], start[:reach]
            part = slice(ROW_AT[field], ROW_AT[field] + reach)
            odd[part] = jnp.where(first_of_pair, first, last)

    odd[ROWS_SENT - 8 :] = jnp.zeros((8, LANES), f32)
    for step in range(STEPS):
        halves = [
            sums[pl.ds(half * high_rows + step, HALO // 2, stride=STEPS)] for half in range(2)
        ]
        rows = jnp.concatenate(halves, axis=0)
        put(step, rows, rows)
    for number in range(4):
        value = sea[number * tile_rows : (number + 1) * tile_rows]
        put(STEPS + number, value, value)


def source_kernel(arrived, sea, fields, even, rhs, label_out, *refs):
    owner, places, column_labels, lhs, sums = refs
    first_of_pair = lax.axis_index("river") % 2 == 0
    groups = arrived.shape[0] // SENT
    tile_rows, tile_cols = sea.shape[0] // 4, sea.shape[1]

    cells = arrived[pl.ds(STEPS, groups, stride=SENT)].astype(i32)
    row, column = cell_labels(cells, tile_cols)
    label_out[...] = row.astype(f32)
    column_labels[...] = column.astype(f32)
    total = add_in_chunks(arrived, label_out, column_labels, owner, places, lhs, rhs)
    high_rows = total.shape[0]
    for half in range(2):
        part = slice(half * high_rows, (half + 1) * high_rows)
        sums[part] = total[:, half * LANES : (half + 1) * LANES]

    def put(field, value):
        fields[field * tile_rows : (field + 1) * tile_rows] = value
        reach = reach_of(field)
        if reach:
            last, first = value[tile_rows - reach :], value[:reach]
            part = slice(ROW_AT[field], ROW_AT[field] + reach)
            even[part] = jnp.where(first_of_pair, last, first)

    even[ROWS_SENT - 8 :] = jnp.zeros((8, LANES), f32)
    for step in range(STEPS):
        halves = [sums[pl.ds(half * high_rows + step, TALL, stride=STEPS)] for half in range(2)]
        put(step, jnp.concatenate(halves, axis=0))
    for number in range(4):
        put(STEPS + number, sea[number * tile_rows : (number + 1) * tile_rows])


def strip_kernel(fields, from_odd, from_even, tall, odd, even):
    upper = lax.axis_index("river") % 2 == 0
    first_of_pair = lax.axis_index("coast") % 2 == 0
    from_before = jnp.where(upper, from_odd[...], from_even[...])
    from_after = jnp.where(upper, from_even[...], from_odd[...])
    tile_rows = fields.shape[0] // FIELDS
    height = tall.shape[0] // FIELDS
    lane = lax.broadcasted_iota(i32, (height, LANES), 1)
    ends = jnp.zeros((height, LANES), f32)
    starts = jnp.zeros((height, LANES), f32)
    for field in range(FIELDS):
        reach, at = reach_of(field), ROW_AT[field]
        parts = [fields[field * tile_rows : (field + 1) * tile_rows]]
        if reach:
            parts.append(from_after[at : at + reach])
        if reach < HALO:
            parts.append(jnp.zeros((2 * HALO - 2 * reach, LANES), f32))
        if reach:
            parts.append(from_before[at : at + reach])
        value = jnp.concatenate(parts, axis=0)
        tall[field * height : (field + 1) * height] = value
        if reach:
            here = (lane >= at) & (lane < at + reach)
            ends = jnp.where(here, turn(value, at + reach - LANES), ends)
            starts = jnp.where(here, turn(value, at), starts)
    odd[...] = jnp.where(first_of_pair, starts, ends)
    even[...] = jnp.where(first_of_pair, ends, starts)


def ocean_kernel(
    tile_rows, tall, from_odd, from_even, row_labels, hot, level_out, replies, history, level_end, departure
):
    height = tall.shape[0] // FIELDS
    width = 2 * LANES
    river, coast = lax.axis_index("river"), lax.axis_index("coast")
    rivers, coasts = lax.axis_size("river"), lax.axis_size("coast")
    lane = lax.broadcasted_iota(i32, (height, LANES), 1)
    from_left = jnp.where(coast % 2 == 0, from_odd[...], from_even[...])
    from_right = jnp.where(coast % 2 == 0, from_even[...], from_odd[...])

    def whole(field):
        reach, at = reach_of(field), ROW_AT[field]
        beside = jnp.zeros((height, LANES), f32)
        if reach:
            beside = jnp.where(lane < reach, turn(from_right, -at), beside)
            beside = jnp.where(lane >= LANES - reach, turn(from_left, -at - reach), beside)
        return jnp.concatenate([tall[field * height : (field + 1) * height], beside], axis=1)

    level, bed, east, north = [whole(STEPS + number) for number in range(4)]

    row = lax.broadcasted_iota(i32, (height, width), 0)
    column = lax.broadcasted_iota(i32, (height, width), 1)
    row_in = jnp.where(
        row < tile_rows, 1, jnp.where(row < tile_rows + HALO, (river < rivers - 1).astype(i32), (river > 0).astype(i32))
    )
    column_in = jnp.where(
        column < LANES, 1, jnp.where(column < LANES + LANES // 2, (coast < coasts - 1).astype(i32), (coast > 0).astype(i32))
    )
    inside = row_in * column_in == 1

    def next_row(value):
        return pltpu.roll(value, height - 1, 0)

    def next_column(value):
        return pltpu.roll(value, width - 1, 1)

    bed_east = jnp.maximum(bed, next_row(bed))
    bed_north = jnp.maximum(bed, next_column(bed))
    drive = gravity * step_seconds / cell_metres

    def ocean_turn(first, steps, step, level, east, north):
        source = whole(step) * (step_seconds / (cell_metres * cell_metres))
        east = flow_after(east, level, next_row(level), bed_east, drive, ocean_manning)
        north = flow_after(north, level, next_column(level), bed_north, drive, ocean_manning)
        spread = east - pltpu.roll(east, 1, 0) + north - pltpu.roll(north, 1, 1)
        level = level - step_seconds / cell_metres * spread + source
        level = jnp.where(inside, level, 0.0)
        for half in range(2):
            part = level[half * TALL : (half + 1) * TALL, :LANES]
            at = TALL * (2 * first + half * steps) + step - first
            history[pl.ds(at, TALL, stride=steps)] = part
        return level, east, north

    def table_of(first, steps):
        high_rows, at = TALL * steps, 2 * TALL * first
        halves = [history[at + half * high_rows : at + (half + 1) * high_rows] for half in range(2)]
        return jnp.concatenate(in_two(jnp.concatenate(halves, axis=1)), axis=0)

    def reply(table, first, steps, group, of):
        count = replies.shape[0] // STEPS // of
        for s in range(group * count, (group + 1) * count, 2):
            rows = jnp.concatenate([row_labels[s : s + 1], row_labels[s + 1 : s + 2]], axis=1)
            found = look_up(table, rows, hot[:, s * LANES : (s + 2) * LANES], steps)
            for half in range(2):
                at = (s + half) * STEPS + first
                replies[at : at + steps] = found[:, half * LANES : (half + 1) * LANES]

    waiting = []
    for part, (first, steps) in enumerate(LOOKED_UP):
        for step in range(first, first + steps):
            level, east, north = ocean_turn(first, steps, step, level, east, north)
            if waiting:
                reply(*waiting, step - first, steps)
        if part == len(LOOKED_UP) - 1:
            level_end[...] = level[:tile_rows, :LANES]
            finished = pltpu.make_async_copy(level_end, level_out, departure)
            finished.start()
        waiting = [table_of(first, steps), first, steps]
    reply(*waiting, 0, 1)
    finished.wait()


def mouth_kernel(returned, address, level_out, whole, series, hot, block, departures):
    rows = address.shape[0]
    groups = LANES // MPB
    place = lax.broadcasted_iota(i32, (TALL, 2 * LANES), 0).astype(f32).astype(bf16)

    def place_of(label, part):
        return label - part == place

    labels = []
    for i in range(0, rows, 2):
        pair = jnp.concatenate([address[i : i + 1], address[i + 1 : i + 2]], axis=1)
        high, low = [label.astype(f32) for label in split_label(pair, WIDE)]
        one_hot_columns(low, place_of, hot, slice(i * LANES, (i + 2) * LANES))
        labels.append(high)
    lane = lax.broadcasted_iota(i32, (rows, LANES), 1)
    copies = []
    for first, steps in LOOKED_UP:
        for row in range(TALL):
            for half in range(2):
                at = (2 * row + half) * STEPS + first
                to = first * TALL + row * steps
                lanes = slice(half * LANES, (half + 1) * LANES)
                whole[to : to + steps, lanes] = returned[at : at + steps]
        own = whole[first * TALL : (first + steps) * TALL]
        table = jnp.concatenate(in_two(own), axis=0)
        for i in range(0, rows, 2):
            lanes = slice(i * LANES, (i + 2) * LANES)
            found = look_up(table, labels[i // 2], hot[:, lanes], steps)
            series[pl.ds(first * rows + i, steps, stride=rows)] = found[:, :LANES]
            series[pl.ds(first * rows + i + 1, steps, stride=rows)] = found[:, LANES:]
        for number in range(first // groups, (first + steps) // groups):
            for g in range(groups):
                result = jnp.zeros((rows, LANES), f32)
                for place in range(groups):
                    at = (number * groups + place) * rows
                    part = turn(series[at : at + rows], (place - g) * MPB)
                    result = jnp.where(lane // MPB == place, part, result)
                block[number, g * rows : (g + 1) * rows] = result
            to = level_out.at[:, pl.ds(number * LANES, LANES)]
            copies.append(pltpu.make_async_copy(block.at[number], to, departures.at[number]))
            copies[-1].start()
    for copy in copies:
        copy.wait()


def shape(*dims, dtype=f32):
    return jax.ShapeDtypeStruct(dims, dtype)


def cost(products):
    return pl.CostEstimate(flops=2 * products, bytes_accessed=8 << 20, transcendentals=0)


def in_hbm(*arrays):
    return [pltpu.with_memory_space_constraint(whole, pltpu.HBM) for whole in arrays]


def swap(values, tall, devices, capacity):
    per = LANES // capacity
    if per > 1:
        values = values.reshape(devices // per, tall, per, capacity).transpose(0, 2, 1, 3)
    values = values.reshape(devices, 1, tall * capacity)
    values = lax.all_to_all(values, ("coast", "river"), split_axis=0, concat_axis=0, tiled=True)
    if per > 1:
        values = values.reshape(devices // per, per, tall, capacity).transpose(0, 2, 1, 3)
    return values.reshape(devices // per * tall, LANES)


def with_neighbour(value, axis, start):
    pairs = range(start, lax.axis_size(axis) - 1, 2)
    return lax.ppermute(value, axis, [(i + k, i + 1 - k) for i in pairs for k in range(2)])


def per_device(
    reach_depth,
    reach_flow,
    reach_bed,
    reach_width,
    reach_length,
    runoff,
    flows_into,
    mouth_prev,
    mouth_tile,
    mouth_cell,
    sea_level,
    sea_bed,
    wet_mask,
    flux_east,
    flux_north,
):
    devices = lax.axis_size("river") * lax.axis_size("coast")
    blocks = reach_depth.shape[0]
    tile_rows, tile_cols = sea_level.shape
    mouths = blocks * MPB
    capacity = max(2, 2 * mouths // devices)
    groups = devices * capacity // LANES
    rows = mouths // LANES
    height = tile_rows + 2 * HALO

    depth_after, sending, address, sea = pl.pallas_call(
        functools.partial(river_kernel, devices, lax.axis_size("coast"), capacity),
        name="river",
        out_shape=(
            shape(blocks, RB),
            shape(groups * SENT, LANES),
            shape(rows, LANES, dtype=i32),
            shape(4 * tile_rows, tile_cols),
        ),
        in_specs=[pl.BlockSpec(memory_space=pltpu.HBM)] * 15,
        out_specs=(
            pl.BlockSpec(memory_space=pltpu.HBM),
            pl.BlockSpec(memory_space=pltpu.VMEM),
            pl.BlockSpec(memory_space=pltpu.VMEM),
            pl.BlockSpec(memory_space=pltpu.VMEM),
        ),
        scratch_shapes=[pltpu.VMEM((blocks, RB), f32)] * 6
        + [
            pltpu.VMEM((blocks, RB), i32),
            pltpu.VMEM((MPB, blocks), f32),
            pltpu.VMEM((MPB, blocks), i32),
            pltpu.VMEM((MPB, blocks), i32),
            pltpu.VMEM((tile_rows, tile_cols), f32),
            pltpu.VMEM((tile_rows, tile_cols), f32),
            pltpu.VMEM((tile_rows, tile_cols), i32),
            pltpu.VMEM((tile_rows, tile_cols), f32),
            pltpu.VMEM((tile_rows, tile_cols), f32),
            pltpu.SemaphoreType.DMA((16,)),
            pltpu.VMEM((blocks, RB), f32),
            pltpu.VMEM((reach_offsets, blocks, RB), f32),
            pltpu.VMEM((SENT * rows, LANES), f32),
            pltpu.VMEM((RB, LANES), f32),
            pltpu.VMEM((rows, LANES), i32),
            pltpu.VMEM((rows * devices, LANES), bf16),
            pltpu.VMEM((rows * devices, 2 * LANES), f32),
            pltpu.VMEM((rows, LANES), f32),
            pltpu.VMEM((LANES, rows), f32),
            pltpu.VMEM((mouths, WIDE), bf16),
            *[pltpu.VMEM((TALL * steps, LANES), bf16) for _, steps in PARTS],
            *[
                pltpu.VMEM((2 * TALL * (steps + (first == 0)), mouths), bf16)
                for first, steps in PARTS
            ],
        ],
        compiler_params=PARAMS,
    )(
        *in_hbm(
            reach_depth,
            reach_flow,
            reach_bed,
            reach_width,
            reach_length,
            runoff,
            flows_into,
            mouth_prev.T,
            mouth_tile[:, :, 0].T,
            mouth_cell.T,
            sea_level,
            sea_bed,
            wet_mask,
            flux_east,
            flux_north,
        )
    )
    arrived = swap(sending, SENT, devices, capacity)

    edge_rows = -(-HALO // 2 * STEPS // TALL) * TALL
    odd, sea = pl.pallas_call(
        edge_kernel,
        name="edges",
        out_shape=(shape(ROWS_SENT, LANES), shape(4 * tile_rows, tile_cols)),
        scratch_shapes=[
            pltpu.VMEM((edge_rows, LANES), bf16),
            pltpu.VMEM((WIDE, LANES), bf16),
            pltpu.VMEM((groups, LANES), f32),
            pltpu.VMEM((groups, LANES), f32),
            pltpu.VMEM((2 * edge_rows, groups * LANES), bf16),
            pltpu.VMEM((WIDE, groups * LANES), bf16),
            pltpu.VMEM((2 * edge_rows, LANES), f32),
        ],
        cost_estimate=cost(2 * edge_rows * WIDE * groups * LANES),
        compiler_params=PARAMS,
    )(arrived, sea)
    from_odd = with_neighbour(odd, "river", 1)

    fields, even, hot, labels = pl.pallas_call(
        source_kernel,
        name="sources",
        out_shape=(
            shape(FIELDS * tile_rows, LANES),
            shape(ROWS_SENT, LANES),
            shape(WIDE, groups * LANES, dtype=bf16),
            shape(groups, LANES),
        ),
        scratch_shapes=[
            pltpu.VMEM((TALL * STEPS, LANES), bf16),
            pltpu.VMEM((WIDE, LANES), bf16),
            pltpu.VMEM((groups, LANES), f32),
            pltpu.VMEM((2 * TALL * STEPS, groups * LANES), bf16),
            pltpu.VMEM((2 * TALL * STEPS, LANES), f32),
        ],
        cost_estimate=cost(2 * TALL * STEPS * WIDE * groups * LANES),
        compiler_params=PARAMS,
    )(arrived, sea)
    from_even = with_neighbour(even, "river", 0)

    tall, odd, even = pl.pallas_call(
        strip_kernel,
        name="strips",
        out_shape=(shape(FIELDS * height, LANES), shape(height, LANES), shape(height, LANES)),
        compiler_params=PARAMS,
    )(fields, from_odd, from_even)
    from_odd, from_even = with_neighbour(odd, "coast", 1), with_neighbour(even, "coast", 0)

    level_after, replies = pl.pallas_call(
        functools.partial(ocean_kernel, tile_rows),
        name="ocean",
        out_shape=(shape(tile_rows, tile_cols), shape(groups * STEPS, LANES)),
        scratch_shapes=[
            pltpu.VMEM((2 * TALL * STEPS, LANES), f32),
            pltpu.VMEM((tile_rows, tile_cols), f32),
            pltpu.SemaphoreType.DMA,
        ],
        out_specs=(
            pl.BlockSpec(memory_space=pltpu.HBM),
            pl.BlockSpec(memory_space=pltpu.VMEM),
        ),
        compiler_params=PARAMS,
    )(tall, from_odd, from_even, labels, hot)
    returned = swap(replies, STEPS, devices, capacity)

    mouth_level = pl.pallas_call(
        mouth_kernel,
        name="mouths",
        out_shape=shape(blocks, STEPS * MPB),
        scratch_shapes=[
            pltpu.VMEM((TALL * STEPS, WIDE), f32),
            pltpu.VMEM((STEPS * rows, LANES), f32),
            pltpu.VMEM((WIDE, mouths), bf16),
            pltpu.VMEM((STEPS * MPB // LANES, blocks, LANES), f32),
            pltpu.SemaphoreType.DMA((STEPS * MPB // LANES,)),
        ],
        out_specs=pl.BlockSpec(memory_space=pltpu.HBM),
        compiler_params=PARAMS,
    )(returned, address)
    return (depth_after, level_after, mouth_level)


def solution(mesh):
    by_block = P(("river", "coast"), None)
    tiled = P("river", "coast")
    return jax.shard_map(
        per_device,
        mesh=mesh,
        in_specs=(by_block,) * 8
        + (P(("river", "coast"), None, None), by_block)
        + (tiled,) * 5,
        out_specs=(by_block, tiled, by_block),
        check_vma=False,
    )
```

```python
import functools
import math

import jax
import jax.numpy as jnp
from jax import lax
from jax.experimental import pallas as pl
from jax.experimental.pallas import tpu as pltpu
from jax.sharding import PartitionSpec as P

RB = 128
MPB = 32
STEPS = 12

gravity = 9.81
step_seconds = 300.0
cell_metres = 3000.0
river_manning = 0.035
ocean_manning = 0.025
depth_floor = 0.05
reach_offsets = 16

LANES = 128
SENT = 13
TALL = 16
WIDE = 256
PARTS = ((0, 8), (8, 2), (10, 2))
LOOKED_UP = ((0, 8), (8, 4))
CHUNK = 4
HALO = 12
FIELDS = 16
f32, bf16, i32 = jnp.float32, jnp.bfloat16, jnp.int32

PARAMS = pltpu.CompilerParams(vmem_limit_bytes=40 * 1024 * 1024)


def flow_after(unit_flow, upper, lower, bed_top, drive, manning):
    face_depth = jnp.maximum(upper, lower) - bed_top
    driving = drive * jnp.maximum(face_depth, 0.0) * (upper - lower)
    power = -7.0 / 3.0 * math.log2(math.e)
    thin = jnp.exp2(jnp.log(jnp.maximum(face_depth, depth_floor)) * power)
    friction = (gravity * step_seconds * manning * manning) * jnp.abs(unit_flow) * thin
    divisor = 1.0 + friction
    inverse = pl.reciprocal(divisor, approx=True)
    return ((unit_flow + driving) * inverse) * (2.0 - divisor * inverse)


def in_two(values):
    high = values.astype(bf16)
    return high, (values - high.astype(f32)).astype(bf16)


def small(labels):
    return jnp.broadcast_to(labels, (TALL, labels.shape[1])).astype(bf16)


def one_hot_columns(columns, place_of, rhs, lanes):
    labels = small(columns)
    one, none = jnp.ones(labels.shape, bf16), jnp.zeros(labels.shape, bf16)
    for part in range(0, WIDE, TALL):
        hit = place_of(labels, part)
        rhs[part : part + TALL, lanes] = jnp.where(hit, one, none)


def row_owners(owner, steps):
    for part in range(0, owner.shape[0], TALL):
        number = part + lax.broadcasted_iota(i32, (TALL, LANES), 0)
        owner[part : part + TALL] = (number // steps).astype(f32).astype(bf16)


def in_turn(series, at, stride, steps, first):
    parts, row = [], first
    while row < first + 8:
        step = row % steps
        count = min(steps - step, first + 8 - row)
        parts.append(series[pl.ds(at + step * stride, count, stride=stride)])
        row += count
    return parts[0] if len(parts) == 1 else jnp.concatenate(parts, axis=0)


def lay_out(series, at, stride, steps, rows, owner, lhs, lanes):
    turns = math.lcm(steps, 8) // 8
    cycle = [in_turn(series, at, stride, steps, 8 * turn) for turn in range(turns)]
    pairs = [(cycle[2 * k % turns], cycle[(2 * k + 1) % turns]) for k in range(turns)]
    halves = [in_two(jnp.concatenate(pair, axis=0)) for pair in pairs]
    labels = small(rows)
    none = jnp.zeros(labels.shape, bf16)
    high_rows = owner.shape[0]
    for part in range(0, high_rows, TALL):
        hit = labels == owner[part : part + TALL]
        for number, half in enumerate(halves[part // TALL % turns]):
            at_rows = slice(number * high_rows + part, number * high_rows + part + TALL)
            lhs[at_rows, lanes] = jnp.where(hit, half, none)


def look_up(table, rows, hot, steps):
    found = jnp.dot(table, hot, preferred_element_type=f32)
    per = 2 if steps > 6 else 4
    several = (per * steps, rows.shape[1])
    number = (lax.broadcasted_iota(i32, several, 0) // steps).astype(f32)
    labels = jnp.broadcast_to(rows, several) - number
    total = jnp.zeros(several, f32)
    for row in range(0, TALL, per):
        high = found[row * steps : (row + per) * steps]
        low = found[(TALL + row) * steps : (TALL + row + per) * steps]
        total = total + jnp.where(labels == row, high + low, 0.0)
    result = total[:steps]
    for number in range(1, per):
        result = result + total[number * steps : (number + 1) * steps]
    return result


def split_label(number, size):
    return lax.shift_right_logical(number, size.bit_length() - 1), number & (size - 1)


def cell_labels(cells, tile_cols):
    row, column = split_label(cells, tile_cols)
    upper, row = split_label(row, TALL)
    return row, upper * tile_cols + column


def river_kernel(
    devices,
    coasts,
    capacity,
    *refs,
):
    inputs, (depth_out, send_out, address_out, sea_out), refs = refs[:15], refs[15:19], refs[19:]
    arrivals = refs[15]
    copies = [
        pltpu.make_async_copy(whole, own, arrivals.at[number])
        for number, (whole, own) in enumerate(zip(inputs, refs[:15]))
    ]
    copies, of_sea = copies[:10], copies[10:]
    for copy in copies[::-1] + of_sea:
        copy.start()
    outputs = (depth_out, send_out, address_out)
    river_steps(devices, coasts, capacity, copies, *refs[:10], *outputs, *refs[16:])

    sea_level, sea_bed, wet_mask, flux_east, flux_north = refs[10:15]
    tile_rows = sea_level.shape[0]
    for copy in of_sea:
        copy.wait()
    bed = sea_bed[...]
    level = jnp.where(wet_mask[...] == 1, jnp.maximum(sea_level[...], bed), bed)
    for number, value in enumerate((level, bed, flux_east[...], flux_north[...])):
        sea_out[number * tile_rows : (number + 1) * tile_rows] = value


def river_steps(
    devices,
    coasts,
    capacity,
    copies,
    depth_in,
    flow_in,
    bed_in,
    width_in,
    length_in,
    runoff_in,
    into_in,
    prev_in,
    tile_in,
    cell_in,
    depth_out,
    send_out,
    address_out,
    enters,
    series,
    turned,
    tiles,
    hots,
    counted,
    high_labels,
    low_labels,
    rhs,
    *parts,
):
    owners, slots = parts[: len(PARTS)], parts[len(PARTS) :]
    blocks = depth_in.shape[0]
    groups = LANES // MPB
    rows = blocks // groups
    inland = RB - MPB
    lane = lax.broadcasted_iota(i32, (blocks, RB), 1)

    for copy in copies:
        copy.wait()

    turned[...] = jnp.zeros_like(turned)
    turned[0:MPB, 0:blocks] = tile_in[...].astype(f32)
    turned[MPB : 2 * MPB, 0:blocks] = cell_in[...].astype(f32)
    turned[inland:RB, 0:blocks] = prev_in[...]
    mouths = jnp.transpose(turned[...])[0:blocks]
    prev = mouths

    def grouped(array, first):
        lanes16 = lax.broadcasted_iota(i32, (rows, LANES), 1)
        result = jnp.zeros((rows, LANES), f32)
        for g in range(groups):
            part = array[g * rows : (g + 1) * rows]
            shift = (g * MPB - first) % LANES
            part = part if shift == 0 else pltpu.roll(part, shift, 1)
            result = jnp.where(lanes16 // MPB == g, part, result)
        return result

    tile = grouped(mouths, 0).astype(i32)
    tiles[...] = tile % coasts * (devices // coasts) + tile // coasts
    series[STEPS * rows :] = grouped(mouths, MPB)

    into = into_in[...]
    at_mouth = lane >= inland
    down = jnp.where(at_mouth, 0, into)
    offset = jnp.where(at_mouth, 0, into - lane)
    bed = bed_in[...]

    sources = [(down - 4 * a) & (RB - 1) for a in range(reach_offsets // 4)]

    def below_of(value, a=0):
        return jnp.take_along_axis(value, sources[a], axis=1, mode="promise_in_bounds")

    bed_below = below_of(bed)
    bed_top = jnp.where(at_mouth, bed, jnp.maximum(bed, bed_below))
    drive = gravity * step_seconds / length_in[...]
    width = width_in[...]
    area = step_seconds / (width * length_in[...])
    gain = area * runoff_in[...]
    loss = area * width
    moved = [(turn(offset, 1 + b), turn(width, 1 + b)) for b in range(4)]
    for o in range(reach_offsets):
        where_to, its_width = moved[o % 4]
        weight = its_width * turn(area, -(o - o % 4))
        enters[o] = jnp.where(where_to == o + 1, weight, 0.0)

    def river_turn(substep, depth, flow, below):
        below = jnp.where(at_mouth, prev, below)
        flow = flow_after(flow, bed + depth, below, bed_top, drive, river_manning)
        moved = [turn(flow, 1 + b) for b in range(4)]
        sums = []
        for a in range(0, reach_offsets, 4):
            one, other = [
                enters[a + b] * moved[b] + enters[a + b + 1] * moved[b + 1] for b in (0, 2)
            ]
            sums.append(one + other)
        sums[0] = sums[0] + (depth + gain - loss * flow)
        depth, below = [
            (places[0] + places[1]) + (places[2] + places[3])
            for places in (
                [turn(value, 4 * a) for a, value in enumerate(sums)],
                [below_of(value, a) for a, value in enumerate(sums)],
            )
        ]
        series[substep * rows : (substep + 1) * rows] = grouped(flow * width, inland)
        return depth, flow, bed_below + below

    def count_mouths():
        for i in range(rows):
            names = jnp.broadcast_to(tiles[i : i + 1], (devices, LANES))
            hit = names == lax.broadcasted_iota(i32, (devices, LANES), 0)
            hots[i * devices : (i + 1) * devices] = jnp.where(hit, 1.0, 0.0).astype(bf16)
        shape = (LANES, 2 * LANES)
        earlier = lax.broadcasted_iota(i32, shape, 0) < lax.broadcasted_iota(i32, shape, 1)
        counted[...] = jnp.dot(
            hots[...], jnp.where(earlier, 1.0, 0.0).astype(bf16), preferred_element_type=f32
        )

    def rank_mouths():
        before = jnp.zeros((devices, LANES), f32)
        for i in range(rows):
            part = slice(i * devices, (i + 1) * devices)
            ranks = (counted[part, :LANES] + before) * hots[part].astype(f32)
            rank = jnp.sum(ranks, axis=0, keepdims=True).astype(i32)
            address_out[i : i + 1] = tiles[i : i + 1] * capacity + rank
            before = before + counted[part, LANES:]

    one, none = jnp.ones((LANES, LANES), bf16), jnp.zeros((LANES, LANES), bf16)
    number = lax.broadcasted_iota(i32, (TALL, LANES), 0).astype(f32)

    def label_mouths():
        high, low = split_label(address_out[...], WIDE)
        high_labels[...] = high.astype(f32)
        low_labels[...] = jnp.transpose(low.astype(f32))

    def slot_columns(group):
        place = lax.broadcasted_iota(i32, (LANES, LANES), 1).astype(f32).astype(bf16)
        for i in range(group * rows // 4, (group + 1) * rows // 4):
            lanes = slice(i * LANES, (i + 1) * LANES)
            column = jnp.broadcast_to(low_labels[:, i : i + 1], (LANES, LANES)).astype(bf16)
            for half in range(2):
                hit = column - half * LANES == place
                rhs[lanes, half * LANES : (half + 1) * LANES] = jnp.where(hit, one, none)

    def place_series(part, group):
        first, steps = PARTS[part]
        owner, lhs = owners[part], slots[part]
        for i in range(group * rows // 4, (group + 1) * rows // 4):
            lanes = slice(i * LANES, (i + 1) * LANES)
            labels = high_labels[i : i + 1]
            lay_out(series, first * rows + i, rows, steps, labels, owner, lhs, lanes)
            if part == 0:
                cells = series[STEPS * rows + i : STEPS * rows + i + 1]
                cells = jnp.where(number == labels, cells, 0.0)
                for half, value in enumerate(in_two(cells)):
                    at = 2 * TALL * steps + half * TALL
                    lhs[at : at + TALL, lanes] = value

    def pack(part):
        first, steps = PARTS[part]
        high_rows = TALL * steps
        lhs = slots[part]
        both = jnp.dot(lhs[...], rhs[...], preferred_element_type=f32)
        packed = both[:high_rows] + both[high_rows : 2 * high_rows]
        for half in range(2):
            lanes = slice(half * LANES, (half + 1) * LANES)
            for row in range(TALL):
                at = (2 * row + half) * SENT + first
                send_out[at : at + steps] = packed[row * steps : (row + 1) * steps, lanes]
            if part == 0:
                cells = both[2 * high_rows : 2 * high_rows + TALL] + both[2 * high_rows + TALL :]
                send_out[pl.ds(half * SENT + STEPS, TALL, stride=2 * SENT)] = cells[:, lanes]

    beside = {0: [count_mouths], 1: [rank_mouths], 2: [label_mouths]}
    beside |= {3 + group: [functools.partial(slot_columns, group)] for group in range(4)}
    beside |= {8: [functools.partial(place_series, 0, group) for group in range(2)]}
    beside |= {9: [functools.partial(place_series, 0, group) for group in range(2, 4)]}
    beside |= {10: [functools.partial(pack, 0)]}
    beside[10] += [functools.partial(place_series, 1, group) for group in range(4)]
    beside |= {11: [functools.partial(pack, 1)]}
    for owner, (_, steps) in zip(owners, PARTS):
        row_owners(owner, steps)
    depth, flow = depth_in[...], flow_in[...]
    below = bed_below + below_of(depth)
    for substep in range(STEPS):
        depth, flow, below = river_turn(substep, depth, flow, below)
        for work in beside.get(substep, []):
            work()
    depth_out[...] = depth
    for group in range(4):
        place_series(2, group)
    pack(2)


def reach_of(field):
    return STEPS - 1 - field if field < STEPS else HALO


def turn(value, lanes):
    lanes %= value.shape[1]
    return value if lanes == 0 else pltpu.roll(value, lanes, 1)


ROW_AT = [sum(reach_of(f) for f in range(field)) for field in range(FIELDS + 1)]
ROWS_SENT = -(-ROW_AT[FIELDS] // 8) * 8


def add_in_chunks(arrived, row_labels, column_labels, owner, places, lhs, rhs):
    row_owners(owner, STEPS)
    row_owners(places, 1)
    groups = arrived.shape[0] // SENT

    def place_of(label, part):
        return label == places[part : part + TALL]

    def place(chunk):
        for s in range(chunk, chunk + CHUNK):
            lanes = slice(s * LANES, (s + 1) * LANES)
            lay_out(arrived, s * SENT, 1, STEPS, row_labels[s : s + 1], owner, lhs, lanes)
            one_hot_columns(column_labels[s : s + 1], place_of, rhs, lanes)

    both = jnp.zeros((lhs.shape[0], WIDE), f32)
    place(0)
    for chunk in range(0, groups, CHUNK):
        if chunk + CHUNK < groups:
            place(chunk + CHUNK)
        lanes = slice(chunk * LANES, (chunk + CHUNK) * LANES)
        both = both + lax.dot_general(
            lhs[:, lanes], rhs[:, lanes], (((1,), (1,)), ((), ())), preferred_element_type=f32
        )
    half = lhs.shape[0] // 2
    return both[:half] + both[half:]


def edge_kernel(arrived, sea, odd, sea_out, *refs):
    owner, places, row_labels, column_labels, lhs, rhs, sums = refs
    first_of_pair = lax.axis_index("river") % 2 == 0
    groups = arrived.shape[0] // SENT
    tile_rows, tile_cols = sea.shape[0] // 4, sea.shape[1]
    sea_out[...] = sea[...]

    cells = arrived[pl.ds(STEPS, groups, stride=SENT)].astype(i32)
    row, column = split_label(cells, tile_cols)
    row = row - jnp.where(first_of_pair, 0, tile_rows - HALO)
    upper = jnp.where(row >= HALO // 2, 1, 0)
    inside = (row >= 0) & (row < HALO)
    row_labels[...] = jnp.where(inside, row - upper * (HALO // 2), WIDE - 1).astype(f32)
    column_labels[...] = (column + upper * tile_cols).astype(f32)
    total = add_in_chunks(arrived, row_labels, column_labels, owner, places, lhs, rhs)
    high_rows = total.shape[0]
    for half in range(2):
        part = slice(half * high_rows, (half + 1) * high_rows)
        sums[part] = total[:, half * LANES : (half + 1) * LANES]

    def put(field, start, end):
        reach = reach_of(field)
        if reach:
            last, first = end[end.shape[0] - reach :], start[:reach]
            part = slice(ROW_AT[field], ROW_AT[field] + reach)
            odd[part] = jnp.where(first_of_pair, first, last)

    odd[ROWS_SENT - 8 :] = jnp.zeros((8, LANES), f32)
    for step in range(STEPS):
        halves = [
            sums[pl.ds(half * high_rows + step, HALO // 2, stride=STEPS)] for half in range(2)
        ]
        rows = jnp.concatenate(halves, axis=0)
        put(step, rows, rows)
    for number in range(4):
        value = sea[number * tile_rows : (number + 1) * tile_rows]
        put(STEPS + number, value, value)


def source_kernel(arrived, sea, depth, fields, even, rhs, label_out, depth_out, *refs):
    owner, places, column_labels, lhs, sums, departure = refs
    finished = pltpu.make_async_copy(depth, depth_out, departure)
    finished.start()
    first_of_pair = lax.axis_index("river") % 2 == 0
    groups = arrived.shape[0] // SENT
    tile_rows, tile_cols = sea.shape[0] // 4, sea.shape[1]

    cells = arrived[pl.ds(STEPS, groups, stride=SENT)].astype(i32)
    row, column = cell_labels(cells, tile_cols)
    label_out[...] = row.astype(f32)
    column_labels[...] = column.astype(f32)
    total = add_in_chunks(arrived, label_out, column_labels, owner, places, lhs, rhs)
    high_rows = total.shape[0]
    for half in range(2):
        part = slice(half * high_rows, (half + 1) * high_rows)
        sums[part] = total[:, half * LANES : (half + 1) * LANES]

    def put(field, value):
        fields[field * tile_rows : (field + 1) * tile_rows] = value
        reach = reach_of(field)
        if reach:
            last, first = value[tile_rows - reach :], value[:reach]
            part = slice(ROW_AT[field], ROW_AT[field] + reach)
            even[part] = jnp.where(first_of_pair, last, first)

    even[ROWS_SENT - 8 :] = jnp.zeros((8, LANES), f32)
    for step in range(STEPS):
        halves = [sums[pl.ds(half * high_rows + step, TALL, stride=STEPS)] for half in range(2)]
        put(step, jnp.concatenate(halves, axis=0))
    for number in range(4):
        put(STEPS + number, sea[number * tile_rows : (number + 1) * tile_rows])
    finished.wait()


def strip_kernel(fields, from_odd, from_even, tall, odd, even):
    upper = lax.axis_index("river") % 2 == 0
    first_of_pair = lax.axis_index("coast") % 2 == 0
    from_before = jnp.where(upper, from_odd[...], from_even[...])
    from_after = jnp.where(upper, from_even[...], from_odd[...])
    tile_rows = fields.shape[0] // FIELDS
    height = tall.shape[0] // FIELDS
    lane = lax.broadcasted_iota(i32, (height, LANES), 1)
    ends = jnp.zeros((height, LANES), f32)
    starts = jnp.zeros((height, LANES), f32)
    for field in range(FIELDS):
        reach, at = reach_of(field), ROW_AT[field]
        parts = [fields[field * tile_rows : (field + 1) * tile_rows]]
        if reach:
            parts.append(from_after[at : at + reach])
        if reach < HALO:
            parts.append(jnp.zeros((2 * HALO - 2 * reach, LANES), f32))
        if reach:
            parts.append(from_before[at : at + reach])
        value = jnp.concatenate(parts, axis=0)
        tall[field * height : (field + 1) * height] = value
        if reach:
            here = (lane >= at) & (lane < at + reach)
            ends = jnp.where(here, turn(value, at + reach - LANES), ends)
            starts = jnp.where(here, turn(value, at), starts)
    odd[...] = jnp.where(first_of_pair, starts, ends)
    even[...] = jnp.where(first_of_pair, ends, starts)


def ocean_kernel(
    tile_rows, tall, from_odd, from_even, row_labels, hot, level_out, replies, history, level_end, departure
):
    height = tall.shape[0] // FIELDS
    width = 2 * LANES
    river, coast = lax.axis_index("river"), lax.axis_index("coast")
    rivers, coasts = lax.axis_size("river"), lax.axis_size("coast")
    lane = lax.broadcasted_iota(i32, (height, LANES), 1)
    from_left = jnp.where(coast % 2 == 0, from_odd[...], from_even[...])
    from_right = jnp.where(coast % 2 == 0, from_even[...], from_odd[...])

    def whole(field):
        reach, at = reach_of(field), ROW_AT[field]
        beside = jnp.zeros((height, LANES), f32)
        if reach:
            beside = jnp.where(lane < reach, turn(from_right, -at), beside)
            beside = jnp.where(lane >= LANES - reach, turn(from_left, -at - reach), beside)
        return jnp.concatenate([tall[field * height : (field + 1) * height], beside], axis=1)

    level, bed, east, north = [whole(STEPS + number) for number in range(4)]

    row = lax.broadcasted_iota(i32, (height, width), 0)
    column = lax.broadcasted_iota(i32, (height, width), 1)
    row_in = jnp.where(
        row < tile_rows, 1, jnp.where(row < tile_rows + HALO, (river < rivers - 1).astype(i32), (river > 0).astype(i32))
    )
    column_in = jnp.where(
        column < LANES, 1, jnp.where(column < LANES + LANES // 2, (coast < coasts - 1).astype(i32), (coast > 0).astype(i32))
    )
    inside = row_in * column_in == 1

    def next_row(value):
        return pltpu.roll(value, height - 1, 0)

    def next_column(value):
        return pltpu.roll(value, width - 1, 1)

    bed_east = jnp.maximum(bed, next_row(bed))
    bed_north = jnp.maximum(bed, next_column(bed))
    drive = gravity * step_seconds / cell_metres

    def ocean_turn(first, steps, step, level, east, north):
        source = whole(step) * (step_seconds / (cell_metres * cell_metres))
        east = flow_after(east, level, next_row(level), bed_east, drive, ocean_manning)
        north = flow_after(north, level, next_column(level), bed_north, drive, ocean_manning)
        spread = east - pltpu.roll(east, 1, 0) + north - pltpu.roll(north, 1, 1)
        level = level - step_seconds / cell_metres * spread + source
        level = jnp.where(inside, level, 0.0)
        for half in range(2):
            part = level[half * TALL : (half + 1) * TALL, :LANES]
            at = TALL * (2 * first + half * steps) + step - first
            history[pl.ds(at, TALL, stride=steps)] = part
        return level, east, north

    def table_of(first, steps):
        high_rows, at = TALL * steps, 2 * TALL * first
        halves = [history[at + half * high_rows : at + (half + 1) * high_rows] for half in range(2)]
        return jnp.concatenate(in_two(jnp.concatenate(halves, axis=1)), axis=0)

    def reply(table, first, steps, group, of):
        count = replies.shape[0] // STEPS // of
        for s in range(group * count, (group + 1) * count, 2):
            rows = jnp.concatenate([row_labels[s : s + 1], row_labels[s + 1 : s + 2]], axis=1)
            found = look_up(table, rows, hot[:, s * LANES : (s + 2) * LANES], steps)
            for half in range(2):
                at = (s + half) * STEPS + first
                replies[at : at + steps] = found[:, half * LANES : (half + 1) * LANES]

    waiting = []
    for part, (first, steps) in enumerate(LOOKED_UP):
        for step in range(first, first + steps):
            level, east, north = ocean_turn(first, steps, step, level, east, north)
            if waiting:
                reply(*waiting, step - first, steps)
        if part == len(LOOKED_UP) - 1:
            level_end[...] = level[:tile_rows, :LANES]
            finished = pltpu.make_async_copy(level_end, level_out, departure)
            finished.start()
        waiting = [table_of(first, steps), first, steps]
    reply(*waiting, 0, 1)
    finished.wait()


def mouth_kernel(returned, address, level_out, whole, series, hot, block, departures):
    rows = address.shape[0]
    groups = LANES // MPB
    place = lax.broadcasted_iota(i32, (TALL, 2 * LANES), 0).astype(f32).astype(bf16)

    def place_of(label, part):
        return label - part == place

    labels = []
    for i in range(0, rows, 2):
        pair = jnp.concatenate([address[i : i + 1], address[i + 1 : i + 2]], axis=1)
        high, low = [label.astype(f32) for label in split_label(pair, WIDE)]
        one_hot_columns(low, place_of, hot, slice(i * LANES, (i + 2) * LANES))
        labels.append(high)
    lane = lax.broadcasted_iota(i32, (rows, LANES), 1)
    copies = []
    for first, steps in LOOKED_UP:
        for row in range(TALL):
            for half in range(2):
                at = (2 * row + half) * STEPS + first
                to = first * TALL + row * steps
                lanes = slice(half * LANES, (half + 1) * LANES)
                whole[to : to + steps, lanes] = returned[at : at + steps]
        own = whole[first * TALL : (first + steps) * TALL]
        table = jnp.concatenate(in_two(own), axis=0)
        for i in range(0, rows, 2):
            lanes = slice(i * LANES, (i + 2) * LANES)
            found = look_up(table, labels[i // 2], hot[:, lanes], steps)
            series[pl.ds(first * rows + i, steps, stride=rows)] = found[:, :LANES]
            series[pl.ds(first * rows + i + 1, steps, stride=rows)] = found[:, LANES:]
        for number in range(first // groups, (first + steps) // groups):
            for g in range(groups):
                result = jnp.zeros((rows, LANES), f32)
                for place in range(groups):
                    at = (number * groups + place) * rows
                    part = turn(series[at : at + rows], (place - g) * MPB)
                    result = jnp.where(lane // MPB == place, part, result)
                block[number, g * rows : (g + 1) * rows] = result
            to = level_out.at[:, pl.ds(number * LANES, LANES)]
            copies.append(pltpu.make_async_copy(block.at[number], to, departures.at[number]))
            copies[-1].start()
    for copy in copies:
        copy.wait()


def shape(*dims, dtype=f32):
    return jax.ShapeDtypeStruct(dims, dtype)


def cost(products):
    return pl.CostEstimate(flops=2 * products, bytes_accessed=8 << 20, transcendentals=0)


def in_hbm(*arrays):
    return [pltpu.with_memory_space_constraint(whole, pltpu.HBM) for whole in arrays]


def swap(values, tall, devices, capacity):
    per = LANES // capacity
    if per > 1:
        values = values.reshape(devices // per, tall, per, capacity).transpose(0, 2, 1, 3)
    values = values.reshape(devices, 1, tall * capacity)
    values = lax.all_to_all(values, ("coast", "river"), split_axis=0, concat_axis=0, tiled=True)
    if per > 1:
        values = values.reshape(devices // per, per, tall, capacity).transpose(0, 2, 1, 3)
    return values.reshape(devices // per * tall, LANES)


def with_neighbour(value, axis, start):
    pairs = range(start, lax.axis_size(axis) - 1, 2)
    return lax.ppermute(value, axis, [(i + k, i + 1 - k) for i in pairs for k in range(2)])


def per_device(
    reach_depth,
    reach_flow,
    reach_bed,
    reach_width,
    reach_length,
    runoff,
    flows_into,
    mouth_prev,
    mouth_tile,
    mouth_cell,
    sea_level,
    sea_bed,
    wet_mask,
    flux_east,
    flux_north,
):
    devices = lax.axis_size("river") * lax.axis_size("coast")
    blocks = reach_depth.shape[0]
    tile_rows, tile_cols = sea_level.shape
    mouths = blocks * MPB
    capacity = max(2, 2 * mouths // devices)
    groups = devices * capacity // LANES
    rows = mouths // LANES
    height = tile_rows + 2 * HALO

    depth, sending, address, sea = pl.pallas_call(
        functools.partial(river_kernel, devices, lax.axis_size("coast"), capacity),
        name="river",
        out_shape=(
            shape(blocks, RB),
            shape(groups * SENT, LANES),
            shape(rows, LANES, dtype=i32),
            shape(4 * tile_rows, tile_cols),
        ),
        in_specs=[pl.BlockSpec(memory_space=pltpu.HBM)] * 15,
        scratch_shapes=[pltpu.VMEM((blocks, RB), f32)] * 6
        + [
            pltpu.VMEM((blocks, RB), i32),
            pltpu.VMEM((MPB, blocks), f32),
            pltpu.VMEM((MPB, blocks), i32),
            pltpu.VMEM((MPB, blocks), i32),
            pltpu.VMEM((tile_rows, tile_cols), f32),
            pltpu.VMEM((tile_rows, tile_cols), f32),
            pltpu.VMEM((tile_rows, tile_cols), i32),
            pltpu.VMEM((tile_rows, tile_cols), f32),
            pltpu.VMEM((tile_rows, tile_cols), f32),
            pltpu.SemaphoreType.DMA((15,)),
            pltpu.VMEM((reach_offsets, blocks, RB), f32),
            pltpu.VMEM((SENT * rows, LANES), f32),
            pltpu.VMEM((RB, LANES), f32),
            pltpu.VMEM((rows, LANES), i32),
            pltpu.VMEM((rows * devices, LANES), bf16),
            pltpu.VMEM((rows * devices, 2 * LANES), f32),
            pltpu.VMEM((rows, LANES), f32),
            pltpu.VMEM((LANES, rows), f32),
            pltpu.VMEM((mouths, WIDE), bf16),
            *[pltpu.VMEM((TALL * steps, LANES), bf16) for _, steps in PARTS],
            *[
                pltpu.VMEM((2 * TALL * (steps + (first == 0)), mouths), bf16)
                for first, steps in PARTS
            ],
        ],
        compiler_params=PARAMS,
    )(
        *in_hbm(
            reach_depth,
            reach_flow,
            reach_bed,
            reach_width,
            reach_length,
            runoff,
            flows_into,
            mouth_prev.T,
            mouth_tile[:, :, 0].T,
            mouth_cell.T,
            sea_level,
            sea_bed,
            wet_mask,
            flux_east,
            flux_north,
        )
    )
    arrived = swap(sending, SENT, devices, capacity)

    edge_rows = -(-HALO // 2 * STEPS // TALL) * TALL
    odd, sea = pl.pallas_call(
        edge_kernel,
        name="edges",
        out_shape=(shape(ROWS_SENT, LANES), shape(4 * tile_rows, tile_cols)),
        scratch_shapes=[
            pltpu.VMEM((edge_rows, LANES), bf16),
            pltpu.VMEM((WIDE, LANES), bf16),
            pltpu.VMEM((groups, LANES), f32),
            pltpu.VMEM((groups, LANES), f32),
            pltpu.VMEM((2 * edge_rows, groups * LANES), bf16),
            pltpu.VMEM((WIDE, groups * LANES), bf16),
            pltpu.VMEM((2 * edge_rows, LANES), f32),
        ],
        cost_estimate=cost(2 * edge_rows * WIDE * groups * LANES),
        compiler_params=PARAMS,
    )(arrived, sea)
    from_odd = with_neighbour(odd, "river", 1)

    fields, even, hot, labels, depth_after = pl.pallas_call(
        source_kernel,
        name="sources",
        out_shape=(
            shape(FIELDS * tile_rows, LANES),
            shape(ROWS_SENT, LANES),
            shape(WIDE, groups * LANES, dtype=bf16),
            shape(groups, LANES),
            shape(blocks, RB),
        ),
        out_specs=(pl.BlockSpec(memory_space=pltpu.VMEM),) * 4
        + (pl.BlockSpec(memory_space=pltpu.HBM),),
        scratch_shapes=[
            pltpu.VMEM((TALL * STEPS, LANES), bf16),
            pltpu.VMEM((WIDE, LANES), bf16),
            pltpu.VMEM((groups, LANES), f32),
            pltpu.VMEM((2 * TALL * STEPS, groups * LANES), bf16),
            pltpu.VMEM((2 * TALL * STEPS, LANES), f32),
            pltpu.SemaphoreType.DMA,
        ],
        cost_estimate=cost(2 * TALL * STEPS * WIDE * groups * LANES),
        compiler_params=PARAMS,
    )(arrived, sea, depth)
    from_even = with_neighbour(even, "river", 0)

    tall, odd, even = pl.pallas_call(
        strip_kernel,
        name="strips",
        out_shape=(shape(FIELDS * height, LANES), shape(height, LANES), shape(height, LANES)),
        compiler_params=PARAMS,
    )(fields, from_odd, from_even)
    from_odd, from_even = with_neighbour(odd, "coast", 1), with_neighbour(even, "coast", 0)

    level_after, replies = pl.pallas_call(
        functools.partial(ocean_kernel, tile_rows),
        name="ocean",
        out_shape=(shape(tile_rows, tile_cols), shape(groups * STEPS, LANES)),
        scratch_shapes=[
            pltpu.VMEM((2 * TALL * STEPS, LANES), f32),
            pltpu.VMEM((tile_rows, tile_cols), f32),
            pltpu.SemaphoreType.DMA,
        ],
        out_specs=(
            pl.BlockSpec(memory_space=pltpu.HBM),
            pl.BlockSpec(memory_space=pltpu.VMEM),
        ),
        compiler_params=PARAMS,
    )(tall, from_odd, from_even, labels, hot)
    returned = swap(replies, STEPS, devices, capacity)

    mouth_level = pl.pallas_call(
        mouth_kernel,
        name="mouths",
        out_shape=shape(blocks, STEPS * MPB),
        scratch_shapes=[
            pltpu.VMEM((TALL * STEPS, WIDE), f32),
            pltpu.VMEM((STEPS * rows, LANES), f32),
            pltpu.VMEM((WIDE, mouths), bf16),
            pltpu.VMEM((STEPS * MPB // LANES, blocks, LANES), f32),
            pltpu.SemaphoreType.DMA((STEPS * MPB // LANES,)),
        ],
        out_specs=pl.BlockSpec(memory_space=pltpu.HBM),
        compiler_params=PARAMS,
    )(returned, address)
    return (depth_after, level_after, mouth_level)


def solution(mesh):
    by_block = P(("river", "coast"), None)
    tiled = P("river", "coast")
    return jax.shard_map(
        per_device,
        mesh=mesh,
        in_specs=(by_block,) * 8
        + (P(("river", "coast"), None, None), by_block)
        + (tiled,) * 5,
        out_specs=(by_block, tiled, by_block),
        check_vma=False,
    )
```
